128 devices in a mesh: gx: 8 (over y_hi, x), gy: 16 (over z, y_lo, core).
Axes of the slice: x: 4, y: 4 (y_hi: 2, y_lo: 2; y = y_hi * 2 + y_lo), z: 4, core: 2. Of those that a mesh axis runs over, the one named last changes fastest.
Arguments:
- resid: bfloat16 [1024, 16384], P('gx', 'gy'), may hold values from -6 to 6
- queries: bfloat16 [1024, 16384], P('gy', 'gx'), may hold values from -480 to 480
- tree_kv: bfloat16 [1024, 2048], P('gy', 'gx'), may hold values from -6 to 6
- cache: bfloat16 [8, 128, 128, 256], P('gx', 'gy'), may hold values from -6 to 6
- page_table: int32 [16, 8], P('gy'), may hold values from 0 to 7, as said below
- cache_len: int32 [16], P('gy'), may hold values from 128 to 1024
- tree_size: int32 [16], P('gy'), may hold values from 16 to 64
- parents: int32 [16, 64], P('gy'), may hold values from -1 to 62, as said below
- w_out: bfloat16 [16384, 16384], P('gx', 'gy'), may hold values from -0.046875 to 0.046875
- gain: bfloat16 [16384], P('gy'), may hold values from 0.099609375 to 1.8984375
- w_gate: bfloat16 [16384, 26624], P('gy', 'gx'), may hold values from -0.046875 to 0.046875
- w_up: bfloat16 [16384, 26624], P('gy', 'gx'), may hold values from -0.046875 to 0.046875
- w_down: bfloat16 [26624, 16384], P('gx', 'gy'), may hold values from -0.0390625 to 0.0390625
Outputs:
- layer_out: bfloat16 [1024, 16384], P('gx', 'gy')
The draws below stay inside these ranges and needn't reach their ends.
Inputs may be any that keep to these rules, and one draw needn't show every extreme that they name: `page_table`: the one request r held at an index of gy names each of the 8 pages of that index exactly once. parents[r, 0] is -1 and parents[r, n] lies in 0 to n - 1 for n >= 1.
All inputs are finite; a program needn't handle non-finite values.
Results may differ from the reference program's by a relative error of at most 0.025.
Values may be sent and summed in bfloat16 or wider, within the bound.
A program may use at most 192 MiB of HBM per device.

```python
import jax
import jax.numpy as jnp
from jax import lax

D = 16384
FF = 26624
HQ = 128
KVH = 8
HD = 128
MAXTREE = 64
PAGE = 128
MAXPAGES = 8
REQ_DEV = 1
REQ = 16
ROWS = 1024
POOL = 128
N_GY = 16


def draw_queries(key, part):
    key = jax.random.fold_in(key, 1)
    base_key = jax.random.fold_in(key, 0)
    values = jax.random.normal(base_key, (ROWS, HQ * HD), jnp.float32)
    values = jnp.clip(values, -6.0, 6.0)
    return values.astype(jnp.bfloat16)


def draw_cache_len(key, part):
    key = jax.random.fold_in(key, 11)
    lengths = jax.random.randint(key, (REQ,), PAGE, MAXPAGES * PAGE + 1, jnp.int32)
    return lengths.at[0].set(MAXPAGES * PAGE)


def draw_tree_size(key, part):
    key = jax.random.fold_in(key, 12)
    sizes = jax.random.randint(key, (REQ,), MAXTREE // 4, MAXTREE + 1, jnp.int32)
    return sizes.at[0].set(MAXTREE)


def draw_parents(key, part):
    key = jax.random.fold_in(key, 13)
    raw = jax.random.randint(key, (REQ, MAXTREE), 0, 1 << 20, jnp.int32)
    nodes = jnp.arange(MAXTREE, dtype=jnp.int32)[None, :]
    picked = raw % jnp.maximum(nodes, 1)
    return jnp.where(nodes == 0, -1, picked).astype(jnp.int32)


def draw_page_table(key, part):
    key = jax.random.fold_in(key, 14)
    owners = REQ // REQ_DEV
    keys = jax.random.split(key, owners)
    orders = jax.vmap(lambda one_key: jax.random.permutation(one_key, REQ_DEV * MAXPAGES))(keys)
    return orders.reshape(REQ, MAXPAGES).astype(jnp.int32)


def block_levels(rng, shape, cuts, low, top_value):
    level, own = 1.0, jax.random.fold_in(rng, 6)
    for dim, blocks in cuts:
        draws = jnp.exp(jax.random.uniform(jax.random.fold_in(own, dim), (blocks,), jnp.float32, low / len(cuts), top_value / len(cuts)))
        level = level * jnp.repeat(draws, shape[dim] // blocks).reshape([-1 if axis == dim else 1 for axis in range(len(shape))])
    return level


def bell_draw(stream_key, dims, width, bound, cuts=(), held_as=jnp.bfloat16):
    level = block_levels(stream_key, dims, cuts, -0.22, 0.18) if cuts else 1.0
    entries = jax.random.normal(stream_key, dims, jnp.float32) * width * level
    return jnp.minimum(jnp.maximum(entries, -bound), bound).astype(held_as)


def setup_inputs(seed: int = 0) -> dict:
    splits = jax.random.split(jax.random.key(seed), 14)
    return {
        "resid": bell_draw(splits[0], (ROWS, D), 1.0, 6.0, ((0, 8), (1, 16))),
        "queries": draw_queries(jax.random.fold_in(splits[13], 71), 0),
        "tree_kv": bell_draw(splits[2], (ROWS, KVH * 2 * HD), 1.0, 6.0, ((0, 16), (1, 8))),
        "cache": bell_draw(splits[3], (KVH, POOL, PAGE, 2 * HD), 1.0, 6.0, ((0, 8), (1, 16))),
        "page_table": draw_page_table(jax.random.fold_in(splits[13], 71), 0),
        "cache_len": draw_cache_len(jax.random.fold_in(splits[13], 71), 0),
        "tree_size": draw_tree_size(jax.random.fold_in(splits[13], 71), 0),
        "parents": draw_parents(jax.random.fold_in(splits[13], 71), 0),
        "w_out": bell_draw(splits[8], (HQ * HD, D), (HQ * HD) ** -0.5, 0.046875, ((0, 8), (1, 16))),
        "gain": jnp.clip(1.0 + 0.18 * jax.random.normal(splits[9], (D,), jnp.float32), 0.099609375, 1.8984375).astype(jnp.bfloat16),
        "w_gate": bell_draw(splits[10], (D, FF), D ** -0.5, 0.046875, ((0, 16), (1, 8))),
        "w_up": bell_draw(splits[11], (D, FF), D ** -0.5, 0.046875, ((0, 16), (1, 8))),
        "w_down": bell_draw(splits[12], (FF, D), FF ** -0.5, 0.0390625, ((0, 8), (1, 16))),
    }


EPSILON = 1e-05

def ancestry(parent_row, tree_len):
    nodes = jnp.arange(MAXTREE, dtype=jnp.int32)
    linked = (parent_row[:, None] == nodes[None, :]).astype(jnp.float32)
    reach = jnp.eye(MAXTREE, dtype=jnp.float32) + linked
    for sweep in range(max(1, (MAXTREE - 1).bit_length())):
        reach = jnp.minimum(jnp.dot(reach, reach, precision=lax.Precision.HIGHEST), 1.0)
    return (reach > 0.5) & (nodes[None, :] < tree_len)

def attend(query_rows, tree_rows, context, ctx_len, tree_len, parent_row):
    groups = HQ // KVH
    scale = HD ** (-0.5)
    allowed_tree = ancestry(parent_row, tree_len)[:, None, :]
    positions = jnp.arange(context.shape[1], dtype=jnp.int32)
    allowed_ctx = (positions < ctx_len)[None, None, :]
    live = (jnp.arange(MAXTREE, dtype=jnp.int32) < tree_len)[:, None, None]
    outputs = []
    for head_group in range(context.shape[0]):
        q_block = query_rows[:, head_group * groups * HD:(head_group + 1) * groups * HD]
        q_block = q_block.reshape(MAXTREE, groups, HD).astype(jnp.float32)
        base = head_group * 2 * HD
        tree_keys = tree_rows[:, base:base + HD].astype(jnp.float32)
        tree_vals = tree_rows[:, base + HD:base + 2 * HD].astype(jnp.float32)
        ctx_keys = context[head_group, :, :HD].astype(jnp.float32)
        ctx_vals = context[head_group, :, HD:].astype(jnp.float32)
        ctx_scores = jnp.einsum('ngd,td->ngt', q_block, ctx_keys) * scale
        tree_scores = jnp.einsum('ngd,md->ngm', q_block, tree_keys) * scale
        ctx_scores = jnp.where(allowed_ctx, ctx_scores, -1e+30)
        tree_scores = jnp.where(allowed_tree, tree_scores, -1e+30)
        row_max = jnp.maximum(lax.optimization_barrier(jnp.max(ctx_scores, axis=-1, keepdims=True)), lax.optimization_barrier(jnp.max(tree_scores, axis=-1, keepdims=True)))
        ctx_exp = jnp.exp(ctx_scores - row_max)
        tree_exp = jnp.exp(tree_scores - row_max)
        total = lax.optimization_barrier(jnp.sum(ctx_exp, axis=-1, keepdims=True)) + lax.optimization_barrier(jnp.sum(tree_exp, axis=-1, keepdims=True))
        ctx_probs = (ctx_exp / total).astype(jnp.bfloat16).astype(jnp.float32)
        tree_probs = (tree_exp / total).astype(jnp.bfloat16).astype(jnp.float32)
        mixed = jnp.einsum('ngt,td->ngd', ctx_probs, ctx_vals) + jnp.einsum('ngm,md->ngd', tree_probs, tree_vals)
        mixed = jnp.where(live, mixed, 0.0)
        outputs.append(mixed.astype(jnp.bfloat16).reshape(MAXTREE, groups * HD))
    return jnp.concatenate(outputs, axis=1)

def reference(resid, queries, tree_kv, cache, page_table, cache_len, tree_size, parents, w_out, gain, w_gate, w_up, w_down):
    pool_dev = REQ_DEV * MAXPAGES

    def one_request(index):
        home = index // REQ_DEV
        slots = (home * pool_dev + page_table[index]).astype(jnp.int32)
        context = jnp.take(cache, slots, axis=1).reshape(KVH, MAXPAGES * PAGE, 2 * HD)
        query_rows = lax.dynamic_slice_in_dim(queries, (index * MAXTREE).astype(jnp.int32), MAXTREE, 0)
        tree_rows = lax.dynamic_slice_in_dim(tree_kv, (index * MAXTREE).astype(jnp.int32), MAXTREE, 0)
        return attend(query_rows, tree_rows, context, cache_len[index], tree_size[index], parents[index])
    attn = lax.map(one_request, jnp.arange(REQ, dtype=jnp.int32)).reshape(ROWS, HQ * HD)
    projected = jnp.dot(attn, w_out, preferred_element_type=jnp.float32)
    hid = (resid.astype(jnp.float32) + projected).astype(jnp.bfloat16)
    hid_wide = hid.astype(jnp.float32)
    mean_sq = lax.optimization_barrier(jnp.mean(hid_wide * hid_wide, axis=1, keepdims=True))
    normed = (hid_wide * lax.rsqrt(mean_sq + EPSILON) * gain.astype(jnp.float32)[None, :]).astype(jnp.bfloat16)
    block = D // N_GY

    def add_block(carry, index):
        rows = lax.dynamic_slice_in_dim(normed, (index * block).astype(jnp.int32), block, 1)
        gate_part = jnp.dot(rows, lax.dynamic_slice_in_dim(w_gate, (index * block).astype(jnp.int32), block, 0), preferred_element_type=jnp.float32)
        up_part = jnp.dot(rows, lax.dynamic_slice_in_dim(w_up, (index * block).astype(jnp.int32), block, 0), preferred_element_type=jnp.float32)
        gate_part = lax.optimization_barrier(gate_part.astype(jnp.bfloat16)).astype(jnp.float32)
        up_part = lax.optimization_barrier(up_part.astype(jnp.bfloat16)).astype(jnp.float32)
        return ((carry[0] + gate_part, carry[1] + up_part), None)
    start_sums = (jnp.zeros((ROWS, FF), jnp.float32), jnp.zeros((ROWS, FF), jnp.float32))
    (gate, up), unused = lax.scan(add_block, start_sums, jnp.arange(N_GY, dtype=jnp.int32))
    hidden = (jax.nn.silu(gate) * up).astype(jnp.bfloat16)
    down = jnp.dot(hidden, w_down, preferred_element_type=jnp.float32)
    return (hid.astype(jnp.float32) + down).astype(jnp.bfloat16)
```

```python
import jax
import jax.numpy as jnp
from jax import lax
from jax.experimental import pallas as pl
from jax.experimental.pallas import tpu as pltpu
from jax.sharding import PartitionSpec as P

D = 16384
HD = 128
MAXTREE = 64
PAGE = 128
MAXPAGES = 8
EPSILON = 1e-05

MESH = pl.DeviceIdType.MESH
BF = jnp.bfloat16
F32 = jnp.float32

CHUNKS = 4
NODES = MAXTREE // CHUNKS
BLOCK = 2 * NODES
ROWS = 8 * BLOCK
LANES = 128
TILE = 256


def visible_nodes(parents, tree_len):
    shape = (MAXTREE, MAXTREE)
    column, row = lax.broadcasted_iota(jnp.int32, shape, 1), lax.broadcasted_iota(jnp.int32, shape, 0)
    eye = jnp.where(row == column, 1.0, 0.0)
    reach = eye + jnp.where(parents == row, 1.0, 0.0)
    for sweep in range((MAXTREE - 1).bit_length()):
        held = reach.astype(BF)
        reach = jnp.minimum(jnp.dot(held, held, preferred_element_type=F32), 1.0)
    turned = lax.dot_general(
        reach.astype(BF), eye.astype(BF), (((0,), (0,)), ((), ())), preferred_element_type=F32
    )
    return jnp.where(column < tree_len, turned, 0.0)


def attend(query, visible, live, cached, tree_kv, cache, page_table):
    heads = query.shape[1] // HD
    keys = jnp.concatenate([query[:, h * HD : (h + 1) * HD] for h in range(heads)], axis=0)
    contract = (((1,), (1,)), ((), ()))
    context = cache[0].reshape(MAXPAGES * PAGE, 2 * HD)
    scale = HD ** (-0.5)
    ctx_scores = lax.dot_general(keys, context[:, 0:HD], contract, preferred_element_type=F32) * scale
    tree_scores = lax.dot_general(keys, tree_kv[:, 0:HD], contract, preferred_element_type=F32) * scale
    offset = lax.broadcasted_iota(jnp.int32, (1, PAGE), 1)
    bounds = []
    for page in range(MAXPAGES):
        place = jnp.int32(0)
        for p in range(1, MAXPAGES):
            place = jnp.where(page_table[0, p] == page, p, place)
        bounds.append(offset < cached - place * PAGE)
    allowed = jnp.concatenate([jnp.where(bound, 1.0, 0.0) for bound in bounds], axis=1)
    ctx_scores = jnp.where(allowed > 0.5, ctx_scores, -1e30)
    seen = jnp.concatenate([visible] * heads, axis=0)
    tree_scores = jnp.where(seen > 0.5, tree_scores, -1e30)
    row_max = jnp.maximum(
        jnp.max(ctx_scores, axis=-1, keepdims=True), jnp.max(tree_scores, axis=-1, keepdims=True)
    )
    ctx_exp = jnp.exp(ctx_scores - row_max)
    tree_exp = jnp.exp(tree_scores - row_max)
    total = jnp.sum(ctx_exp, axis=-1, keepdims=True) + jnp.sum(tree_exp, axis=-1, keepdims=True)
    share = 1.0 / total
    mixed = jnp.dot((ctx_exp * share).astype(BF), context[:, HD:], preferred_element_type=F32)
    mixed += jnp.dot((tree_exp * share).astype(BF), tree_kv[:, HD:], preferred_element_type=F32)
    count = query.shape[0]
    parts = [jnp.where(live, mixed[h * count : (h + 1) * count, :], 0.0).astype(BF) for h in range(heads)]
    return jnp.concatenate(parts, axis=1)


def remote(src, dst, send_sem, recv_sem, device):
    return pltpu.make_async_remote_copy(
        src_ref=src,
        dst_ref=dst,
        send_sem=send_sem,
        recv_sem=recv_sem,
        device_id=device,
        device_id_type=MESH,
    )


class Place:
    def __init__(self, r, p, prev, follow, pair, sib, core, index):
        self.r, self.p = r, p
        self.prev, self.follow, self.pair, self.sib = prev, follow, pair, sib
        self.core = core
        self.index = index

    def block(self, p, shift):
        return self.index(p, lax.rem(self.r + (4 + shift), 4))


class Scatter:
    def __init__(self, place, part, far, near, last, send, recv):
        self.at = place
        self.part, self.far, self.near, self.last = part, far, near, last
        self.send, self.recv = send, recv
        self.open = {}

    def push(self, k, src, dst, sem, device):
        copy = remote(src, dst, self.send.at[k, sem], self.recv.at[k, sem], device)
        copy.start()
        self.open.setdefault(k, []).append(copy)

    def arrived(self, k, ref, sem):
        remote(ref, ref, self.send.at[k, sem], self.recv.at[k, sem], self.at.pair).wait_recv()

    def step1(self, k):
        at, part = self.at, self.part(k)
        self.push(k, part.at[at.block(0, 2)], self.far.at[k, 0], 0, at.follow)
        self.push(k, part.at[at.block(1, 2)], self.far.at[k, 1], 1, at.prev)
        self.push(k, part.at[at.block(1, 1)], self.near.at[k, 0, 1], 3, at.follow)
        self.push(k, part.at[at.block(0, -1)], self.near.at[k, 1, 0], 4, at.prev)

    def step2(self, k):
        at, part = self.at, self.part(k)
        for way, (p, shift, device, sem) in enumerate(((0, 1, at.follow, 2), (1, -1, at.prev, 5))):
            self.arrived(k, self.far.at[k, way], way)
            mine = at.block(p, shift)
            part[mine] = (part[mine].astype(F32) + self.far[k, way].astype(F32)).astype(BF)
            self.push(k, part.at[mine], self.near.at[k, way, p], sem, device)

    def ring_sum(self, k, p):
        part = self.part(k)
        for way in (0, 1):
            self.arrived(k, self.near.at[k, way, p], 2 + 2 * way + p)
        return (
            part[self.at.block(p, 0)].astype(F32)
            + self.near[k, 0, p].astype(F32)
            + self.near[k, 1, p].astype(F32)
        )

    def step3(self, k):
        at, part = self.at, self.part(k)
        other = 1 - at.p
        theirs = at.block(other, 0)
        part[theirs] = self.ring_sum(k, other).astype(BF)
        self.push(k, part.at[theirs], self.last.at[k], 6, at.pair)

    def step4(self, k):
        total = self.ring_sum(k, self.at.p)
        self.arrived(k, self.last.at[k], 6)
        return total + self.last[k].astype(F32)

    def close(self, k):
        for copy in self.open.pop(k, []):
            copy.wait_send()


class Gather:
    def __init__(self, place, ref, send, recv):
        self.at, self.ref = place, ref
        self.send, self.recv = send, recv
        self.open = {}

    def push(self, k, block, sem, device):
        ref = self.ref(k, self.at.core, block)
        copy = remote(ref, ref, self.send.at[k, sem], self.recv.at[k, sem], device)
        copy.start()
        self.open.setdefault(k, []).append(copy)

    def arrived(self, k, block, sem, core):
        ref = self.ref(k, core, block)
        remote(ref, ref, self.send.at[k, sem], self.recv.at[k, sem], self.at.pair).wait_recv()

    def share(self, k, block):
        self.push(k, block, 7 + block, self.at.sib)

    def step1(self, k):
        at = self.at
        mine = at.block(at.p, 0)
        self.push(k, mine, 0, at.pair)
        self.push(k, mine, 1 + at.p, at.follow)
        self.push(k, mine, 3 + at.p, at.prev)
        self.share(k, mine)

    def step2(self, k):
        at = self.at
        other = 1 - at.p
        block = at.block(other, 0)
        self.arrived(k, block, 0, at.core)
        self.push(k, block, 1 + other, at.follow)
        self.push(k, block, 3 + other, at.prev)
        self.share(k, block)

    def step3(self, k):
        at = self.at
        left, right = at.block(0, -1), at.block(1, 1)
        self.arrived(k, left, 1, at.core)
        self.push(k, left, 5, at.follow)
        self.share(k, left)
        self.arrived(k, right, 4, at.core)
        self.push(k, right, 6, at.prev)
        self.share(k, right)
        left, right = at.block(1, -1), at.block(0, 1)
        self.arrived(k, left, 2, at.core)
        self.share(k, left)
        self.arrived(k, right, 3, at.core)
        self.share(k, right)

    def step4(self, k):
        at = self.at
        left, right = at.block(0, -2), at.block(1, 2)
        self.arrived(k, left, 5, at.core)
        self.share(k, left)
        self.arrived(k, right, 6, at.core)
        self.share(k, right)

    def step5(self, k):
        for block in range(8):
            self.arrived(k, block, 7 + block, 1 - self.at.core)

    def close(self, k):
        for copy in self.open.pop(k, []):
            copy.wait_send()


def layer_kernel(
    page_table,
    cache_len,
    tree_size,
    parents,
    queries,
    tree_kv,
    cache,
    resid,
    gain,
    w_out,
    w_gate,
    w_up,
    w_down,
    out,
    wo,
    wgu,
    wd,
    attn_all,
    proj,
    hid,
    normed_all,
    sums,
    hidden_all,
    visible,
    far_a,
    near_a,
    last_a,
    far_b,
    near_b,
    last_b,
    far_c,
    near_c,
    last_c,
    load_sem,
    swap_send,
    swap_recv,
    ga_send,
    ga_recv,
    gb_send,
    gb_recv,
    gc_send,
    gc_recv,
    sa_send,
    sa_recv,
    sb_send,
    sb_recv,
    sc_send,
    sc_recv,
):
    gx, gy = lax.axis_index("gx"), lax.axis_index("gy")
    yh, x = lax.div(gx, 4), lax.rem(gx, 4)
    z, yl, core = lax.div(gy, 4), lax.rem(lax.div(gy, 2), 2), lax.rem(gy, 2)
    width = wo.shape[1]
    half = wgu.shape[1] // 2
    depth = w_gate.shape[0]

    sib = (gx, z * 4 + yl * 2 + (1 - core))
    along_x = Place(
        x,
        yh,
        (yh * 4 + lax.rem(x + 3, 4), gy),
        (yh * 4 + lax.rem(x + 1, 4), gy),
        ((1 - yh) * 4 + x, gy),
        sib,
        core,
        lambda p, r: p * 4 + r,
    )
    along_z = Place(
        z,
        yl,
        (gx, lax.rem(z + 3, 4) * 4 + yl * 2 + core),
        (gx, lax.rem(z + 1, 4) * 4 + yl * 2 + core),
        (gx, z * 4 + (1 - yl) * 2 + core),
        sib,
        core,
        lambda p, r: r * 2 + p,
    )

    loads = []

    def load(src, dst):
        copy = pltpu.make_async_copy(src, dst, load_sem.at[len(loads)])
        copy.start()
        loads.append(copy)

    load(w_out, wo)
    mine, theirs = pl.multiple_of(core * half, LANES), pl.multiple_of((1 - core) * half, LANES)
    deep = pl.ds(pl.multiple_of(core * depth, depth), depth)
    load(w_gate.at[:, pl.ds(mine, half)], wgu.at[deep, pl.ds(0, half)])
    load(w_up.at[:, pl.ds(mine, half)], wgu.at[deep, pl.ds(half, half)])
    load(w_down, wd)

    barrier = pltpu.get_barrier_semaphore()
    for device in (along_x.prev, along_x.follow, along_x.pair, along_z.prev, along_z.follow, along_z.pair, sib):
        pl.semaphore_signal(barrier, inc=1, device_id=device, device_id_type=MESH)
    pl.semaphore_wait(barrier, 7)

    gather_a = Gather(along_z, lambda k, c, b: attn_all.at[k, b, c], ga_send, ga_recv)
    gather_b = Gather(along_x, lambda k, c, b: normed_all.at[k, c, b], gb_send, gb_recv)
    gather_c = Gather(along_z, lambda k, c, b: hidden_all.at[k, c, b], gc_send, gc_recv)
    scatter_a = Scatter(along_x, lambda k: proj.at[k], far_a, near_a, last_a, sa_send, sa_recv)
    scatter_b = Scatter(along_z, lambda k: sums.at[k % 2], far_b, near_b, last_b, sb_send, sb_recv)
    scatter_c = Scatter(along_x, lambda k: proj.at[k], far_c, near_c, last_c, sc_send, sc_recv)

    swaps = [
        remote(
            w.at[:, pl.ds(theirs, half)],
            wgu.at[deep, pl.ds(n * half, half)],
            swap_send.at[n],
            swap_recv.at[n],
            sib,
        )
        for n, w in enumerate((w_gate, w_up))
    ]

    visible[...] = visible_nodes(parents[...], tree_size[0])

    def start(k):
        nodes = slice(k * NODES, (k + 1) * NODES)
        node = lax.broadcasted_iota(jnp.int32, (NODES, 1), 0) + k * NODES
        attn_all[k, along_z.block(yl, 0), core] = attend(
            queries[nodes, :], visible[nodes, :], node < tree_size[0], cache_len[0], tree_kv[...], cache, page_table
        )
        gather_a.step1(k)

    def project(k):
        gather_a.step5(k)
        if k == 0:
            loads[0].wait()

        def tile(n, carry):
            columns = pl.ds(pl.multiple_of(n * TILE, TILE), TILE)
            rows = attn_all[k].reshape(ROWS, attn_all.shape[-1])
            product = jnp.dot(rows, wo[:, columns], preferred_element_type=F32)
            proj[k, :, :, columns] = product.astype(BF).reshape(8, BLOCK, TILE)
            return carry

        lax.fori_loop(0, width // TILE, tile, 0)
        scatter_a.step1(k)
        if k == 0:
            for copy in swaps:
                copy.start()

    def norm(k):
        projected = scatter_a.step4(k)
        rows = jnp.concatenate([resid[r * MAXTREE + k * NODES : r * MAXTREE + (k + 1) * NODES, :] for r in (0, 1)], axis=0)
        value = (rows.astype(F32) + projected).astype(BF)
        hid[k] = value
        wide = value.astype(F32)
        mine = along_x.block(yh, 0)
        normed_all[k, core, mine, :, 0:width] = (wide * gain[...].astype(F32)).astype(BF)
        squares = jnp.sum(wide * wide, axis=1, keepdims=True)
        normed_all[k, core, mine, :, width:] = jnp.broadcast_to(squares, (BLOCK, LANES)).astype(BF)
        gather_b.step1(k)

    def gate_up(k):
        gather_b.step5(k)
        if k == 0:
            loads[1].wait()
            loads[2].wait()
            for copy in swaps:
                copy.wait()
        if k >= 2:
            scatter_b.close(k - 2)
        part = sums.at[k % 2]

        def tile(n, carry):
            columns = pl.ds(pl.multiple_of(n * TILE, TILE), TILE)
            product = jnp.dot(
                normed_all[k, 0, :, :, 0:width].reshape(ROWS, width), wgu[0:depth, columns], preferred_element_type=F32
            )
            product += jnp.dot(
                normed_all[k, 1, :, :, 0:width].reshape(ROWS, width), wgu[depth:, columns], preferred_element_type=F32
            )
            part[:, :, columns] = product.astype(BF).reshape(8, BLOCK, TILE)
            return carry

        lax.fori_loop(0, 2 * half // TILE, tile, 0)
        squares = normed_all[k, 0, :, :, width:].astype(F32) + normed_all[k, 1, :, :, width:].astype(F32)
        part[:, :, 2 * half :] = squares.astype(BF)
        scatter_b.step1(k)

    def activate(k):
        total = scatter_b.step4(k)
        scale = lax.rsqrt(total[:, 2 * half : 2 * half + 1] / D + EPSILON)
        gate = total[:, 0:half] * scale
        up = total[:, half : 2 * half] * scale
        hidden_all[k, core, along_z.block(yl, 0)] = (gate / (1.0 + jnp.exp(-gate)) * up).astype(BF)
        gather_c.step1(k)

    def down(k):
        gather_c.step5(k)
        if k == 0:
            loads[3].wait()
        scatter_a.close(k)

        def tile(n, carry):
            columns = pl.ds(pl.multiple_of(n * TILE, TILE), TILE)
            product = jnp.dot(
                hidden_all[k, 0].reshape(ROWS, half), wd[0:half, columns], preferred_element_type=F32
            )
            product += jnp.dot(
                hidden_all[k, 1].reshape(ROWS, half), wd[half:, columns], preferred_element_type=F32
            )
            proj[k, :, :, columns] = product.astype(BF).reshape(8, BLOCK, TILE)
            return carry

        lax.fori_loop(0, width // TILE, tile, 0)
        scatter_c.step1(k)

    def finish(k):
        total = (hid[k].astype(F32) + scatter_c.step4(k)).astype(BF)
        for r in (0, 1):
            out[r * MAXTREE + k * NODES : r * MAXTREE + (k + 1) * NODES, :] = total[r * NODES : (r + 1) * NODES, :]

    stages = [
        start,
        gather_a.step2,
        gather_a.step3,
        gather_a.step4,
        project,
        scatter_a.step2,
        scatter_a.step3,
        norm,
        gather_b.step2,
        gather_b.step3,
        gather_b.step4,
        gate_up,
        scatter_b.step2,
        scatter_b.step3,
        activate,
        gather_c.step2,
        gather_c.step3,
        gather_c.step4,
        down,
        scatter_c.step2,
        scatter_c.step3,
        finish,
    ]
    assert len(ORDER) == len(stages) * CHUNKS
    for stage, k in ORDER:
        stages[stage](k)
    for group in (gather_a, gather_b, gather_c, scatter_a, scatter_b, scatter_c):
        for k in range(CHUNKS):
            group.close(k)


ORDER = sorted(((s, k) for s in range(22) for k in range(CHUNKS)), key=lambda e: (e[0] + 2 * e[1], -e[1]))


def layer(page_table, cache_len, tree_size, parents, queries, tree_kv, cache, resid, gain, w_out, w_gate, w_up, w_down):
    heads, width = w_out.shape
    depth, units = w_gate.shape
    half = units // 2
    sums = 2 * half + LANES
    vmem = pl.BlockSpec(memory_space=pltpu.VMEM)
    smem = pl.BlockSpec(memory_space=pltpu.SMEM)
    hbm = pl.BlockSpec(memory_space=pl.ANY)
    sem = pltpu.SemaphoreType.DMA

    def scatter_buffers(lanes):
        return [
            pltpu.VMEM((CHUNKS, 2, BLOCK, lanes), BF),
            pltpu.VMEM((CHUNKS, 2, 2, BLOCK, lanes), BF),
            pltpu.VMEM((CHUNKS, BLOCK, lanes), BF),
        ]

    scratch = [
        pltpu.VMEM((heads, width), BF),
        pltpu.VMEM((2 * depth, units), BF),
        pltpu.VMEM((units, width), BF),
        pltpu.VMEM((CHUNKS, 8, 2, NODES, heads), BF),
        pltpu.VMEM((CHUNKS, 8, BLOCK, width), BF),
        pltpu.VMEM((CHUNKS, BLOCK, width), BF),
        pltpu.VMEM((CHUNKS, 2, 8, BLOCK, width + LANES), BF),
        pltpu.VMEM((2, 8, BLOCK, sums), BF),
        pltpu.VMEM((CHUNKS, 2, 8, BLOCK, half), BF),
        pltpu.VMEM((MAXTREE, MAXTREE), F32),
        *scatter_buffers(width),
        *scatter_buffers(sums),
        *scatter_buffers(width),
        sem((4,)),
        sem((2,)),
        sem((2,)),
        *[sem((CHUNKS, 15))] * 6,
        *[sem((CHUNKS, 7))] * 6,
    ]
    return pl.pallas_call(
        layer_kernel,
        out_shape=jax.ShapeDtypeStruct(resid.shape, BF),
        in_specs=[smem, smem, smem, vmem, vmem, vmem, vmem, vmem, vmem, hbm, hbm, hbm, hbm],
        out_specs=vmem,
        scratch_shapes=scratch,
        compiler_params=pltpu.CompilerParams(
            collective_id=0, has_side_effects=True, vmem_limit_bytes=62 * 1024 * 1024
        ),
        cost_estimate=pl.CostEstimate(
            flops=2 * 1024 * (heads * width + 3 * depth * units), bytes_accessed=26 * 1024 * 1024, transcendentals=0
        ),
    )(
        page_table,
        cache_len,
        tree_size,
        parents,
        queries,
        tree_kv,
        cache,
        resid,
        gain,
        w_out,
        w_gate,
        w_up,
        w_down,
    )


def body(
    resid,
    queries,
    tree_kv,
    cache,
    page_table,
    cache_len,
    tree_size,
    parents,
    w_out,
    gain,
    w_gate,
    w_up,
    w_down,
):
    return layer(
        page_table,
        cache_len,
        tree_size,
        parents,
        queries,
        tree_kv,
        cache,
        resid,
        gain.reshape(1, -1),
        w_out,
        w_gate,
        w_up,
        w_down,
    )


def solution(mesh):
    in_specs = (
        P("gx", "gy"),
        P("gy", "gx"),
        P("gy", "gx"),
        P("gx", "gy", None, None),
        P("gy", None),
        P("gy"),
        P("gy"),
        P("gy", None),
        P("gx", "gy"),
        P("gy"),
        P("gy", "gx"),
        P("gy", "gx"),
        P("gx", "gy"),
    )
    out_specs = P("gx", "gy")
    return jax.shard_map(body, mesh=mesh, in_specs=in_specs, out_specs=out_specs, check_vma=False)
```

```python
import jax
import jax.numpy as jnp
from jax import lax
from jax.experimental import pallas as pl
from jax.experimental.pallas import tpu as pltpu
from jax.sharding import PartitionSpec as P

D = 16384
HD = 128
MAXTREE = 64
PAGE = 128
MAXPAGES = 8
EPSILON = 1e-05

MESH = pl.DeviceIdType.MESH
BF = jnp.bfloat16
F32 = jnp.float32

CHUNKS = 4
NODES = MAXTREE // CHUNKS
BLOCK = 2 * NODES
ROWS = 8 * BLOCK
LANES = 128
TILE = 512


def visible_nodes(parents, tree_len):
    shape = (MAXTREE, MAXTREE)
    column, row = lax.broadcasted_iota(jnp.int32, shape, 1), lax.broadcasted_iota(jnp.int32, shape, 0)
    eye = jnp.where(row == column, 1.0, 0.0)
    reach = eye + jnp.where(parents == row, 1.0, 0.0)
    for sweep in range((MAXTREE - 1).bit_length()):
        held = reach.astype(BF)
        reach = jnp.minimum(jnp.dot(held, held, preferred_element_type=F32), 1.0)
    turned = lax.dot_general(
        reach.astype(BF), eye.astype(BF), (((0,), (0,)), ((), ())), preferred_element_type=F32
    )
    return jnp.where(column < tree_len, turned, 0.0)


def attend(query, visible, live, cached, tree_kv, cache, page_table):
    heads = query.shape[1] // HD
    keys = jnp.concatenate([query[:, h * HD : (h + 1) * HD] for h in range(heads)], axis=0)
    contract = (((1,), (1,)), ((), ()))
    context = cache[0].reshape(MAXPAGES * PAGE, 2 * HD)
    scale = HD ** (-0.5)
    ctx_scores = lax.dot_general(keys, context[:, 0:HD], contract, preferred_element_type=F32) * scale
    tree_scores = lax.dot_general(keys, tree_kv[:, 0:HD], contract, preferred_element_type=F32) * scale
    offset = lax.broadcasted_iota(jnp.int32, (1, PAGE), 1)
    bounds = []
    for page in range(MAXPAGES):
        place = jnp.int32(0)
        for p in range(1, MAXPAGES):
            place = jnp.where(page_table[0, p] == page, p, place)
        bounds.append(offset < cached - place * PAGE)
    allowed = jnp.concatenate([jnp.where(bound, 1.0, 0.0) for bound in bounds], axis=1)
    ctx_scores = jnp.where(allowed > 0.5, ctx_scores, -1e30)
    seen = jnp.concatenate([visible] * heads, axis=0)
    tree_scores = jnp.where(seen > 0.5, tree_scores, -1e30)
    row_max = jnp.maximum(
        jnp.max(ctx_scores, axis=-1, keepdims=True), jnp.max(tree_scores, axis=-1, keepdims=True)
    )
    ctx_exp = jnp.exp(ctx_scores - row_max)
    tree_exp = jnp.exp(tree_scores - row_max)
    total = jnp.sum(ctx_exp, axis=-1, keepdims=True) + jnp.sum(tree_exp, axis=-1, keepdims=True)
    share = 1.0 / total
    mixed = jnp.dot((ctx_exp * share).astype(BF), context[:, HD:], preferred_element_type=F32)
    mixed += jnp.dot((tree_exp * share).astype(BF), tree_kv[:, HD:], preferred_element_type=F32)
    count = query.shape[0]
    parts = [jnp.where(live, mixed[h * count : (h + 1) * count, :], 0.0).astype(BF) for h in range(heads)]
    return jnp.concatenate(parts, axis=1)


def remote(src, dst, send_sem, recv_sem, device):
    return pltpu.make_async_remote_copy(
        src_ref=src,
        dst_ref=dst,
        send_sem=send_sem,
        recv_sem=recv_sem,
        device_id=device,
        device_id_type=MESH,
    )


def multiply(rows, weights, result):
    width = weights.shape[1]

    def columns(at, size):
        product = jnp.dot(rows(), weights[:, pl.ds(at, size)], preferred_element_type=F32)
        result[:, :, pl.ds(at, size)] = product.astype(BF).reshape(8, BLOCK, size)

    def tile(n, carry):
        columns(pl.multiple_of(n * TILE, TILE), TILE)
        return carry

    lax.fori_loop(0, width // TILE, tile, 0)
    if width % TILE:
        columns(width - width % TILE, width % TILE)


class Place:
    def __init__(self, r, p, prev, follow, pair, sib, core, index):
        self.r, self.p = r, p
        self.prev, self.follow, self.pair, self.sib = prev, follow, pair, sib
        self.core = core
        self.index = index

    def block(self, p, shift):
        return self.index(p, lax.rem(self.r + (4 + shift), 4))


class Scatter:
    def __init__(self, place, part, far, near, last, send, recv):
        self.at = place
        self.part, self.far, self.near, self.last = part, far, near, last
        self.send, self.recv = send, recv
        self.open = {}

    def push(self, k, src, dst, sem, device):
        copy = remote(src, dst, self.send.at[k, sem], self.recv.at[k, sem], device)
        copy.start()
        self.open.setdefault(k, []).append(copy)

    def arrived(self, k, ref, sem):
        remote(ref, ref, self.send.at[k, sem], self.recv.at[k, sem], self.at.pair).wait_recv()

    def step1(self, k):
        at, part = self.at, self.part(k)
        self.push(k, part.at[at.block(0, 2)], self.far.at[k, 0], 0, at.follow)
        self.push(k, part.at[at.block(1, 2)], self.far.at[k, 1], 1, at.prev)
        self.push(k, part.at[at.block(1, 1)], self.near.at[k, 0, 1], 3, at.follow)
        self.push(k, part.at[at.block(0, -1)], self.near.at[k, 1, 0], 4, at.prev)

    def step2(self, k):
        at, part = self.at, self.part(k)
        for way, (p, shift, device, sem) in enumerate(((0, 1, at.follow, 2), (1, -1, at.prev, 5))):
            self.arrived(k, self.far.at[k, way], way)
            mine = at.block(p, shift)
            part[mine] = (part[mine].astype(F32) + self.far[k, way].astype(F32)).astype(BF)
            self.push(k, part.at[mine], self.near.at[k, way, p], sem, device)

    def ring_sum(self, k, p):
        part = self.part(k)
        for way in (0, 1):
            self.arrived(k, self.near.at[k, way, p], 2 + 2 * way + p)
        return (
            part[self.at.block(p, 0)].astype(F32)
            + self.near[k, 0, p].astype(F32)
            + self.near[k, 1, p].astype(F32)
        )

    def step3(self, k):
        at, part = self.at, self.part(k)
        other = 1 - at.p
        theirs = at.block(other, 0)
        part[theirs] = self.ring_sum(k, other).astype(BF)
        self.push(k, part.at[theirs], self.last.at[k], 6, at.pair)

    def step4(self, k):
        total = self.ring_sum(k, self.at.p)
        self.arrived(k, self.last.at[k], 6)
        return total + self.last[k].astype(F32)

    def close(self, k):
        for copy in self.open.pop(k, []):
            copy.wait_send()


class Gather:
    def __init__(self, place, ref, send, recv):
        self.at, self.ref = place, ref
        self.send, self.recv = send, recv
        self.open = {}

    def push(self, k, block, sem, device):
        ref = self.ref(k, self.at.core, block)
        copy = remote(ref, ref, self.send.at[k, sem], self.recv.at[k, sem], device)
        copy.start()
        self.open.setdefault(k, []).append(copy)

    def arrived(self, k, block, sem, core):
        ref = self.ref(k, core, block)
        remote(ref, ref, self.send.at[k, sem], self.recv.at[k, sem], self.at.pair).wait_recv()

    def share(self, k, block):
        self.push(k, block, 7 + block, self.at.sib)

    def step1(self, k):
        at = self.at
        mine = at.block(at.p, 0)
        self.push(k, mine, 0, at.pair)
        self.push(k, mine, 1 + at.p, at.follow)
        self.push(k, mine, 3 + at.p, at.prev)
        self.share(k, mine)

    def step2(self, k):
        at = self.at
        other = 1 - at.p
        block = at.block(other, 0)
        self.arrived(k, block, 0, at.core)
        self.push(k, block, 1 + other, at.follow)
        self.push(k, block, 3 + other, at.prev)
        self.share(k, block)

    def step3(self, k):
        at = self.at
        left, right = at.block(0, -1), at.block(1, 1)
        self.arrived(k, left, 1, at.core)
        self.push(k, left, 5, at.follow)
        self.share(k, left)
        self.arrived(k, right, 4, at.core)
        self.push(k, right, 6, at.prev)
        self.share(k, right)
        left, right = at.block(1, -1), at.block(0, 1)
        self.arrived(k, left, 2, at.core)
        self.share(k, left)
        self.arrived(k, right, 3, at.core)
        self.share(k, right)

    def step4(self, k):
        at = self.at
        left, right = at.block(0, -2), at.block(1, 2)
        self.arrived(k, left, 5, at.core)
        self.share(k, left)
        self.arrived(k, right, 6, at.core)
        self.share(k, right)

    def step5(self, k):
        for block in range(8):
            self.arrived(k, block, 7 + block, 1 - self.at.core)

    def close(self, k):
        for copy in self.open.pop(k, []):
            copy.wait_send()


def layer_kernel(
    page_table,
    cache_len,
    tree_size,
    parents,
    queries,
    tree_kv,
    cache,
    resid,
    gain,
    w_out,
    w_gate,
    w_up,
    w_down,
    out,
    wo,
    wgu,
    wd,
    attn_all,
    proj,
    hid,
    normed_all,
    sums,
    hidden_all,
    visible,
    far_a,
    near_a,
    last_a,
    far_b,
    near_b,
    last_b,
    far_c,
    near_c,
    last_c,
    load_sem,
    swap_send,
    swap_recv,
    ga_send,
    ga_recv,
    gb_send,
    gb_recv,
    gc_send,
    gc_recv,
    sa_send,
    sa_recv,
    sb_send,
    sb_recv,
    sc_send,
    sc_recv,
):
    gx, gy = lax.axis_index("gx"), lax.axis_index("gy")
    yh, x = lax.div(gx, 4), lax.rem(gx, 4)
    z, yl, core = lax.div(gy, 4), lax.rem(lax.div(gy, 2), 2), lax.rem(gy, 2)
    width = wo.shape[1]
    half = wgu.shape[1] // 2
    depth = w_gate.shape[0]

    sib = (gx, z * 4 + yl * 2 + (1 - core))
    along_x = Place(
        x,
        yh,
        (yh * 4 + lax.rem(x + 3, 4), gy),
        (yh * 4 + lax.rem(x + 1, 4), gy),
        ((1 - yh) * 4 + x, gy),
        sib,
        core,
        lambda p, r: p * 4 + r,
    )
    along_z = Place(
        z,
        yl,
        (gx, lax.rem(z + 3, 4) * 4 + yl * 2 + core),
        (gx, lax.rem(z + 1, 4) * 4 + yl * 2 + core),
        (gx, z * 4 + (1 - yl) * 2 + core),
        sib,
        core,
        lambda p, r: r * 2 + p,
    )

    loads = []

    def load(src, dst):
        copy = pltpu.make_async_copy(src, dst, load_sem.at[len(loads)])
        copy.start()
        loads.append(copy)

    load(w_out, wo)
    mine, theirs = pl.multiple_of(core * half, LANES), pl.multiple_of((1 - core) * half, LANES)
    deep = pl.ds(pl.multiple_of(core * depth, depth), depth)
    load(w_gate.at[:, pl.ds(mine, half)], wgu.at[deep, pl.ds(0, half)])
    load(w_up.at[:, pl.ds(mine, half)], wgu.at[deep, pl.ds(half, half)])
    load(w_down, wd)

    barrier = pltpu.get_barrier_semaphore()
    for device in (along_x.prev, along_x.follow, along_x.pair, along_z.prev, along_z.follow, along_z.pair, sib):
        pl.semaphore_signal(barrier, inc=1, device_id=device, device_id_type=MESH)
    pl.semaphore_wait(barrier, 7)

    gather_a = Gather(along_z, lambda k, c, b: attn_all.at[k, b, c], ga_send, ga_recv)
    gather_b = Gather(along_x, lambda k, c, b: normed_all.at[k, c, b], gb_send, gb_recv)
    gather_c = Gather(along_z, lambda k, c, b: hidden_all.at[k, c, b], gc_send, gc_recv)
    scatter_a = Scatter(along_x, lambda k: proj.at[k], far_a, near_a, last_a, sa_send, sa_recv)
    scatter_b = Scatter(along_z, lambda k: sums.at[k % 2], far_b, near_b, last_b, sb_send, sb_recv)
    scatter_c = Scatter(along_x, lambda k: proj.at[k], far_c, near_c, last_c, sc_send, sc_recv)

    swaps = [
        remote(
            w.at[:, pl.ds(theirs, half)],
            wgu.at[deep, pl.ds(n * half, half)],
            swap_send.at[n],
            swap_recv.at[n],
            sib,
        )
        for n, w in enumerate((w_gate, w_up))
    ]

    visible[...] = visible_nodes(parents[...], tree_size[0])

    def start(k):
        nodes = slice(k * NODES, (k + 1) * NODES)
        node = lax.broadcasted_iota(jnp.int32, (NODES, 1), 0) + k * NODES
        attn_all[k, along_z.block(yl, 0), core] = attend(
            queries[nodes, :], visible[nodes, :], node < tree_size[0], cache_len[0], tree_kv[...], cache, page_table
        )
        gather_a.step1(k)

    def project(k):
        gather_a.step5(k)
        if k == 0:
            loads[0].wait()

        multiply(lambda: attn_all[k].reshape(ROWS, attn_all.shape[-1]), wo, proj.at[k])
        scatter_a.step1(k)
        if k == 0:
            for copy in swaps:
                copy.start()

    def norm(k):
        projected = scatter_a.step4(k)
        rows = jnp.concatenate([resid[r * MAXTREE + k * NODES : r * MAXTREE + (k + 1) * NODES, :] for r in (0, 1)], axis=0)
        value = (rows.astype(F32) + projected).astype(BF)
        hid[k] = value
        wide = value.astype(F32)
        mine = along_x.block(yh, 0)
        normed_all[k, core, mine, :, 0:width] = (wide * gain[...].astype(F32).reshape(1, width)).astype(BF)
        squares = jnp.sum(wide * wide, axis=1, keepdims=True)
        normed_all[k, core, mine, :, width:] = jnp.broadcast_to(squares, (BLOCK, LANES)).astype(BF)
        gather_b.step1(k)

    def gate_up(k):
        gather_b.step5(k)
        if k == 0:
            loads[1].wait()
            loads[2].wait()
            for copy in swaps:
                copy.wait()
        if k >= 2:
            scatter_b.close(k - 2)
        part = sums.at[k % 2]

        multiply(
            lambda: jnp.concatenate(
                [normed_all[k, c, :, :, 0:width].reshape(ROWS, width) for c in (0, 1)], axis=1
            ),
            wgu,
            part,
        )
        squares = normed_all[k, 0, :, :, width:].astype(F32) + normed_all[k, 1, :, :, width:].astype(F32)
        part[:, :, 2 * half :] = squares.astype(BF)
        scatter_b.step1(k)

    def activate(k):
        total = scatter_b.step4(k)
        scale = lax.rsqrt(total[:, 2 * half : 2 * half + 1] / D + EPSILON)
        gate = total[:, 0:half] * scale
        up = total[:, half : 2 * half] * scale
        hidden_all[k, core, along_z.block(yl, 0)] = (gate / (1.0 + jnp.exp(-gate)) * up).astype(BF)
        gather_c.step1(k)

    def down(k):
        gather_c.step5(k)
        if k == 0:
            loads[3].wait()
        scatter_a.close(k)

        multiply(
            lambda: jnp.concatenate([hidden_all[k, c].reshape(ROWS, half) for c in (0, 1)], axis=1), wd, proj.at[k]
        )
        scatter_c.step1(k)

    def finish(k):
        total = (hid[k].astype(F32) + scatter_c.step4(k)).astype(BF)
        for r in (0, 1):
            out[r * MAXTREE + k * NODES : r * MAXTREE + (k + 1) * NODES, :] = total[r * NODES : (r + 1) * NODES, :]

    stages = [
        start,
        gather_a.step2,
        gather_a.step3,
        gather_a.step4,
        project,
        scatter_a.step2,
        scatter_a.step3,
        norm,
        gather_b.step2,
        gather_b.step3,
        gather_b.step4,
        gate_up,
        scatter_b.step2,
        scatter_b.step3,
        activate,
        gather_c.step2,
        gather_c.step3,
        gather_c.step4,
        down,
        scatter_c.step2,
        scatter_c.step3,
        finish,
    ]
    ahead = [iter(stages) for k in range(CHUNKS)]
    for k in TURNS:
        next(ahead[k])(k)
    for group in (gather_a, gather_b, gather_c, scatter_a, scatter_b, scatter_c):
        for k in range(CHUNKS):
            group.close(k)


TURNS = (
    0, 1, 0, 3, 0, 1, 2, 0, 1, 0, 2, 0, 1, 2, 0, 1, 2, 3, 0, 1, 2, 3,
    1, 0, 3, 2, 0, 1, 2, 3, 0, 1, 0, 1, 2, 3, 1, 2, 0, 3, 1, 0, 2, 2,
    3, 1, 0, 2, 3, 1, 3, 0, 3, 1, 2, 0, 3, 0, 2, 0, 3, 1, 2, 0, 2, 3,
    1, 2, 3, 1, 0, 2, 3, 1, 3, 2, 3, 1, 2, 3, 1, 2, 0, 3, 3, 2, 1, 3,
)


def layer(page_table, cache_len, tree_size, parents, queries, tree_kv, cache, resid, gain, w_out, w_gate, w_up, w_down):
    heads, width = w_out.shape
    depth, units = w_gate.shape
    half = units // 2
    sums = 2 * half + LANES
    vmem = pl.BlockSpec(memory_space=pltpu.VMEM)
    smem = pl.BlockSpec(memory_space=pltpu.SMEM)
    hbm = pl.BlockSpec(memory_space=pl.ANY)
    sem = pltpu.SemaphoreType.DMA

    def scatter_buffers(lanes):
        return [
            pltpu.VMEM((CHUNKS, 2, BLOCK, lanes), BF),
            pltpu.VMEM((CHUNKS, 2, 2, BLOCK, lanes), BF),
            pltpu.VMEM((CHUNKS, BLOCK, lanes), BF),
        ]

    scratch = [
        pltpu.VMEM((heads, width), BF),
        pltpu.VMEM((2 * depth, units), BF),
        pltpu.VMEM((units, width), BF),
        pltpu.VMEM((CHUNKS, 8, 2, NODES, heads), BF),
        pltpu.VMEM((CHUNKS, 8, BLOCK, width), BF),
        pltpu.VMEM((CHUNKS, BLOCK, width), BF),
        pltpu.VMEM((CHUNKS, 2, 8, BLOCK, width + LANES), BF),
        pltpu.VMEM((2, 8, BLOCK, sums), BF),
        pltpu.VMEM((CHUNKS, 2, 8, BLOCK, half), BF),
        pltpu.VMEM((MAXTREE, MAXTREE), F32),
        *scatter_buffers(width),
        *scatter_buffers(sums),
        *scatter_buffers(width),
        sem((4,)),
        sem((2,)),
        sem((2,)),
        *[sem((CHUNKS, 15))] * 6,
        *[sem((CHUNKS, 7))] * 6,
    ]
    return pl.pallas_call(
        layer_kernel,
        out_shape=jax.ShapeDtypeStruct(resid.shape, BF),
        in_specs=[smem, smem, smem, vmem, vmem, vmem, vmem, vmem, vmem, hbm, hbm, hbm, hbm],
        out_specs=vmem,
        scratch_shapes=scratch,
        compiler_params=pltpu.CompilerParams(
            collective_id=0, has_side_effects=True, vmem_limit_bytes=62 * 1024 * 1024
        ),
        cost_estimate=pl.CostEstimate(
            flops=2 * 1024 * (heads * width + 3 * depth * units), bytes_accessed=26 * 1024 * 1024, transcendentals=0
        ),
    )(
        page_table,
        cache_len,
        tree_size,
        parents,
        queries,
        tree_kv,
        cache,
        resid,
        gain,
        w_out,
        w_gate,
        w_up,
        w_down,
    )


def body(
    resid,
    queries,
    tree_kv,
    cache,
    page_table,
    cache_len,
    tree_size,
    parents,
    w_out,
    gain,
    w_gate,
    w_up,
    w_down,
):
    return layer(
        page_table,
        cache_len,
        tree_size,
        parents,
        queries,
        tree_kv,
        cache,
        resid,
        gain,
        w_out,
        w_gate,
        w_up,
        w_down,
    )


def solution(mesh):
    in_specs = (
        P("gx", "gy"),
        P("gy", "gx"),
        P("gy", "gx"),
        P("gx", "gy", None, None),
        P("gy", None),
        P("gy"),
        P("gy"),
        P("gy", None),
        P("gx", "gy"),
        P("gy"),
        P("gy", "gx"),
        P("gy", "gx"),
        P("gx", "gy"),
    )
    out_specs = P("gx", "gy")
    return jax.shard_map(body, mesh=mesh, in_specs=in_specs, out_specs=out_specs, check_vma=False)
```

```python
import jax
import jax.numpy as jnp
from jax import lax
from jax.experimental import pallas as pl
from jax.experimental.pallas import tpu as pltpu
from jax.sharding import PartitionSpec as P

D = 16384
HD = 128
MAXTREE = 64
PAGE = 128
MAXPAGES = 8
EPSILON = 1e-05

MESH = pl.DeviceIdType.MESH
BF = jnp.bfloat16
F32 = jnp.float32

CHUNKS = 4
NODES = MAXTREE // CHUNKS
BLOCK = 2 * NODES
ROWS = 8 * BLOCK
LANES = 128
TILE = 1024


def visible_nodes(parents, tree_len):
    shape = (MAXTREE, MAXTREE)
    column, row = lax.broadcasted_iota(jnp.int32, shape, 1), lax.broadcasted_iota(jnp.int32, shape, 0)
    eye = jnp.where(row == column, 1.0, 0.0)
    reach = eye + jnp.where(parents == row, 1.0, 0.0)
    for sweep in range((MAXTREE - 1).bit_length()):
        held = reach.astype(BF)
        reach = jnp.minimum(jnp.dot(held, held, preferred_element_type=F32), 1.0)
    turned = lax.dot_general(
        reach.astype(BF), eye.astype(BF), (((0,), (0,)), ((), ())), preferred_element_type=F32
    )
    return jnp.where(column < tree_len, turned, 0.0)


def attend(query, visible, live, cached, tree_kv, cache, page_table):
    heads = query.shape[1] // HD
    keys = jnp.concatenate([query[:, h * HD : (h + 1) * HD] for h in range(heads)], axis=0)
    contract = (((1,), (1,)), ((), ()))
    context = cache[0].reshape(MAXPAGES * PAGE, 2 * HD)
    scale = HD ** (-0.5)
    ctx_scores = lax.dot_general(keys, context[:, 0:HD], contract, preferred_element_type=F32) * scale
    tree_scores = lax.dot_general(keys, tree_kv[:, 0:HD], contract, preferred_element_type=F32) * scale
    offset = lax.broadcasted_iota(jnp.int32, (1, PAGE), 1)
    bounds = []
    for page in range(MAXPAGES):
        place = jnp.int32(0)
        for p in range(1, MAXPAGES):
            place = jnp.where(page_table[0, p] == page, p, place)
        bounds.append(offset < cached - place * PAGE)
    allowed = jnp.concatenate([jnp.where(bound, 1.0, 0.0) for bound in bounds], axis=1)
    ctx_scores = jnp.where(allowed > 0.5, ctx_scores, -1e30)
    seen = jnp.concatenate([visible] * heads, axis=0)
    tree_scores = jnp.where(seen > 0.5, tree_scores, -1e30)
    row_max = jnp.maximum(
        jnp.max(ctx_scores, axis=-1, keepdims=True), jnp.max(tree_scores, axis=-1, keepdims=True)
    )
    ctx_exp = jnp.exp(ctx_scores - row_max)
    tree_exp = jnp.exp(tree_scores - row_max)
    total = jnp.sum(ctx_exp, axis=-1, keepdims=True) + jnp.sum(tree_exp, axis=-1, keepdims=True)
    share = 1.0 / total
    mixed = jnp.dot((ctx_exp * share).astype(BF), context[:, HD:], preferred_element_type=F32)
    mixed += jnp.dot((tree_exp * share).astype(BF), tree_kv[:, HD:], preferred_element_type=F32)
    count = query.shape[0]
    parts = [jnp.where(live, mixed[h * count : (h + 1) * count, :], 0.0).astype(BF) for h in range(heads)]
    return jnp.concatenate(parts, axis=1)


def remote(src, dst, send_sem, recv_sem, device):
    return pltpu.make_async_remote_copy(
        src_ref=src,
        dst_ref=dst,
        send_sem=send_sem,
        recv_sem=recv_sem,
        device_id=device,
        device_id_type=MESH,
    )


def multiply(rows, weights, result):
    width = weights.shape[1]

    def columns(at, size):
        product = jnp.dot(rows(), weights[:, pl.ds(at, size)], preferred_element_type=F32)
        result[:, :, pl.ds(at, size)] = product.astype(BF).reshape(8, BLOCK, size)

    def tile(n, carry):
        columns(pl.multiple_of(n * TILE, TILE), TILE)
        return carry

    lax.fori_loop(0, width // TILE, tile, 0)
    if width % TILE:
        columns(width - width % TILE, width % TILE)


class Place:
    def __init__(self, r, p, prev, follow, pair, sib, core, index):
        self.r, self.p = r, p
        self.prev, self.follow, self.pair, self.sib = prev, follow, pair, sib
        self.core = core
        self.index = index

    def block(self, p, shift):
        return self.index(p, lax.rem(self.r + (4 + shift), 4))


class Scatter:
    def __init__(self, place, part, far, near, last, send, recv):
        self.at = place
        self.part, self.far, self.near, self.last = part, far, near, last
        self.send, self.recv = send, recv
        self.open = {}

    def push(self, k, src, dst, sem, device):
        copy = remote(src, dst, self.send.at[k, sem], self.recv.at[k, sem], device)
        copy.start()
        self.open.setdefault(k, []).append(copy)

    def arrived(self, k, ref, sem):
        remote(ref, ref, self.send.at[k, sem], self.recv.at[k, sem], self.at.pair).wait_recv()

    def step1(self, k):
        at, part = self.at, self.part(k)
        self.push(k, part.at[at.block(0, 2)], self.far.at[k, 0], 0, at.follow)
        self.push(k, part.at[at.block(1, 2)], self.far.at[k, 1], 1, at.prev)
        self.push(k, part.at[at.block(1, 1)], self.near.at[k, 0, 1], 3, at.follow)
        self.push(k, part.at[at.block(0, -1)], self.near.at[k, 1, 0], 4, at.prev)

    def step2(self, k):
        at, part = self.at, self.part(k)
        for way, (p, shift, device, sem) in enumerate(((0, 1, at.follow, 2), (1, -1, at.prev, 5))):
            self.arrived(k, self.far.at[k, way], way)
            mine = at.block(p, shift)
            part[mine] = (part[mine].astype(F32) + self.far[k, way].astype(F32)).astype(BF)
            self.push(k, part.at[mine], self.near.at[k, way, p], sem, device)

    def ring_sum(self, k, p):
        part = self.part(k)
        for way in (0, 1):
            self.arrived(k, self.near.at[k, way, p], 2 + 2 * way + p)
        return (
            part[self.at.block(p, 0)].astype(F32)
            + self.near[k, 0, p].astype(F32)
            + self.near[k, 1, p].astype(F32)
        )

    def step3(self, k):
        at, part = self.at, self.part(k)
        other = 1 - at.p
        theirs = at.block(other, 0)
        part[theirs] = self.ring_sum(k, other).astype(BF)
        self.push(k, part.at[theirs], self.last.at[k], 6, at.pair)

    def step4(self, k):
        total = self.ring_sum(k, self.at.p)
        self.arrived(k, self.last.at[k], 6)
        return total + self.last[k].astype(F32)

    def close(self, k):
        for copy in self.open.pop(k, []):
            copy.wait_send()


class Gather:
    def __init__(self, place, ref, send, recv):
        self.at, self.ref = place, ref
        self.send, self.recv = send, recv
        self.open = {}

    def push(self, k, block, sem, device):
        ref = self.ref(k, self.at.core, block)
        copy = remote(ref, ref, self.send.at[k, sem], self.recv.at[k, sem], device)
        copy.start()
        self.open.setdefault(k, []).append(copy)

    def arrived(self, k, block, sem, core):
        ref = self.ref(k, core, block)
        remote(ref, ref, self.send.at[k, sem], self.recv.at[k, sem], self.at.pair).wait_recv()

    def both(self, shift):
        return pl.ds(self.at.block(0, shift), 2)

    def share(self, k, shift):
        self.push(k, self.both(shift), 7 + shift % 4, self.at.sib)

    def step1(self, k):
        at = self.at
        mine = at.block(at.p, 0)
        self.push(k, mine, 0, at.pair)
        self.push(k, mine, 1 + at.p, at.follow)
        self.push(k, mine, 3 + at.p, at.prev)

    def step2(self, k):
        at = self.at
        other = 1 - at.p
        block = at.block(other, 0)
        self.arrived(k, block, 0, at.core)
        self.push(k, block, 1 + other, at.follow)
        self.push(k, block, 3 + other, at.prev)
        self.share(k, 0)

    def step3(self, k):
        at = self.at
        left, right = at.block(0, -1), at.block(1, 1)
        self.arrived(k, left, 1, at.core)
        self.push(k, left, 5, at.follow)
        self.arrived(k, right, 4, at.core)
        self.push(k, right, 6, at.prev)
        self.arrived(k, at.block(1, -1), 2, at.core)
        self.share(k, -1)
        self.arrived(k, at.block(0, 1), 3, at.core)
        self.share(k, 1)

    def step4(self, k):
        at = self.at
        self.arrived(k, at.block(0, 2), 5, at.core)
        self.arrived(k, at.block(1, 2), 6, at.core)
        self.share(k, 2)

    def step5(self, k):
        for shift in (0, 1, -1, 2):
            self.arrived(k, self.both(shift), 7 + shift % 4, 1 - self.at.core)

    def close(self, k):
        for copy in self.open.pop(k, []):
            copy.wait_send()


def layer_kernel(
    page_table,
    cache_len,
    tree_size,
    parents,
    queries,
    tree_kv,
    cache,
    resid,
    gain,
    w_out,
    w_gate,
    w_up,
    w_down,
    out,
    wo,
    wgu,
    wd,
    attn_all,
    proj,
    hid,
    normed_all,
    sums,
    hidden_all,
    visible,
    far_a,
    near_a,
    last_a,
    far_b,
    near_b,
    last_b,
    far_c,
    near_c,
    last_c,
    load_sem,
    swap_send,
    swap_recv,
    ga_send,
    ga_recv,
    gb_send,
    gb_recv,
    gc_send,
    gc_recv,
    sa_send,
    sa_recv,
    sb_send,
    sb_recv,
    sc_send,
    sc_recv,
):
    gx, gy = lax.axis_index("gx"), lax.axis_index("gy")
    yh, x = lax.div(gx, 4), lax.rem(gx, 4)
    z, yl, core = lax.div(gy, 4), lax.rem(lax.div(gy, 2), 2), lax.rem(gy, 2)
    width = wo.shape[1]
    half = wgu.shape[1] // 2
    depth = w_gate.shape[0]

    sib = (gx, z * 4 + yl * 2 + (1 - core))
    along_x = Place(
        x,
        yh,
        (yh * 4 + lax.rem(x + 3, 4), gy),
        (yh * 4 + lax.rem(x + 1, 4), gy),
        ((1 - yh) * 4 + x, gy),
        sib,
        core,
        lambda p, r: r * 2 + p,
    )
    along_z = Place(
        z,
        yl,
        (gx, lax.rem(z + 3, 4) * 4 + yl * 2 + core),
        (gx, lax.rem(z + 1, 4) * 4 + yl * 2 + core),
        (gx, z * 4 + (1 - yl) * 2 + core),
        sib,
        core,
        lambda p, r: r * 2 + p,
    )

    loads = []

    def load(src, dst):
        copy = pltpu.make_async_copy(src, dst, load_sem.at[len(loads)])
        copy.start()
        loads.append(copy)

    load(w_out, wo)
    mine, theirs = pl.multiple_of(core * half, LANES), pl.multiple_of((1 - core) * half, LANES)
    deep = pl.ds(pl.multiple_of(core * depth, depth), depth)
    load(w_gate.at[:, pl.ds(mine, half)], wgu.at[deep, pl.ds(0, half)])
    load(w_up.at[:, pl.ds(mine, half)], wgu.at[deep, pl.ds(half, half)])
    load(w_down, wd)

    barrier = pltpu.get_barrier_semaphore()
    for device in (along_x.prev, along_x.follow, along_x.pair, along_z.prev, along_z.follow, along_z.pair, sib):
        pl.semaphore_signal(barrier, inc=1, device_id=device, device_id_type=MESH)
    pl.semaphore_wait(barrier, 7)

    gather_a = Gather(along_z, lambda k, c, b: attn_all.at[k, b, c], ga_send, ga_recv)
    gather_b = Gather(along_x, lambda k, c, b: normed_all.at[k, c, b], gb_send, gb_recv)
    gather_c = Gather(along_z, lambda k, c, b: hidden_all.at[k, c, b], gc_send, gc_recv)
    scatter_a = Scatter(along_x, lambda k: proj.at[k], far_a, near_a, last_a, sa_send, sa_recv)
    scatter_b = Scatter(along_z, lambda k: sums.at[k % 2], far_b, near_b, last_b, sb_send, sb_recv)
    scatter_c = Scatter(along_x, lambda k: proj.at[k], far_c, near_c, last_c, sc_send, sc_recv)

    swaps = [
        remote(
            w.at[:, pl.ds(theirs, half)],
            wgu.at[deep, pl.ds(n * half, half)],
            swap_send.at[n],
            swap_recv.at[n],
            sib,
        )
        for n, w in enumerate((w_gate, w_up))
    ]

    visible[...] = visible_nodes(parents[...], tree_size[0])

    def start(k):
        nodes = slice(k * NODES, (k + 1) * NODES)
        node = lax.broadcasted_iota(jnp.int32, (NODES, 1), 0) + k * NODES
        attn_all[k, along_z.block(yl, 0), core] = attend(
            queries[nodes, :], visible[nodes, :], node < tree_size[0], cache_len[0], tree_kv[...], cache, page_table
        )
        gather_a.step1(k)

    def project(k):
        gather_a.step5(k)
        if k == 0:
            loads[0].wait()

        multiply(
            lambda: jnp.concatenate(
                [attn_all[k, q].reshape(BLOCK, attn_all.shape[-1]) for q in (0, 4, 1, 5, 2, 6, 3, 7)], axis=0
            ),
            wo,
            proj.at[k],
        )
        scatter_a.step1(k)
        if k == 0:
            for copy in swaps:
                copy.start()

    def norm(k):
        projected = scatter_a.step4(k)
        rows = jnp.concatenate([resid[r * MAXTREE + k * NODES : r * MAXTREE + (k + 1) * NODES, :] for r in (0, 1)], axis=0)
        value = (rows.astype(F32) + projected).astype(BF)
        hid[k] = value
        wide = value.astype(F32)
        mine = along_x.block(yh, 0)
        normed_all[k, core, mine, :, 0:width] = (wide * gain[...].astype(F32).reshape(1, width)).astype(BF)
        squares = jnp.sum(wide * wide, axis=1, keepdims=True)
        normed_all[k, core, mine, :, width:] = jnp.broadcast_to(squares, (BLOCK, LANES)).astype(BF)
        gather_b.step1(k)

    def gate_up(k):
        gather_b.step5(k)
        if k == 0:
            loads[1].wait()
            loads[2].wait()
            for copy in swaps:
                copy.wait()
        if k >= 2:
            scatter_b.close(k - 2)
        part = sums.at[k % 2]

        multiply(
            lambda: jnp.concatenate(
                [normed_all[k, c, :, :, 0:width].reshape(ROWS, width) for c in (0, 1)], axis=1
            ),
            wgu,
            part,
        )
        squares = normed_all[k, 0, :, :, width:].astype(F32) + normed_all[k, 1, :, :, width:].astype(F32)
        part[:, :, 2 * half :] = squares.astype(BF)
        scatter_b.step1(k)

    def activate(k):
        total = scatter_b.step4(k)
        scale = lax.rsqrt(total[:, 2 * half : 2 * half + 1] / D + EPSILON)
        gate = total[:, 0:half] * scale
        up = total[:, half : 2 * half] * scale
        hidden_all[k, core, along_z.block(yl, 0)] = (gate / (1.0 + jnp.exp(-gate)) * up).astype(BF)
        gather_c.step1(k)

    def down(k):
        gather_c.step5(k)
        if k == 0:
            loads[3].wait()
        scatter_a.close(k)

        multiply(
            lambda: jnp.concatenate([hidden_all[k, c].reshape(ROWS, half) for c in (0, 1)], axis=1), wd, proj.at[k]
        )
        scatter_c.step1(k)

    def finish(k):
        total = (hid[k].astype(F32) + scatter_c.step4(k)).astype(BF)
        for r in (0, 1):
            out[r * MAXTREE + k * NODES : r * MAXTREE + (k + 1) * NODES, :] = total[r * NODES : (r + 1) * NODES, :]

    stages = [
        start,
        gather_a.step2,
        gather_a.step3,
        gather_a.step4,
        project,
        scatter_a.step2,
        scatter_a.step3,
        norm,
        gather_b.step2,
        gather_b.step3,
        gather_b.step4,
        gate_up,
        scatter_b.step2,
        scatter_b.step3,
        activate,
        gather_c.step2,
        gather_c.step3,
        gather_c.step4,
        down,
        scatter_c.step2,
        scatter_c.step3,
        finish,
    ]
    ahead = [iter(stages) for k in range(CHUNKS)]
    for k in TURNS:
        next(ahead[k])(k)
    for group in (gather_a, gather_b, gather_c, scatter_a, scatter_b, scatter_c):
        for k in range(CHUNKS):
            group.close(k)


TURNS = (
    0, 1, 0, 3, 0, 1, 2, 0, 1, 0, 2, 1, 0, 1, 2, 3, 0, 1, 2, 3, 0, 2,
    1, 3, 0, 2, 0, 1, 3, 0, 2, 1, 0, 1, 2, 3, 1, 2, 0, 3, 1, 2, 0, 3,
    2, 1, 0, 2, 1, 3, 3, 0, 3, 1, 2, 0, 3, 2, 0, 3, 0, 2, 1, 3, 2, 1,
    0, 2, 3, 1, 0, 2, 3, 1, 3, 2, 1, 3, 2, 3, 1, 3, 2, 0, 3, 2, 1, 3,
)


def layer(page_table, cache_len, tree_size, parents, queries, tree_kv, cache, resid, gain, w_out, w_gate, w_up, w_down):
    heads, width = w_out.shape
    depth, units = w_gate.shape
    half = units // 2
    sums = 2 * half + LANES
    vmem = pl.BlockSpec(memory_space=pltpu.VMEM)
    smem = pl.BlockSpec(memory_space=pltpu.SMEM)
    hbm = pl.BlockSpec(memory_space=pl.ANY)
    sem = pltpu.SemaphoreType.DMA

    def scatter_buffers(lanes):
        return [
            pltpu.VMEM((CHUNKS, 2, BLOCK, lanes), BF),
            pltpu.VMEM((CHUNKS, 2, 2, BLOCK, lanes), BF),
            pltpu.VMEM((CHUNKS, BLOCK, lanes), BF),
        ]

    scratch = [
        pltpu.VMEM((heads, width), BF),
        pltpu.VMEM((2 * depth, units), BF),
        pltpu.VMEM((units, width), BF),
        pltpu.VMEM((CHUNKS, 8, 2, NODES, heads), BF),
        pltpu.VMEM((CHUNKS, 8, BLOCK, width), BF),
        pltpu.VMEM((CHUNKS, BLOCK, width), BF),
        pltpu.VMEM((CHUNKS, 2, 8, BLOCK, width + LANES), BF),
        pltpu.VMEM((2, 8, BLOCK, sums), BF),
        pltpu.VMEM((CHUNKS, 2, 8, BLOCK, half), BF),
        pltpu.VMEM((MAXTREE, MAXTREE), F32),
        *scatter_buffers(width),
        *scatter_buffers(sums),
        *scatter_buffers(width),
        sem((4,)),
        sem((2,)),
        sem((2,)),
        *[sem((CHUNKS, 11))] * 6,
        *[sem((CHUNKS, 7))] * 6,
    ]
    return pl.pallas_call(
        layer_kernel,
        out_shape=jax.ShapeDtypeStruct(resid.shape, BF),
        in_specs=[smem, smem, smem, vmem, vmem, vmem, vmem, vmem, vmem, hbm, hbm, hbm, hbm],
        out_specs=vmem,
        scratch_shapes=scratch,
        compiler_params=pltpu.CompilerParams(
            collective_id=0, has_side_effects=True, vmem_limit_bytes=62 * 1024 * 1024
        ),
        cost_estimate=pl.CostEstimate(
            flops=2 * 1024 * (heads * width + 3 * depth * units), bytes_accessed=26 * 1024 * 1024, transcendentals=0
        ),
    )(
        page_table,
        cache_len,
        tree_size,
        parents,
        queries,
        tree_kv,
        cache,
        resid,
        gain,
        w_out,
        w_gate,
        w_up,
        w_down,
    )


def body(
    resid,
    queries,
    tree_kv,
    cache,
    page_table,
    cache_len,
    tree_size,
    parents,
    w_out,
    gain,
    w_gate,
    w_up,
    w_down,
):
    return layer(
        page_table,
        cache_len,
        tree_size,
        parents,
        queries,
        tree_kv,
        cache,
        resid,
        gain,
        w_out,
        w_gate,
        w_up,
        w_down,
    )


def solution(mesh):
    in_specs = (
        P("gx", "gy"),
        P("gy", "gx"),
        P("gy", "gx"),
        P("gx", "gy", None, None),
        P("gy", None),
        P("gy"),
        P("gy"),
        P("gy", None),
        P("gx", "gy"),
        P("gy"),
        P("gy", "gx"),
        P("gy", "gx"),
        P("gx", "gy"),
    )
    out_specs = P("gx", "gy")
    return jax.shard_map(body, mesh=mesh, in_specs=in_specs, out_specs=out_specs, check_vma=False)
```

```python
import jax
import jax.numpy as jnp
from jax import lax
from jax.experimental import pallas as pl
from jax.experimental.pallas import tpu as pltpu
from jax.sharding import PartitionSpec as P

D = 16384
HD = 128
MAXTREE = 64
PAGE = 128
MAXPAGES = 8
EPSILON = 1e-05

MESH = pl.DeviceIdType.MESH
BF = jnp.bfloat16
F32 = jnp.float32

CHUNKS = 4
NODES = MAXTREE // CHUNKS
BLOCK = 2 * NODES
ROWS = 8 * BLOCK
LANES = 128
FRONT, BACK = pl.ds(0, BLOCK // 2), pl.ds(BLOCK // 2, BLOCK // 2)
TILE = 1024


def visible_nodes(parents, tree_len):
    shape = (MAXTREE, MAXTREE)
    column, row = lax.broadcasted_iota(jnp.int32, shape, 1), lax.broadcasted_iota(jnp.int32, shape, 0)
    eye = jnp.where(row == column, 1.0, 0.0)
    reach = eye + jnp.where(parents == row, 1.0, 0.0)
    for sweep in range((MAXTREE - 1).bit_length()):
        held = reach.astype(BF)
        reach = jnp.minimum(jnp.dot(held, held, preferred_element_type=F32), 1.0)
    turned = lax.dot_general(
        reach.astype(BF), eye.astype(BF), (((0,), (0,)), ((), ())), preferred_element_type=F32
    )
    return jnp.where(column < tree_len, turned, 0.0)


def attend(query, visible, live, cached, tree_kv, cache, page_table):
    heads = query.shape[1] // HD
    keys = jnp.concatenate([query[:, h * HD : (h + 1) * HD] for h in range(heads)], axis=0)
    contract = (((1,), (1,)), ((), ()))
    context = cache[0].reshape(MAXPAGES * PAGE, 2 * HD)
    scale = HD ** (-0.5)
    ctx_scores = lax.dot_general(keys, context[:, 0:HD], contract, preferred_element_type=F32) * scale
    tree_scores = lax.dot_general(keys, tree_kv[:, 0:HD], contract, preferred_element_type=F32) * scale
    offset = lax.broadcasted_iota(jnp.int32, (1, PAGE), 1)
    bounds = []
    for page in range(MAXPAGES):
        place = jnp.int32(0)
        for p in range(1, MAXPAGES):
            place = jnp.where(page_table[0, p] == page, p, place)
        bounds.append(offset < cached - place * PAGE)
    allowed = jnp.concatenate([jnp.where(bound, 1.0, 0.0) for bound in bounds], axis=1)
    ctx_scores = jnp.where(allowed > 0.5, ctx_scores, -1e30)
    seen = jnp.concatenate([visible] * heads, axis=0)
    tree_scores = jnp.where(seen > 0.5, tree_scores, -1e30)
    row_max = jnp.maximum(
        jnp.max(ctx_scores, axis=-1, keepdims=True), jnp.max(tree_scores, axis=-1, keepdims=True)
    )
    ctx_exp = jnp.exp(ctx_scores - row_max)
    tree_exp = jnp.exp(tree_scores - row_max)
    total = jnp.sum(ctx_exp, axis=-1, keepdims=True) + jnp.sum(tree_exp, axis=-1, keepdims=True)
    share = 1.0 / total
    mixed = jnp.dot((ctx_exp * share).astype(BF), context[:, HD:], preferred_element_type=F32)
    mixed += jnp.dot((tree_exp * share).astype(BF), tree_kv[:, HD:], preferred_element_type=F32)
    count = query.shape[0]
    parts = [jnp.where(live, mixed[h * count : (h + 1) * count, :], 0.0).astype(BF) for h in range(heads)]
    return jnp.concatenate(parts, axis=1)


def remote(src, dst, send_sem, recv_sem, device):
    return pltpu.make_async_remote_copy(
        src_ref=src,
        dst_ref=dst,
        send_sem=send_sem,
        recv_sem=recv_sem,
        device_id=device,
        device_id_type=MESH,
    )


def multiply(rows, weights, result):
    width = weights.shape[1]

    def columns(at, size):
        product = jnp.dot(rows(), weights[:, pl.ds(at, size)], preferred_element_type=F32)
        result[:, :, pl.ds(at, size)] = product.astype(BF).reshape(8, BLOCK, size)

    def tile(n, carry):
        columns(pl.multiple_of(n * TILE, TILE), TILE)
        return carry

    lax.fori_loop(0, width // TILE, tile, 0)
    if width % TILE:
        columns(width - width % TILE, width % TILE)


class Place:
    def __init__(self, r, p, prev, follow, pair, sib, core, index):
        self.r, self.p = r, p
        self.prev, self.follow, self.pair, self.sib = prev, follow, pair, sib
        self.core = core
        self.index = index

    def block(self, p, shift):
        return self.index(p, lax.rem(self.r + (4 + shift), 4))


class PairScatter:
    def __init__(self, place, part, first, far, near, last, send, recv):
        self.at = place
        self.part, self.first, self.far, self.near, self.last = part, first, far, near, last
        self.send, self.recv = send, recv
        self.open = {}

    def push(self, k, src, dst, sem, device):
        copy = remote(src, dst, self.send.at[k, sem], self.recv.at[k, sem], device)
        copy.start()
        self.open.setdefault(k, []).append(copy)

    def arrived(self, k, ref, sem):
        remote(ref, ref, self.send.at[k, sem], self.recv.at[k, sem], self.at.pair).wait_recv()

    def step1(self, k):
        at, part = self.at, self.part(k)
        p, other = at.p, 1 - at.p
        self.push(k, part.at[at.block(other, 2)], self.first.at[k], 0, at.pair)
        self.push(k, part.at[at.block(other, 1)], self.near.at[k, 0, other], 3, at.follow)
        self.push(k, part.at[at.block(other, -1)], self.near.at[k, 1, other], 4, at.prev)
        self.push(k, part.at[at.block(p, 1), BACK], self.near.at[k, 0, p, BACK], 6, at.follow)
        self.push(k, part.at[at.block(p, -1), FRONT], self.near.at[k, 1, p, FRONT], 8, at.prev)

    def step2(self, k):
        at, part = self.at, self.part(k)
        self.arrived(k, self.first.at[k], 0)
        mine = at.block(at.p, 2)
        part[mine] = (part[mine].astype(F32) + self.first[k].astype(F32)).astype(BF)
        self.push(k, part.at[mine, FRONT], self.far.at[k, 0], 1, at.follow)
        self.push(k, part.at[mine, BACK], self.far.at[k, 1], 2, at.prev)

    def ring_sum(self, k, p):
        return (
            self.part(k)[self.at.block(p, 0)].astype(F32)
            + self.near[k, 0, p].astype(F32)
            + self.near[k, 1, p].astype(F32)
        )

    def step3(self, k):
        at, part = self.at, self.part(k)
        other = 1 - at.p
        self.arrived(k, self.near.at[k, 0, other], 3)
        self.arrived(k, self.near.at[k, 1, other], 4)
        theirs = at.block(other, 0)
        part[theirs] = self.ring_sum(k, other).astype(BF)
        self.push(k, part.at[theirs], self.last.at[k], 9, at.pair)

    def step4(self, k):
        at, part = self.at, self.part(k)
        for way, (shift, rows, sem, device) in enumerate(((1, FRONT, 5, at.follow), (-1, BACK, 7, at.prev))):
            self.arrived(k, self.far.at[k, way], 1 + way)
            mine = at.block(at.p, shift)
            part[mine, rows] = (part[mine, rows].astype(F32) + self.far[k, way].astype(F32)).astype(BF)
            self.push(k, part.at[mine, rows], self.near.at[k, way, at.p, rows], sem, device)

    def step5(self, k):
        p = self.at.p
        for way, (added, alone) in enumerate(((FRONT, BACK), (BACK, FRONT))):
            self.arrived(k, self.near.at[k, way, p, added], 5 + 2 * way)
            self.arrived(k, self.near.at[k, way, p, alone], 6 + 2 * way)
        self.arrived(k, self.last.at[k], 9)
        return self.ring_sum(k, p) + self.last[k].astype(F32)

    def close(self, k):
        for copy in self.open.pop(k, []):
            copy.wait_send()


class Gather:
    def __init__(self, place, ref, send, recv):
        self.at, self.ref = place, ref
        self.send, self.recv = send, recv
        self.open = {}

    def push(self, k, block, sem, device):
        ref = self.ref(k, self.at.core, block)
        copy = remote(ref, ref, self.send.at[k, sem], self.recv.at[k, sem], device)
        copy.start()
        self.open.setdefault(k, []).append(copy)

    def arrived(self, k, block, sem, core):
        ref = self.ref(k, core, block)
        remote(ref, ref, self.send.at[k, sem], self.recv.at[k, sem], self.at.pair).wait_recv()

    def both(self, shift):
        return pl.ds(self.at.block(0, shift), 2)

    def share(self, k, shift):
        self.push(k, self.both(shift), 7 + shift % 4, self.at.sib)

    def step1(self, k):
        at = self.at
        mine = at.block(at.p, 0)
        self.push(k, mine, 0, at.pair)
        self.push(k, mine, 1 + at.p, at.follow)
        self.push(k, mine, 3 + at.p, at.prev)

    def step2(self, k):
        at = self.at
        other = 1 - at.p
        block = at.block(other, 0)
        self.arrived(k, block, 0, at.core)
        self.push(k, block, 1 + other, at.follow)
        self.push(k, block, 3 + other, at.prev)
        self.share(k, 0)

    def step3(self, k):
        at = self.at
        left, right = at.block(0, -1), at.block(1, 1)
        self.arrived(k, left, 1, at.core)
        self.push(k, left, 5, at.follow)
        self.arrived(k, right, 4, at.core)
        self.push(k, right, 6, at.prev)
        self.arrived(k, at.block(1, -1), 2, at.core)
        self.share(k, -1)
        self.arrived(k, at.block(0, 1), 3, at.core)
        self.share(k, 1)

    def step4(self, k):
        at = self.at
        self.arrived(k, at.block(0, 2), 5, at.core)
        self.arrived(k, at.block(1, 2), 6, at.core)
        self.share(k, 2)

    def step5(self, k):
        for shift in (0, 1, -1, 2):
            self.arrived(k, self.both(shift), 7 + shift % 4, 1 - self.at.core)

    def close(self, k):
        for copy in self.open.pop(k, []):
            copy.wait_send()


def layer_kernel(
    page_table,
    cache_len,
    tree_size,
    parents,
    queries,
    tree_kv,
    cache,
    resid,
    gain,
    w_out,
    w_gate,
    w_up,
    w_down,
    out,
    wo,
    wgu,
    wd,
    attn_all,
    proj,
    hid,
    normed_all,
    sums,
    hidden_all,
    visible,
    first_a,
    far_a,
    near_a,
    last_a,
    first_b,
    far_b,
    near_b,
    last_b,
    first_c,
    far_c,
    near_c,
    last_c,
    load_sem,
    swap_send,
    swap_recv,
    ga_send,
    ga_recv,
    gb_send,
    gb_recv,
    gc_send,
    gc_recv,
    sa_send,
    sa_recv,
    sb_send,
    sb_recv,
    sc_send,
    sc_recv,
):
    gx, gy = lax.axis_index("gx"), lax.axis_index("gy")
    yh, x = lax.div(gx, 4), lax.rem(gx, 4)
    z, yl, core = lax.div(gy, 4), lax.rem(lax.div(gy, 2), 2), lax.rem(gy, 2)
    width = wo.shape[1]
    half = wgu.shape[1] // 2
    depth = w_gate.shape[0]

    sib = (gx, z * 4 + yl * 2 + (1 - core))
    along_x = Place(
        x,
        yh,
        (yh * 4 + lax.rem(x + 3, 4), gy),
        (yh * 4 + lax.rem(x + 1, 4), gy),
        ((1 - yh) * 4 + x, gy),
        sib,
        core,
        lambda p, r: r * 2 + p,
    )
    along_z = Place(
        z,
        yl,
        (gx, lax.rem(z + 3, 4) * 4 + yl * 2 + core),
        (gx, lax.rem(z + 1, 4) * 4 + yl * 2 + core),
        (gx, z * 4 + (1 - yl) * 2 + core),
        sib,
        core,
        lambda p, r: r * 2 + p,
    )

    loads = []

    def load(src, dst):
        copy = pltpu.make_async_copy(src, dst, load_sem.at[len(loads)])
        copy.start()
        loads.append(copy)

    load(w_out, wo)
    mine, theirs = pl.multiple_of(core * half, LANES), pl.multiple_of((1 - core) * half, LANES)
    deep = pl.ds(pl.multiple_of(core * depth, depth), depth)
    load(w_gate.at[:, pl.ds(mine, half)], wgu.at[deep, pl.ds(0, half)])
    load(w_up.at[:, pl.ds(mine, half)], wgu.at[deep, pl.ds(half, half)])
    load(w_down, wd)

    barrier = pltpu.get_barrier_semaphore()
    for device in (along_x.prev, along_x.follow, along_x.pair, along_z.prev, along_z.follow, along_z.pair, sib):
        pl.semaphore_signal(barrier, inc=1, device_id=device, device_id_type=MESH)
    pl.semaphore_wait(barrier, 7)

    gather_a = Gather(along_z, lambda k, c, b: attn_all.at[k, b, c], ga_send, ga_recv)
    gather_b = Gather(along_x, lambda k, c, b: normed_all.at[k, c, b], gb_send, gb_recv)
    gather_c = Gather(along_z, lambda k, c, b: hidden_all.at[k, c, b], gc_send, gc_recv)
    scatter_a = PairScatter(along_x, lambda k: proj.at[k], first_a, far_a, near_a, last_a, sa_send, sa_recv)
    scatter_b = PairScatter(along_z, lambda k: sums.at[k % 2], first_b, far_b, near_b, last_b, sb_send, sb_recv)
    scatter_c = PairScatter(along_x, lambda k: proj.at[k], first_c, far_c, near_c, last_c, sc_send, sc_recv)

    swaps = [
        remote(
            w.at[:, pl.ds(theirs, half)],
            wgu.at[deep, pl.ds(n * half, half)],
            swap_send.at[n],
            swap_recv.at[n],
            sib,
        )
        for n, w in enumerate((w_gate, w_up))
    ]

    visible[...] = visible_nodes(parents[...], tree_size[0])

    def start(k):
        nodes = slice(k * NODES, (k + 1) * NODES)
        node = lax.broadcasted_iota(jnp.int32, (NODES, 1), 0) + k * NODES
        attn_all[k, along_z.block(yl, 0), core] = attend(
            queries[nodes, :], visible[nodes, :], node < tree_size[0], cache_len[0], tree_kv[...], cache, page_table
        )
        gather_a.step1(k)

    def project(k):
        gather_a.step5(k)
        if k == 0:
            loads[0].wait()

        multiply(
            lambda: jnp.concatenate(
                [attn_all[k, q].reshape(BLOCK, attn_all.shape[-1]) for q in (0, 4, 1, 5, 2, 6, 3, 7)], axis=0
            ),
            wo,
            proj.at[k],
        )
        scatter_a.step1(k)
        if k == 0:
            for copy in swaps:
                copy.start()

    def norm(k):
        projected = scatter_a.step5(k)
        rows = jnp.concatenate([resid[r * MAXTREE + k * NODES : r * MAXTREE + (k + 1) * NODES, :] for r in (0, 1)], axis=0)
        value = (rows.astype(F32) + projected).astype(BF)
        hid[k] = value
        wide = value.astype(F32)
        mine = along_x.block(yh, 0)
        normed_all[k, core, mine, :, 0:width] = (wide * gain[...].astype(F32).reshape(1, width)).astype(BF)
        squares = jnp.sum(wide * wide, axis=1, keepdims=True)
        normed_all[k, core, mine, :, width:] = jnp.broadcast_to(squares, (BLOCK, LANES)).astype(BF)
        gather_b.step1(k)

    def gate_up(k):
        gather_b.step5(k)
        if k == 0:
            loads[1].wait()
            loads[2].wait()
            for copy in swaps:
                copy.wait()
        if k >= 2:
            scatter_b.close(k - 2)
        part = sums.at[k % 2]

        multiply(
            lambda: jnp.concatenate(
                [normed_all[k, c, :, :, 0:width].reshape(ROWS, width) for c in (0, 1)], axis=1
            ),
            wgu,
            part,
        )
        squares = normed_all[k, 0, :, :, width:].astype(F32) + normed_all[k, 1, :, :, width:].astype(F32)
        part[:, :, 2 * half :] = squares.astype(BF)
        scatter_b.step1(k)

    def activate(k):
        total = scatter_b.step5(k)
        scale = lax.rsqrt(total[:, 2 * half : 2 * half + 1] / D + EPSILON)
        gate = total[:, 0:half] * scale
        up = total[:, half : 2 * half] * scale
        hidden_all[k, core, along_z.block(yl, 0)] = (gate / (1.0 + jnp.exp(-gate)) * up).astype(BF)
        gather_c.step1(k)

    def down(k):
        gather_c.step5(k)
        if k == 0:
            loads[3].wait()
        scatter_a.close(k)

        multiply(
            lambda: jnp.concatenate([hidden_all[k, c].reshape(ROWS, half) for c in (0, 1)], axis=1), wd, proj.at[k]
        )
        scatter_c.step1(k)

    def finish(k):
        total = (hid[k].astype(F32) + scatter_c.step5(k)).astype(BF)
        for r in (0, 1):
            out[r * MAXTREE + k * NODES : r * MAXTREE + (k + 1) * NODES, :] = total[r * NODES : (r + 1) * NODES, :]

    stages = [
        start,
        gather_a.step2,
        gather_a.step3,
        gather_a.step4,
        project,
        scatter_a.step2,
        scatter_a.step3,
        scatter_a.step4,
        norm,
        gather_b.step2,
        gather_b.step3,
        gather_b.step4,
        gate_up,
        scatter_b.step2,
        scatter_b.step3,
        scatter_b.step4,
        activate,
        gather_c.step2,
        gather_c.step3,
        gather_c.step4,
        down,
        scatter_c.step2,
        scatter_c.step3,
        scatter_c.step4,
        finish,
    ]
    ahead = [iter(stages) for k in range(CHUNKS)]
    for k in TURNS:
        next(ahead[k])(k)
    for group in (gather_a, gather_b, gather_c, scatter_a, scatter_b, scatter_c):
        for k in range(CHUNKS):
            group.close(k)


TURNS = (
    0, 1, 0, 2, 0, 3, 0, 1, 2, 0, 3, 1, 2, 0, 0, 1, 0, 1, 0, 3, 1, 1,
    2, 1, 0, 2, 3, 0, 1, 3, 2, 0, 2, 1, 0, 2, 1, 2, 3, 1, 0, 3, 2, 0,
    3, 0, 1, 2, 0, 3, 2, 1, 2, 3, 1, 3, 1, 2, 0, 1, 3, 2, 2, 0, 1, 3,
    1, 0, 0, 3, 2, 1, 3, 3, 2, 1, 2, 3, 1, 1, 0, 2, 3, 2, 3, 0, 2, 3,
    2, 0, 3, 2, 0, 1, 3, 3, 3, 2, 1, 3,
)


def layer(page_table, cache_len, tree_size, parents, queries, tree_kv, cache, resid, gain, w_out, w_gate, w_up, w_down):
    heads, width = w_out.shape
    depth, units = w_gate.shape
    half = units // 2
    sums = 2 * half + LANES
    vmem = pl.BlockSpec(memory_space=pltpu.VMEM)
    smem = pl.BlockSpec(memory_space=pltpu.SMEM)
    hbm = pl.BlockSpec(memory_space=pl.ANY)
    sem = pltpu.SemaphoreType.DMA

    def scatter_buffers(lanes):
        return [
            pltpu.VMEM((CHUNKS, BLOCK, lanes), BF),
            pltpu.VMEM((CHUNKS, 2, BLOCK // 2, lanes), BF),
            pltpu.VMEM((CHUNKS, 2, 2, BLOCK, lanes), BF),
            pltpu.VMEM((CHUNKS, BLOCK, lanes), BF),
        ]

    scratch = [
        pltpu.VMEM((heads, width), BF),
        pltpu.VMEM((2 * depth, units), BF),
        pltpu.VMEM((units, width), BF),
        pltpu.VMEM((CHUNKS, 8, 2, NODES, heads), BF),
        pltpu.VMEM((CHUNKS, 8, BLOCK, width), BF),
        pltpu.VMEM((CHUNKS, BLOCK, width), BF),
        pltpu.VMEM((CHUNKS, 2, 8, BLOCK, width + LANES), BF),
        pltpu.VMEM((2, 8, BLOCK, sums), BF),
        pltpu.VMEM((CHUNKS, 2, 8, BLOCK, half), BF),
        pltpu.VMEM((MAXTREE, MAXTREE), F32),
        *scatter_buffers(width),
        *scatter_buffers(sums),
        *scatter_buffers(width),
        sem((4,)),
        sem((2,)),
        sem((2,)),
        *[sem((CHUNKS, 11))] * 6,
        *[sem((CHUNKS, 10))] * 6,
    ]
    return pl.pallas_call(
        layer_kernel,
        out_shape=jax.ShapeDtypeStruct(resid.shape, BF),
        in_specs=[smem, smem, smem, vmem, vmem, vmem, vmem, vmem, vmem, hbm, hbm, hbm, hbm],
        out_specs=vmem,
        scratch_shapes=scratch,
        compiler_params=pltpu.CompilerParams(
            collective_id=0, has_side_effects=True, vmem_limit_bytes=62 * 1024 * 1024
        ),
        cost_estimate=pl.CostEstimate(
            flops=2 * 1024 * (heads * width + 3 * depth * units), bytes_accessed=26 * 1024 * 1024, transcendentals=0
        ),
    )(
        page_table,
        cache_len,
        tree_size,
        parents,
        queries,
        tree_kv,
        cache,
        resid,
        gain,
        w_out,
        w_gate,
        w_up,
        w_down,
    )


def body(
    resid,
    queries,
    tree_kv,
    cache,
    page_table,
    cache_len,
    tree_size,
    parents,
    w_out,
    gain,
    w_gate,
    w_up,
    w_down,
):
    return layer(
        page_table,
        cache_len,
        tree_size,
        parents,
        queries,
        tree_kv,
        cache,
        resid,
        gain,
        w_out,
        w_gate,
        w_up,
        w_down,
    )


def solution(mesh):
    in_specs = (
        P("gx", "gy"),
        P("gy", "gx"),
        P("gy", "gx"),
        P("gx", "gy", None, None),
        P("gy", None),
        P("gy"),
        P("gy"),
        P("gy", None),
        P("gx", "gy"),
        P("gy"),
        P("gy", "gx"),
        P("gy", "gx"),
        P("gx", "gy"),
    )
    out_specs = P("gx", "gy")
    return jax.shard_map(body, mesh=mesh, in_specs=in_specs, out_specs=out_specs, check_vma=False)
```

```python
import jax
import jax.numpy as jnp
from jax import lax
from jax.experimental import pallas as pl
from jax.experimental.pallas import tpu as pltpu
from jax.sharding import PartitionSpec as P

D = 16384
HD = 128
MAXTREE = 64
PAGE = 128
MAXPAGES = 8
EPSILON = 1e-05

MESH = pl.DeviceIdType.MESH
BF = jnp.bfloat16
F32 = jnp.float32

CHUNKS = 4
NODES = MAXTREE // CHUNKS
BLOCK = 2 * NODES
ROWS = 8 * BLOCK
LANES = 128
FRONT, BACK = pl.ds(0, BLOCK // 2), pl.ds(BLOCK // 2, BLOCK // 2)
TILE = 1024
PIECES = 4


def visible_nodes(parents, tree_len):
    shape = (MAXTREE, MAXTREE)
    column, row = lax.broadcasted_iota(jnp.int32, shape, 1), lax.broadcasted_iota(jnp.int32, shape, 0)
    eye = jnp.where(row == column, 1.0, 0.0)
    reach = eye + jnp.where(parents == row, 1.0, 0.0)
    for sweep in range((MAXTREE - 1).bit_length()):
        held = reach.astype(BF)
        reach = jnp.minimum(jnp.dot(held, held, preferred_element_type=F32), 1.0)
    turned = lax.dot_general(
        reach.astype(BF), eye.astype(BF), (((0,), (0,)), ((), ())), preferred_element_type=F32
    )
    return jnp.where(column < tree_len, turned, 0.0)


def attend(query, visible, live, cached, tree_kv, cache, page_table):
    heads = query.shape[1] // HD
    keys = jnp.concatenate([query[:, h * HD : (h + 1) * HD] for h in range(heads)], axis=0)
    contract = (((1,), (1,)), ((), ()))
    context = cache[0].reshape(MAXPAGES * PAGE, 2 * HD)
    scale = HD ** (-0.5)
    ctx_scores = lax.dot_general(keys, context[:, 0:HD], contract, preferred_element_type=F32) * scale
    tree_scores = lax.dot_general(keys, tree_kv[:, 0:HD], contract, preferred_element_type=F32) * scale
    offset = lax.broadcasted_iota(jnp.int32, (1, PAGE), 1)
    bounds = []
    for page in range(MAXPAGES):
        place = jnp.int32(0)
        for p in range(1, MAXPAGES):
            place = jnp.where(page_table[0, p] == page, p, place)
        bounds.append(offset < cached - place * PAGE)
    allowed = jnp.concatenate([jnp.where(bound, 1.0, 0.0) for bound in bounds], axis=1)
    ctx_scores = jnp.where(allowed > 0.5, ctx_scores, -1e30)
    seen = jnp.concatenate([visible] * heads, axis=0)
    tree_scores = jnp.where(seen > 0.5, tree_scores, -1e30)
    row_max = jnp.maximum(
        jnp.max(ctx_scores, axis=-1, keepdims=True), jnp.max(tree_scores, axis=-1, keepdims=True)
    )
    ctx_exp = jnp.exp(ctx_scores - row_max)
    tree_exp = jnp.exp(tree_scores - row_max)
    total = jnp.sum(ctx_exp, axis=-1, keepdims=True) + jnp.sum(tree_exp, axis=-1, keepdims=True)
    share = 1.0 / total
    mixed = jnp.dot((ctx_exp * share).astype(BF), context[:, HD:], preferred_element_type=F32)
    mixed += jnp.dot((tree_exp * share).astype(BF), tree_kv[:, HD:], preferred_element_type=F32)
    count = query.shape[0]
    parts = [jnp.where(live, mixed[h * count : (h + 1) * count, :], 0.0).astype(BF) for h in range(heads)]
    return jnp.concatenate(parts, axis=1)


def remote(src, dst, send_sem, recv_sem, device):
    return pltpu.make_async_remote_copy(
        src_ref=src,
        dst_ref=dst,
        send_sem=send_sem,
        recv_sem=recv_sem,
        device_id=device,
        device_id_type=MESH,
    )


def multiply(rows, weights, result, tile, done):
    width = weights.shape[1]
    for j, at in enumerate(range(0, width, tile)):
        size = min(tile, width - at)
        product = jnp.dot(rows(), weights[:, at : at + size], preferred_element_type=F32)
        result[:, :, at : at + size] = product.astype(BF).reshape(8, BLOCK, size)
        done(j)


class Place:
    def __init__(self, r, p, prev, follow, pair, sib, core, index):
        self.r, self.p = r, p
        self.prev, self.follow, self.pair, self.sib = prev, follow, pair, sib
        self.core = core
        self.index = index

    def block(self, p, shift):
        return self.index(p, lax.rem(self.r + (4 + shift), 4))


class Scatter:
    def __init__(self, place, part, buffers, send, recv, cuts):
        self.at, self.part = place, part
        self.far, self.near, self.last = buffers
        self.send, self.recv = send, recv
        self.cuts = cuts
        self.open = {}

    def push(self, slot, src, dst, sem, device):
        copy = remote(src, dst, self.send.at[slot, sem], self.recv.at[slot, sem], device)
        copy.start()
        return copy

    def hand(self, k, src, dst, sem, device):
        self.open.setdefault(k, []).append(self.push(k * len(self.cuts), src, dst, sem, device))

    def arrived(self, k, ref, sem, pieces=False):
        for j, columns in enumerate(self.cuts if pieces else [None]):
            slot = k * len(self.cuts) + j
            piece = ref.at[:, columns] if pieces else ref
            remote(piece, piece, self.send.at[slot, sem], self.recv.at[slot, sem], self.at.pair).wait_recv()

    def first_sends(self, k):
        at, part = self.at, self.part(k)
        return [
            (part.at[at.block(0, 2)], self.far.at[k, 0], 0, at.follow),
            (part.at[at.block(1, 2)], self.far.at[k, 1], 1, at.prev),
            (part.at[at.block(1, 1)], self.near.at[k, 0, 1], 3, at.follow),
            (part.at[at.block(0, -1)], self.near.at[k, 1, 0], 4, at.prev),
        ]

    def step1(self, k, j):
        columns = self.cuts[j]
        for src, dst, sem, device in self.first_sends(k):
            copy = self.push(k * len(self.cuts) + j, src.at[:, columns], dst.at[:, columns], sem, device)
            self.open.setdefault(k, []).append(copy)

    def step2(self, k):
        at, part = self.at, self.part(k)
        for way, (p, shift, device, sem) in enumerate(((0, 1, at.follow, 2), (1, -1, at.prev, 5))):
            self.arrived(k, self.far.at[k, way], way, True)
            mine = at.block(p, shift)
            part[mine] = (part[mine].astype(F32) + self.far[k, way].astype(F32)).astype(BF)
            self.hand(k, part.at[mine], self.near.at[k, way, p], sem, device)

    def ring_sum(self, k, p):
        return (
            self.part(k)[self.at.block(p, 0)].astype(F32)
            + self.near[k, 0, p].astype(F32)
            + self.near[k, 1, p].astype(F32)
        )

    def step3(self, k):
        at, part = self.at, self.part(k)
        self.arrived(k, self.near.at[k, 0, 0], 2)
        self.arrived(k, self.near.at[k, 0, 1], 3, True)
        self.arrived(k, self.near.at[k, 1, 0], 4, True)
        self.arrived(k, self.near.at[k, 1, 1], 5)
        other = 1 - at.p
        theirs = at.block(other, 0)
        part[theirs] = self.ring_sum(k, other).astype(BF)
        self.hand(k, part.at[theirs], self.last.at[k], 6, at.pair)

    def total(self, k):
        self.arrived(k, self.last.at[k], 6)
        return self.ring_sum(k, self.at.p) + self.last[k].astype(F32)

    def close(self, k):
        for copy in self.open.pop(k, []):
            copy.wait_send()


class PairScatter(Scatter):
    def __init__(self, place, part, buffers, send, recv, cuts):
        super().__init__(place, part, buffers[1:], send, recv, cuts)
        self.first = buffers[0]

    def first_sends(self, k):
        at, part = self.at, self.part(k)
        p, other = at.p, 1 - at.p
        return [
            (part.at[at.block(other, 2)], self.first.at[k], 0, at.pair),
            (part.at[at.block(other, 1)], self.near.at[k, 0, other], 3, at.follow),
            (part.at[at.block(other, -1)], self.near.at[k, 1, other], 4, at.prev),
            (part.at[at.block(p, 1), BACK], self.near.at[k, 0, p, BACK], 6, at.follow),
            (part.at[at.block(p, -1), FRONT], self.near.at[k, 1, p, FRONT], 8, at.prev),
        ]

    def step2(self, k):
        at, part = self.at, self.part(k)
        self.arrived(k, self.first.at[k], 0, True)
        mine = at.block(at.p, 2)
        part[mine] = (part[mine].astype(F32) + self.first[k].astype(F32)).astype(BF)
        self.hand(k, part.at[mine, FRONT], self.far.at[k, 0], 1, at.follow)
        self.hand(k, part.at[mine, BACK], self.far.at[k, 1], 2, at.prev)

    def step3(self, k):
        at, part = self.at, self.part(k)
        other = 1 - at.p
        self.arrived(k, self.near.at[k, 0, other], 3, True)
        self.arrived(k, self.near.at[k, 1, other], 4, True)
        theirs = at.block(other, 0)
        part[theirs] = self.ring_sum(k, other).astype(BF)
        self.hand(k, part.at[theirs], self.last.at[k], 9, at.pair)

    def step4(self, k):
        at, part = self.at, self.part(k)
        for way, (shift, rows, sem, device) in enumerate(((1, FRONT, 5, at.follow), (-1, BACK, 7, at.prev))):
            self.arrived(k, self.far.at[k, way], 1 + way)
            mine = at.block(at.p, shift)
            part[mine, rows] = (part[mine, rows].astype(F32) + self.far[k, way].astype(F32)).astype(BF)
            self.hand(k, part.at[mine, rows], self.near.at[k, way, at.p, rows], sem, device)

    def total(self, k):
        p = self.at.p
        for way, (added, alone) in enumerate(((FRONT, BACK), (BACK, FRONT))):
            self.arrived(k, self.near.at[k, way, p, added], 5 + 2 * way)
            self.arrived(k, self.near.at[k, way, p, alone], 6 + 2 * way, True)
        self.arrived(k, self.last.at[k], 9)
        return self.ring_sum(k, p) + self.last[k].astype(F32)


class Gather:
    def __init__(self, place, ref, send, recv):
        self.at, self.ref = place, ref
        self.send, self.recv = send, recv
        self.open = {}

    def push(self, k, block, sem, device):
        ref = self.ref(k, self.at.core, block)
        copy = remote(ref, ref, self.send.at[k, sem], self.recv.at[k, sem], device)
        copy.start()
        self.open.setdefault(k, []).append(copy)

    def arrived(self, k, block, sem, core):
        ref = self.ref(k, core, block)
        remote(ref, ref, self.send.at[k, sem], self.recv.at[k, sem], self.at.pair).wait_recv()

    def both(self, shift):
        return pl.ds(self.at.block(0, shift), 2)

    def share(self, k, shift):
        self.push(k, self.both(shift), 7 + shift % 4, self.at.sib)

    def step1(self, k):
        at = self.at
        mine = at.block(at.p, 0)
        self.push(k, mine, 0, at.pair)
        self.push(k, mine, 1 + at.p, at.follow)
        self.push(k, mine, 3 + at.p, at.prev)

    def step2(self, k):
        at = self.at
        other = 1 - at.p
        block = at.block(other, 0)
        self.arrived(k, block, 0, at.core)
        self.push(k, block, 1 + other, at.follow)
        self.push(k, block, 3 + other, at.prev)
        self.share(k, 0)

    def step3(self, k):
        at = self.at
        left, right = at.block(0, -1), at.block(1, 1)
        self.arrived(k, left, 1, at.core)
        self.push(k, left, 5, at.follow)
        self.arrived(k, right, 4, at.core)
        self.push(k, right, 6, at.prev)
        self.arrived(k, at.block(1, -1), 2, at.core)
        self.share(k, -1)
        self.arrived(k, at.block(0, 1), 3, at.core)
        self.share(k, 1)

    def step4(self, k):
        at = self.at
        self.arrived(k, at.block(0, 2), 5, at.core)
        self.arrived(k, at.block(1, 2), 6, at.core)
        self.share(k, 2)

    def step5(self, k):
        for shift in (0, 1, -1, 2):
            self.arrived(k, self.both(shift), 7 + shift % 4, 1 - self.at.core)

    def close(self, k):
        for copy in self.open.pop(k, []):
            copy.wait_send()


class PairGather(Gather):
    def hand(self, k, ref, sem, device):
        copy = remote(ref, ref, self.send.at[k, sem], self.recv.at[k, sem], device)
        copy.start()
        self.open.setdefault(k, []).append(copy)

    def landed(self, k, ref, sem):
        remote(ref, ref, self.send.at[k, sem], self.recv.at[k, sem], self.at.pair).wait_recv()

    def step1(self, k):
        at = self.at
        mine = at.block(at.p, 0)
        self.push(k, mine, 0, at.pair)
        self.push(k, mine, 1, at.follow)
        self.push(k, mine, 2, at.prev)

    def step2(self, k):
        at = self.at
        block = at.block(1 - at.p, 0)
        self.arrived(k, block, 0, at.core)
        self.push(k, block, 3, at.follow)
        self.push(k, block, 4, at.prev)
        self.share(k, 0)

    def step3(self, k):
        at = self.at
        left, right = at.block(at.p, -1), at.block(at.p, 1)
        self.arrived(k, left, 1, at.core)
        self.hand(k, self.ref(k, at.core, left).at[FRONT], 5, at.follow)
        self.arrived(k, right, 2, at.core)
        self.hand(k, self.ref(k, at.core, right).at[BACK], 6, at.prev)

    def step4(self, k):
        at = self.at
        self.arrived(k, at.block(1 - at.p, -1), 3, at.core)
        self.share(k, -1)
        self.arrived(k, at.block(1 - at.p, 1), 4, at.core)
        self.share(k, 1)

    def far1(self, k):
        at = self.at
        block = at.block(at.p, 2)
        self.landed(k, self.ref(k, at.core, block).at[FRONT], 5)
        self.landed(k, self.ref(k, at.core, block).at[BACK], 6)
        self.push(k, block, 11, at.pair)

    def far2(self, k):
        at = self.at
        self.arrived(k, at.block(1 - at.p, 2), 11, at.core)
        self.share(k, 2)


def layer_kernel(
    page_table,
    cache_len,
    tree_size,
    parents,
    queries,
    tree_kv,
    cache,
    resid,
    gain,
    w_out,
    w_gate,
    w_up,
    w_down,
    out,
    wo,
    wgu,
    wd,
    attn_all,
    proj,
    hid,
    normed_all,
    sums,
    hidden_all,
    visible,
    far_a,
    near_a,
    last_a,
    first_b,
    far_b,
    near_b,
    last_b,
    far_c,
    near_c,
    last_c,
    load_sem,
    swap_send,
    swap_recv,
    ga_send,
    ga_recv,
    gb_send,
    gb_recv,
    gc_send,
    gc_recv,
    sa_send,
    sa_recv,
    sb_send,
    sb_recv,
    sc_send,
    sc_recv,
):
    gx, gy = lax.axis_index("gx"), lax.axis_index("gy")
    yh, x = lax.div(gx, 4), lax.rem(gx, 4)
    z, yl, core = lax.div(gy, 4), lax.rem(lax.div(gy, 2), 2), lax.rem(gy, 2)
    width = wo.shape[1]
    half = wgu.shape[1] // 2
    depth = w_gate.shape[0]

    sib = (gx, z * 4 + yl * 2 + (1 - core))
    along_x = Place(
        x,
        yh,
        (yh * 4 + lax.rem(x + 3, 4), gy),
        (yh * 4 + lax.rem(x + 1, 4), gy),
        ((1 - yh) * 4 + x, gy),
        sib,
        core,
        lambda p, r: r * 2 + p,
    )
    along_z = Place(
        z,
        yl,
        (gx, lax.rem(z + 3, 4) * 4 + yl * 2 + core),
        (gx, lax.rem(z + 1, 4) * 4 + yl * 2 + core),
        (gx, z * 4 + (1 - yl) * 2 + core),
        sib,
        core,
        lambda p, r: r * 2 + p,
    )

    loads = []

    def load(src, dst):
        copy = pltpu.make_async_copy(src, dst, load_sem.at[len(loads)])
        copy.start()
        loads.append(copy)

    load(w_out, wo)
    mine, theirs = pl.multiple_of(core * half, LANES), pl.multiple_of((1 - core) * half, LANES)
    deep = pl.ds(pl.multiple_of(core * depth, depth), depth)
    load(w_gate.at[:, pl.ds(mine, half)], wgu.at[deep, pl.ds(0, half)])
    load(w_up.at[:, pl.ds(mine, half)], wgu.at[deep, pl.ds(half, half)])
    load(w_down, wd)

    barrier = pltpu.get_barrier_semaphore()
    for device in (along_x.prev, along_x.follow, along_x.pair, along_z.prev, along_z.follow, along_z.pair, sib):
        pl.semaphore_signal(barrier, inc=1, device_id=device, device_id_type=MESH)
    visible[...] = visible_nodes(parents[...], tree_size[0])
    pl.semaphore_wait(barrier, 7)

    side = width // 1
    halves = [pl.ds(at, side) for at in range(0, width, side)]
    quarters = [pl.ds(at, min(TILE, sums.shape[-1] - at)) for at in range(0, sums.shape[-1], TILE)]
    assert len(quarters) == PIECES
    gather_a = Gather(along_z, lambda k, c, b: attn_all.at[k, b, c], ga_send, ga_recv)
    gather_b = Gather(along_x, lambda k, c, b: normed_all.at[k, c, b], gb_send, gb_recv)
    gather_c = PairGather(along_z, lambda k, c, b: hidden_all.at[k, c, b], gc_send, gc_recv)
    scatter_a = Scatter(along_x, lambda k: proj.at[k], (far_a, near_a, last_a), sa_send, sa_recv, halves)
    scatter_b = PairScatter(along_z, lambda k: sums.at[k % 2], (first_b, far_b, near_b, last_b), sb_send, sb_recv, quarters)
    scatter_c = Scatter(along_x, lambda k: proj.at[k], (far_c, near_c, last_c), sc_send, sc_recv, halves)

    swaps = [
        remote(
            w.at[:, pl.ds(theirs, half)],
            wgu.at[deep, pl.ds(n * half, half)],
            swap_send.at[n],
            swap_recv.at[n],
            sib,
        )
        for n, w in enumerate((w_gate, w_up))
    ]
    for copy in swaps:
        copy.start()

    def start(k):
        nodes = slice(k * NODES, (k + 1) * NODES)
        node = lax.broadcasted_iota(jnp.int32, (NODES, 1), 0) + k * NODES
        attn_all[k, along_z.block(yl, 0), core] = attend(
            queries[nodes, :], visible[nodes, :], node < tree_size[0], cache_len[0], tree_kv[...], cache, page_table
        )
        gather_a.step1(k)

    def project(k):
        gather_a.step5(k)
        if k == 0:
            loads[0].wait()

        multiply(
            lambda: jnp.concatenate(
                [attn_all[k, q].reshape(BLOCK, attn_all.shape[-1]) for q in (0, 4, 1, 5, 2, 6, 3, 7)], axis=0
            ),
            wo,
            proj.at[k],
            side,
            lambda j: scatter_a.step1(k, j),
        )

    def norm(k):
        projected = scatter_a.total(k)
        rows = jnp.concatenate([resid[r * MAXTREE + k * NODES : r * MAXTREE + (k + 1) * NODES, :] for r in (0, 1)], axis=0)
        value = (rows.astype(F32) + projected).astype(BF)
        hid[k] = value
        wide = value.astype(F32)
        mine = along_x.block(yh, 0)
        normed_all[k, core, mine, :, 0:width] = (wide * gain[...].astype(F32).reshape(1, width)).astype(BF)
        squares = jnp.sum(wide * wide, axis=1, keepdims=True)
        normed_all[k, core, mine, :, width:] = jnp.broadcast_to(squares, (BLOCK, LANES)).astype(BF)
        gather_b.step1(k)

    def gate_up(k):
        gather_b.step5(k)
        if k == 0:
            loads[1].wait()
            loads[2].wait()
            for copy in swaps:
                copy.wait()
        if k >= 2:
            scatter_b.close(k - 2)
        part = sums.at[k % 2]
        squares = normed_all[k, 0, :, :, width:].astype(F32) + normed_all[k, 1, :, :, width:].astype(F32)
        part[:, :, 2 * half :] = squares.astype(BF)

        multiply(
            lambda: jnp.concatenate(
                [normed_all[k, c, :, :, 0:width].reshape(ROWS, width) for c in (0, 1)], axis=1
            ),
            wgu,
            part,
            TILE,
            lambda j: scatter_b.step1(k, j),
        )

    def activate(k):
        total = scatter_b.total(k)
        scale = lax.rsqrt(total[:, 2 * half : 2 * half + 1] / D + EPSILON)
        gate = total[:, 0:half] * scale
        up = total[:, half : 2 * half] * scale
        hidden_all[k, core, along_z.block(yl, 0)] = (gate / (1.0 + jnp.exp(-gate)) * up).astype(BF)
        gather_c.step1(k)

    def down(k):
        gather_c.step5(k)
        if k == 0:
            loads[3].wait()
        scatter_a.close(k)

        multiply(
            lambda: jnp.concatenate([hidden_all[k, c].reshape(ROWS, half) for c in (0, 1)], axis=1),
            wd,
            proj.at[k],
            side,
            lambda j: scatter_c.step1(k, j),
        )

    def finish(k):
        total = (hid[k].astype(F32) + scatter_c.total(k)).astype(BF)
        for r in (0, 1):
            out[r * MAXTREE + k * NODES : r * MAXTREE + (k + 1) * NODES, :] = total[r * NODES : (r + 1) * NODES, :]

    stages = [
        start,
        gather_a.step2,
        gather_a.step3,
        gather_a.step4,
        project,
        scatter_a.step2,
        scatter_a.step3,
        norm,
        gather_b.step2,
        gather_b.step3,
        gather_b.step4,
        gate_up,
        scatter_b.step2,
        scatter_b.step3,
        scatter_b.step4,
        activate,
        gather_c.step2,
        gather_c.step3,
        gather_c.step4,
        gather_c.far1,
        gather_c.far2,
        down,
        scatter_c.step2,
        scatter_c.step3,
        finish,
    ]
    ahead = [iter(stages) for k in range(CHUNKS)]
    for k in TURNS:
        next(ahead[k])(k)
    for group in (gather_a, gather_b, gather_c, scatter_a, scatter_b, scatter_c):
        for k in range(CHUNKS):
            group.close(k)


TURNS = (
    0, 1, 0, 2, 1, 0, 2, 0, 1, 0, 1, 2, 0, 2, 1, 0, 3, 1, 0, 2, 1, 0, 3, 2,
    0, 1, 3, 0, 2, 3, 1, 0, 1, 2, 0, 3, 1, 0, 0, 3, 1, 2, 0, 2, 3, 1, 0, 1,
    2, 1, 3, 2, 3, 1, 3, 2, 0, 2, 0, 1, 1, 3, 3, 0, 1, 2, 1, 3, 3, 2, 3, 2,
    0, 2, 3, 1, 0, 2, 3, 2, 1, 3, 2, 0, 3, 3, 2, 3, 0, 1, 2, 3, 1, 2, 3, 3,
    1, 2, 0, 3,
)


def layer(page_table, cache_len, tree_size, parents, queries, tree_kv, cache, resid, gain, w_out, w_gate, w_up, w_down):
    heads, width = w_out.shape
    depth, units = w_gate.shape
    half = units // 2
    sums = 2 * half + LANES
    vmem = pl.BlockSpec(memory_space=pltpu.VMEM)
    smem = pl.BlockSpec(memory_space=pltpu.SMEM)
    hbm = pl.BlockSpec(memory_space=pl.ANY)
    sem = pltpu.SemaphoreType.DMA

    def scatter_buffers(lanes, pair):
        first = [pltpu.VMEM((CHUNKS, BLOCK, lanes), BF)] if pair else []
        return [
            *first,
            pltpu.VMEM((CHUNKS, 2, BLOCK // 2 if pair else BLOCK, lanes), BF),
            pltpu.VMEM((CHUNKS, 2, 2, BLOCK, lanes), BF),
            pltpu.VMEM((CHUNKS, BLOCK, lanes), BF),
        ]

    scratch = [
        pltpu.VMEM((heads, width), BF),
        pltpu.VMEM((2 * depth, units), BF),
        pltpu.VMEM((units, width), BF),
        pltpu.VMEM((CHUNKS, 8, 2, NODES, heads), BF),
        pltpu.VMEM((CHUNKS, 8, BLOCK, width), BF),
        pltpu.VMEM((CHUNKS, BLOCK, width), BF),
        pltpu.VMEM((CHUNKS, 2, 8, BLOCK, width + LANES), BF),
        pltpu.VMEM((2, 8, BLOCK, sums), BF),
        pltpu.VMEM((CHUNKS, 2, 8, BLOCK, half), BF),
        pltpu.VMEM((MAXTREE, MAXTREE), F32),
        *scatter_buffers(width, False),
        *scatter_buffers(sums, True),
        *scatter_buffers(width, False),
        sem((4,)),
        sem((2,)),
        sem((2,)),
        *[sem((CHUNKS, 12))] * 6,
        *[sem((CHUNKS * PIECES, 10))] * 6,
    ]
    return pl.pallas_call(
        layer_kernel,
        out_shape=jax.ShapeDtypeStruct(resid.shape, BF),
        in_specs=[smem, smem, smem, vmem, vmem, vmem, vmem, vmem, vmem, hbm, hbm, hbm, hbm],
        out_specs=vmem,
        scratch_shapes=scratch,
        compiler_params=pltpu.CompilerParams(
            collective_id=0, has_side_effects=True, vmem_limit_bytes=62 * 1024 * 1024
        ),
        cost_estimate=pl.CostEstimate(
            flops=2 * 1024 * (heads * width + 3 * depth * units), bytes_accessed=26 * 1024 * 1024, transcendentals=0
        ),
    )(
        page_table,
        cache_len,
        tree_size,
        parents,
        queries,
        tree_kv,
        cache,
        resid,
        gain,
        w_out,
        w_gate,
        w_up,
        w_down,
    )


def body(
    resid,
    queries,
    tree_kv,
    cache,
    page_table,
    cache_len,
    tree_size,
    parents,
    w_out,
    gain,
    w_gate,
    w_up,
    w_down,
):
    return layer(
        page_table,
        cache_len,
        tree_size,
        parents,
        queries,
        tree_kv,
        cache,
        resid,
        gain,
        w_out,
        w_gate,
        w_up,
        w_down,
    )


def solution(mesh):
    in_specs = (
        P("gx", "gy"),
        P("gy", "gx"),
        P("gy", "gx"),
        P("gx", "gy", None, None),
        P("gy", None),
        P("gy"),
        P("gy"),
        P("gy", None),
        P("gx", "gy"),
        P("gy"),
        P("gy", "gx"),
        P("gy", "gx"),
        P("gx", "gy"),
    )
    out_specs = P("gx", "gy")
    return jax.shard_map(body, mesh=mesh, in_specs=in_specs, out_specs=out_specs, check_vma=False)
```

```python
import jax
import jax.numpy as jnp
from jax import lax
from jax.experimental import pallas as pl
from jax.experimental.pallas import tpu as pltpu
from jax.sharding import PartitionSpec as P

D = 16384
HD = 128
MAXTREE = 64
PAGE = 128
MAXPAGES = 8
EPSILON = 1e-05

MESH = pl.DeviceIdType.MESH
BF = jnp.bfloat16
F32 = jnp.float32

CHUNKS = 4
NODES = MAXTREE // CHUNKS
BLOCK = 2 * NODES
ROWS = 8 * BLOCK
LANES = 128
GROUP = 4
FRONT, BACK = pl.ds(0, BLOCK // 2), pl.ds(BLOCK // 2, BLOCK // 2)
TILE = 1024
INNER = 512
STRIP = 384
PIECES = 4


def visible_nodes(parents, tree_len):
    shape = (MAXTREE, MAXTREE)
    column, row = lax.broadcasted_iota(jnp.int32, shape, 1), lax.broadcasted_iota(jnp.int32, shape, 0)
    eye = jnp.where(row == column, 1.0, 0.0)
    reach = eye + jnp.where(parents == row, 1.0, 0.0)
    for sweep in range((MAXTREE - 1).bit_length()):
        held = reach.astype(BF)
        reach = jnp.minimum(jnp.dot(held, held, preferred_element_type=F32), 1.0)
    turned = lax.dot_general(
        reach.astype(BF), eye.astype(BF), (((0,), (0,)), ((), ())), preferred_element_type=F32
    )
    return jnp.where(column < tree_len, turned, 0.0)


def attend(queries, nodes, visible, live, cached, tree_kv, cache, page_table, out):
    contract = (((1,), (1,)), ((), ()))
    scale = HD ** (-0.5)
    offset = lax.broadcasted_iota(jnp.int32, (1, PAGE), 1)
    bounds = []
    for page in range(MAXPAGES):
        place = jnp.int32(0)
        for p in range(1, MAXPAGES):
            place = jnp.where(page_table[0, p] == page, p, place)
        bounds.append(offset < cached - place * PAGE)
    allowed = jnp.concatenate([jnp.where(bound, 1.0, 0.0) for bound in bounds], axis=1)
    seen = jnp.concatenate([visible] * GROUP, axis=0)

    def group(g, carry):
        columns = pl.ds(pl.multiple_of(g * GROUP * HD, LANES), GROUP * HD)
        query = queries[nodes, columns]
        rows = jnp.concatenate([query[:, h * HD : (h + 1) * HD] for h in range(GROUP)], axis=0)
        keys = cache[0, :, :, 0:HD].reshape(MAXPAGES * PAGE, HD)
        ctx_scores = lax.dot_general(rows, keys, contract, preferred_element_type=F32) * scale
        tree_scores = lax.dot_general(rows, tree_kv[:, 0:HD], contract, preferred_element_type=F32) * scale
        ctx_scores = jnp.where(allowed > 0.5, ctx_scores, -1e30)
        tree_scores = jnp.where(seen > 0.5, tree_scores, -1e30)
        row_max = jnp.maximum(
            jnp.max(ctx_scores, axis=-1, keepdims=True), jnp.max(tree_scores, axis=-1, keepdims=True)
        )
        ctx_exp = jnp.exp(ctx_scores - row_max)
        tree_exp = jnp.exp(tree_scores - row_max)
        total = jnp.sum(ctx_exp, axis=-1, keepdims=True) + jnp.sum(tree_exp, axis=-1, keepdims=True)
        share = 1.0 / total
        values = cache[0, :, :, HD:].reshape(MAXPAGES * PAGE, HD)
        mixed = jnp.dot((ctx_exp * share).astype(BF), values, preferred_element_type=F32)
        mixed += jnp.dot((tree_exp * share).astype(BF), tree_kv[:, HD:], preferred_element_type=F32)
        parts = [jnp.where(live, mixed[h * NODES : (h + 1) * NODES, :], 0.0).astype(BF) for h in range(GROUP)]
        out[:, columns] = jnp.concatenate(parts, axis=1)
        return carry

    lax.fori_loop(0, queries.shape[1] // (GROUP * HD), group, 0)


def remote(src, dst, send_sem, recv_sem, device):
    return pltpu.make_async_remote_copy(
        src_ref=src,
        dst_ref=dst,
        send_sem=send_sem,
        recv_sem=recv_sem,
        device_id=device,
        device_id_type=MESH,
    )


def multiply(rows, weights, result, tile, done):
    width = weights.shape[1]

    def columns(at, size):
        product = jnp.dot(rows(), weights[:, pl.ds(at, size)], preferred_element_type=F32)
        result[:, :, pl.ds(at, size)] = product.astype(BF).reshape(8, BLOCK, size)

    for j, start in enumerate(range(0, width, tile)):
        size = min(tile, width - start)
        whole = size // INNER

        def step(n, carry, start=start):
            columns(pl.multiple_of(start + n * INNER, LANES), INNER)
            return carry

        if whole:
            lax.fori_loop(0, whole, step, 0)
        if size % INNER:
            columns(start + whole * INNER, size % INNER)
        done(j)


def strips(width, size, work):
    def step(n, carry):
        work(pl.ds(pl.multiple_of(n * size, LANES), size))
        return carry

    lax.fori_loop(0, width // size, step, 0)
    if width % size:
        work(pl.ds(width - width % size, width % size))


def accumulate(target, source):
    def work(columns):
        target[:, columns] = (target[:, columns].astype(F32) + source[:, columns].astype(F32)).astype(BF)

    strips(target.shape[1], STRIP, work)


class Place:
    def __init__(self, r, p, prev, follow, pair, sib, core, index):
        self.r, self.p = r, p
        self.prev, self.follow, self.pair, self.sib = prev, follow, pair, sib
        self.core = core
        self.index = index

    def block(self, p, shift):
        return self.index(p, lax.rem(self.r + (4 + shift), 4))


class Scatter:
    def __init__(self, place, part, buffers, send, recv, cuts):
        self.at, self.part = place, part
        self.far, self.near, self.last = buffers
        self.send, self.recv = send, recv
        self.cuts = cuts
        self.open = {}

    def push(self, slot, src, dst, sem, device):
        copy = remote(src, dst, self.send.at[slot, sem], self.recv.at[slot, sem], device)
        copy.start()
        return copy

    def hand(self, k, src, dst, sem, device):
        self.open.setdefault(k, []).append(self.push(k * len(self.cuts), src, dst, sem, device))

    def arrived(self, k, ref, sem, pieces=False):
        for j, columns in enumerate(self.cuts if pieces else [None]):
            slot = k * len(self.cuts) + j
            piece = ref.at[:, columns] if pieces else ref
            remote(piece, piece, self.send.at[slot, sem], self.recv.at[slot, sem], self.at.pair).wait_recv()

    def first_sends(self, k):
        at, part = self.at, self.part(k)
        return [
            (part.at[at.block(0, 2)], self.far.at[k, 0], 0, at.follow),
            (part.at[at.block(1, 2)], self.far.at[k, 1], 1, at.prev),
            (part.at[at.block(1, 1)], self.near.at[k, 0, 1], 3, at.follow),
            (part.at[at.block(0, -1)], self.near.at[k, 1, 0], 4, at.prev),
        ]

    def step1(self, k, j):
        columns = self.cuts[j]
        for src, dst, sem, device in self.first_sends(k):
            copy = self.push(k * len(self.cuts) + j, src.at[:, columns], dst.at[:, columns], sem, device)
            self.open.setdefault(k, []).append(copy)

    def step2(self, k):
        at, part = self.at, self.part(k)
        for way, (p, shift, device, sem) in enumerate(((0, 1, at.follow, 2), (1, -1, at.prev, 5))):
            self.arrived(k, self.far.at[k, way], way, True)
            mine = at.block(p, shift)
            accumulate(part.at[mine], self.far.at[k, way])
            self.hand(k, part.at[mine], self.near.at[k, way, p], sem, device)

    def ring_sum(self, k, p, columns):
        return (
            self.part(k)[self.at.block(p, 0), :, columns].astype(F32)
            + self.near[k, 0, p, :, columns].astype(F32)
            + self.near[k, 1, p, :, columns].astype(F32)
        )

    def pair_sum(self, k, p):
        ours = self.part(k).at[self.at.block(p, 0)]

        def work(columns):
            ours[:, columns] = self.ring_sum(k, p, columns).astype(BF)

        strips(ours.shape[1], STRIP, work)

    def total(self, k, columns):
        return self.ring_sum(k, self.at.p, columns) + self.last[k, :, columns].astype(F32)

    def step3(self, k):
        at, part = self.at, self.part(k)
        self.arrived(k, self.near.at[k, 0, 0], 2)
        self.arrived(k, self.near.at[k, 0, 1], 3, True)
        self.arrived(k, self.near.at[k, 1, 0], 4, True)
        self.arrived(k, self.near.at[k, 1, 1], 5)
        other = 1 - at.p
        theirs = at.block(other, 0)
        self.pair_sum(k, other)
        self.hand(k, part.at[theirs], self.last.at[k], 6, at.pair)

    def settle(self, k):
        self.arrived(k, self.last.at[k], 6)

    def close(self, k):
        for copy in self.open.pop(k, []):
            copy.wait_send()


class PairScatter(Scatter):
    def __init__(self, place, part, buffers, send, recv, cuts):
        super().__init__(place, part, buffers[1:], send, recv, cuts)
        self.first = buffers[0]

    def first_sends(self, k):
        at, part = self.at, self.part(k)
        p, other = at.p, 1 - at.p
        return [
            (part.at[at.block(other, 2)], self.first.at[k], 0, at.pair),
            (part.at[at.block(other, 1)], self.near.at[k, 0, other], 3, at.follow),
            (part.at[at.block(other, -1)], self.near.at[k, 1, other], 4, at.prev),
            (part.at[at.block(p, 1), BACK], self.near.at[k, 0, p, BACK], 6, at.follow),
            (part.at[at.block(p, -1), FRONT], self.near.at[k, 1, p, FRONT], 8, at.prev),
        ]

    def step2(self, k):
        at, part = self.at, self.part(k)
        self.arrived(k, self.first.at[k], 0, True)
        mine = at.block(at.p, 2)
        accumulate(part.at[mine], self.first.at[k])
        self.hand(k, part.at[mine, FRONT], self.far.at[k, 0], 1, at.follow)
        self.hand(k, part.at[mine, BACK], self.far.at[k, 1], 2, at.prev)

    def step3(self, k):
        at, part = self.at, self.part(k)
        other = 1 - at.p
        self.arrived(k, self.near.at[k, 0, other], 3, True)
        self.arrived(k, self.near.at[k, 1, other], 4, True)
        theirs = at.block(other, 0)
        self.pair_sum(k, other)
        self.hand(k, part.at[theirs], self.last.at[k], 9, at.pair)

    def step4(self, k):
        at, part = self.at, self.part(k)
        for way, (shift, rows, sem, device) in enumerate(((1, FRONT, 5, at.follow), (-1, BACK, 7, at.prev))):
            self.arrived(k, self.far.at[k, way], 1 + way)
            mine = at.block(at.p, shift)
            accumulate(part.at[mine, rows], self.far.at[k, way])
            self.hand(k, part.at[mine, rows], self.near.at[k, way, at.p, rows], sem, device)

    def settle(self, k):
        p = self.at.p
        for way, (added, alone) in enumerate(((FRONT, BACK), (BACK, FRONT))):
            self.arrived(k, self.near.at[k, way, p, added], 5 + 2 * way)
            self.arrived(k, self.near.at[k, way, p, alone], 6 + 2 * way, True)
        self.arrived(k, self.last.at[k], 9)


class Gather:
    def __init__(self, place, ref, send, recv):
        self.at, self.ref = place, ref
        self.send, self.recv = send, recv
        self.open = {}

    def push(self, k, block, sem, device):
        ref = self.ref(k, self.at.core, block)
        copy = remote(ref, ref, self.send.at[k, sem], self.recv.at[k, sem], device)
        copy.start()
        self.open.setdefault(k, []).append(copy)

    def arrived(self, k, block, sem, core):
        ref = self.ref(k, core, block)
        remote(ref, ref, self.send.at[k, sem], self.recv.at[k, sem], self.at.pair).wait_recv()

    def both(self, shift):
        return pl.ds(self.at.block(0, shift), 2)

    def share(self, k, shift):
        self.push(k, self.both(shift), 7 + shift % 4, self.at.sib)

    def step1(self, k):
        at = self.at
        mine = at.block(at.p, 0)
        self.push(k, mine, 0, at.pair)
        self.push(k, mine, 1 + at.p, at.follow)
        self.push(k, mine, 3 + at.p, at.prev)

    def step2(self, k):
        at = self.at
        other = 1 - at.p
        block = at.block(other, 0)
        self.arrived(k, block, 0, at.core)
        self.push(k, block, 1 + other, at.follow)
        self.push(k, block, 3 + other, at.prev)
        self.share(k, 0)

    def step3(self, k):
        at = self.at
        left, right = at.block(0, -1), at.block(1, 1)
        self.arrived(k, left, 1, at.core)
        self.push(k, left, 5, at.follow)
        self.arrived(k, right, 4, at.core)
        self.push(k, right, 6, at.prev)
        self.arrived(k, at.block(1, -1), 2, at.core)
        self.share(k, -1)
        self.arrived(k, at.block(0, 1), 3, at.core)
        self.share(k, 1)

    def step4(self, k):
        at = self.at
        self.arrived(k, at.block(0, 2), 5, at.core)
        self.arrived(k, at.block(1, 2), 6, at.core)
        self.share(k, 2)

    def step5(self, k):
        for shift in (0, 1, -1, 2):
            self.arrived(k, self.both(shift), 7 + shift % 4, 1 - self.at.core)

    def close(self, k):
        for copy in self.open.pop(k, []):
            copy.wait_send()


class PairGather(Gather):
    def hand(self, k, ref, sem, device):
        copy = remote(ref, ref, self.send.at[k, sem], self.recv.at[k, sem], device)
        copy.start()
        self.open.setdefault(k, []).append(copy)

    def landed(self, k, ref, sem):
        remote(ref, ref, self.send.at[k, sem], self.recv.at[k, sem], self.at.pair).wait_recv()

    def step1(self, k):
        at = self.at
        mine = at.block(at.p, 0)
        self.push(k, mine, 0, at.pair)
        self.push(k, mine, 1, at.follow)
        self.push(k, mine, 2, at.prev)

    def step2(self, k):
        at = self.at
        block = at.block(1 - at.p, 0)
        self.arrived(k, block, 0, at.core)
        self.push(k, block, 3, at.follow)
        self.push(k, block, 4, at.prev)
        self.share(k, 0)

    def step3(self, k):
        at = self.at
        left, right = at.block(at.p, -1), at.block(at.p, 1)
        self.arrived(k, left, 1, at.core)
        self.hand(k, self.ref(k, at.core, left).at[FRONT], 5, at.follow)
        self.arrived(k, right, 2, at.core)
        self.hand(k, self.ref(k, at.core, right).at[BACK], 6, at.prev)

    def step4(self, k):
        at = self.at
        self.arrived(k, at.block(1 - at.p, -1), 3, at.core)
        self.share(k, -1)
        self.arrived(k, at.block(1 - at.p, 1), 4, at.core)
        self.share(k, 1)

    def far1(self, k):
        at = self.at
        block = at.block(at.p, 2)
        self.landed(k, self.ref(k, at.core, block).at[FRONT], 5)
        self.landed(k, self.ref(k, at.core, block).at[BACK], 6)
        self.push(k, block, 11, at.pair)

    def far2(self, k):
        at = self.at
        self.arrived(k, at.block(1 - at.p, 2), 11, at.core)
        self.share(k, 2)


def layer_kernel(
    page_table,
    cache_len,
    tree_size,
    parents,
    queries,
    tree_kv,
    cache,
    resid,
    gain,
    w_out,
    w_gate,
    w_up,
    w_down,
    out,
    wo,
    wgu,
    wd,
    attn_all,
    proj,
    hid,
    normed_all,
    sums,
    hidden_all,
    visible,
    far_a,
    near_a,
    last_a,
    first_b,
    far_b,
    near_b,
    last_b,
    far_c,
    near_c,
    last_c,
    load_sem,
    swap_send,
    swap_recv,
    ga_send,
    ga_recv,
    gb_send,
    gb_recv,
    gc_send,
    gc_recv,
    sa_send,
    sa_recv,
    sb_send,
    sb_recv,
    sc_send,
    sc_recv,
):
    gx, gy = lax.axis_index("gx"), lax.axis_index("gy")
    yh, x = lax.div(gx, 4), lax.rem(gx, 4)
    z, yl, core = lax.div(gy, 4), lax.rem(lax.div(gy, 2), 2), lax.rem(gy, 2)
    width = wo.shape[1]
    half = wgu.shape[1] // 2
    depth = w_gate.shape[0]

    sib = (gx, z * 4 + yl * 2 + (1 - core))
    along_x = Place(
        x,
        yh,
        (yh * 4 + lax.rem(x + 3, 4), gy),
        (yh * 4 + lax.rem(x + 1, 4), gy),
        ((1 - yh) * 4 + x, gy),
        sib,
        core,
        lambda p, r: r * 2 + p,
    )
    along_z = Place(
        z,
        yl,
        (gx, lax.rem(z + 3, 4) * 4 + yl * 2 + core),
        (gx, lax.rem(z + 1, 4) * 4 + yl * 2 + core),
        (gx, z * 4 + (1 - yl) * 2 + core),
        sib,
        core,
        lambda p, r: r * 2 + p,
    )

    loads = []

    def load(src, dst):
        copy = pltpu.make_async_copy(src, dst, load_sem.at[len(loads)])
        copy.start()
        loads.append(copy)

    load(w_out, wo)
    mine, theirs = pl.multiple_of(core * half, LANES), pl.multiple_of((1 - core) * half, LANES)
    deep = pl.ds(pl.multiple_of(core * depth, depth), depth)
    load(w_gate.at[:, pl.ds(mine, half)], wgu.at[deep, pl.ds(0, half)])
    load(w_up.at[:, pl.ds(mine, half)], wgu.at[deep, pl.ds(half, half)])
    load(w_down, wd)

    barrier = pltpu.get_barrier_semaphore()
    for device in (along_x.prev, along_x.follow, along_x.pair, along_z.prev, along_z.follow, along_z.pair, sib):
        pl.semaphore_signal(barrier, inc=1, device_id=device, device_id_type=MESH)
    visible[...] = visible_nodes(parents[...], tree_size[0])
    pl.semaphore_wait(barrier, 7)

    side = width // 1
    halves = [pl.ds(at, side) for at in range(0, width, side)]
    quarters = [pl.ds(at, min(TILE, sums.shape[-1] - at)) for at in range(0, sums.shape[-1], TILE)]
    assert len(quarters) == PIECES
    gather_a = Gather(along_z, lambda k, c, b: attn_all.at[k, b, c], ga_send, ga_recv)
    gather_b = Gather(along_x, lambda k, c, b: normed_all.at[k, c, b], gb_send, gb_recv)
    gather_c = PairGather(along_z, lambda k, c, b: hidden_all.at[k, c, b], gc_send, gc_recv)
    scatter_a = Scatter(along_x, lambda k: proj.at[k], (far_a, near_a, last_a), sa_send, sa_recv, halves)
    scatter_b = PairScatter(along_z, lambda k: sums.at[k % 2], (first_b, far_b, near_b, last_b), sb_send, sb_recv, quarters)
    scatter_c = Scatter(along_x, lambda k: proj.at[k], (far_c, near_c, last_c), sc_send, sc_recv, halves)

    swaps = [
        remote(
            w.at[:, pl.ds(theirs, half)],
            wgu.at[deep, pl.ds(n * half, half)],
            swap_send.at[n],
            swap_recv.at[n],
            sib,
        )
        for n, w in enumerate((w_gate, w_up))
    ]
    for copy in swaps:
        copy.start()

    def start(k):
        nodes = slice(k * NODES, (k + 1) * NODES)
        node = lax.broadcasted_iota(jnp.int32, (NODES, 1), 0) + k * NODES
        attend(
            queries,
            nodes,
            visible[nodes, :],
            node < tree_size[0],
            cache_len[0],
            tree_kv,
            cache,
            page_table,
            attn_all.at[k, along_z.block(yl, 0), core],
        )
        gather_a.step1(k)

    def project(k):
        gather_a.step5(k)
        if k == 0:
            loads[0].wait()

        multiply(
            lambda: jnp.concatenate(
                [attn_all[k, q].reshape(BLOCK, attn_all.shape[-1]) for q in (0, 4, 1, 5, 2, 6, 3, 7)], axis=0
            ),
            wo,
            proj.at[k],
            side,
            lambda j: scatter_a.step1(k, j),
        )

    def norm(k):
        scatter_a.settle(k)
        mine = along_x.block(yh, 0)
        squares = jnp.zeros((BLOCK, 1), F32)
        for at in range(0, width, 512):
            columns = pl.ds(at, 512)
            rows = jnp.concatenate(
                [resid[r * MAXTREE + k * NODES : r * MAXTREE + (k + 1) * NODES, columns] for r in (0, 1)], axis=0
            )
            value = (rows.astype(F32) + scatter_a.total(k, columns)).astype(BF)
            hid[k, :, columns] = value
            wide = value.astype(F32)
            scaled = wide * gain[at : at + 512].astype(F32).reshape(1, 512)
            normed_all[k, core, mine, :, columns] = scaled.astype(BF)
            squares += jnp.sum(wide * wide, axis=1, keepdims=True)
        normed_all[k, core, mine, :, width:] = jnp.broadcast_to(squares, (BLOCK, LANES)).astype(BF)
        gather_b.step1(k)

    def gate_up(k):
        gather_b.step5(k)
        if k == 0:
            loads[1].wait()
            loads[2].wait()
            for copy in swaps:
                copy.wait()
        if k >= 2:
            scatter_b.close(k - 2)
        part = sums.at[k % 2]
        squares = normed_all[k, 0, :, :, width:].astype(F32) + normed_all[k, 1, :, :, width:].astype(F32)
        part[:, :, 2 * half :] = squares.astype(BF)

        multiply(
            lambda: jnp.concatenate(
                [normed_all[k, c, :, :, 0:width].reshape(ROWS, width) for c in (0, 1)], axis=1
            ),
            wgu,
            part,
            TILE,
            lambda j: scatter_b.step1(k, j),
        )

    def activate(k):
        scatter_b.settle(k)
        squares = scatter_b.total(k, pl.ds(2 * half, LANES))[:, 0:1]
        scale = lax.rsqrt(squares / D + EPSILON)
        mine = along_z.block(yl, 0)

        def work(columns):
            gate = scatter_b.total(k, columns) * scale
            up = scatter_b.total(k, pl.ds(half + columns.start, columns.size)) * scale
            hidden_all[k, core, mine, :, columns] = (gate / (1.0 + jnp.exp(-gate)) * up).astype(BF)

        strips(half, 256, work)
        gather_c.step1(k)

    def down(k):
        gather_c.step5(k)
        if k == 0:
            loads[3].wait()
        scatter_a.close(k)

        multiply(
            lambda: jnp.concatenate([hidden_all[k, c].reshape(ROWS, half) for c in (0, 1)], axis=1),
            wd,
            proj.at[k],
            side,
            lambda j: scatter_c.step1(k, j),
        )

    def finish(k):
        scatter_c.settle(k)
        for at in range(0, width, 512):
            columns = pl.ds(at, 512)
            total = (hid[k, :, columns].astype(F32) + scatter_c.total(k, columns)).astype(BF)
            for r in (0, 1):
                rows = slice(r * MAXTREE + k * NODES, r * MAXTREE + (k + 1) * NODES)
                out[rows, columns] = total[r * NODES : (r + 1) * NODES, :]

    stages = [
        start,
        gather_a.step2,
        gather_a.step3,
        gather_a.step4,
        project,
        scatter_a.step2,
        scatter_a.step3,
        norm,
        gather_b.step2,
        gather_b.step3,
        gather_b.step4,
        gate_up,
        scatter_b.step2,
        scatter_b.step3,
        scatter_b.step4,
        activate,
        gather_c.step2,
        gather_c.step3,
        gather_c.step4,
        gather_c.far1,
        gather_c.far2,
        down,
        scatter_c.step2,
        scatter_c.step3,
        finish,
    ]
    ahead = [iter(stages) for k in range(CHUNKS)]
    for k in TURNS:
        next(ahead[k])(k)
    for group in (gather_a, gather_b, gather_c, scatter_a, scatter_b, scatter_c):
        for k in range(CHUNKS):
            group.close(k)


TURNS = (
    0, 1, 0, 2, 1, 0, 2, 0, 1, 0, 1, 2, 0, 2, 1, 0, 3, 1, 0, 2, 1, 0, 3, 2,
    0, 1, 3, 0, 2, 3, 1, 0, 1, 2, 0, 3, 1, 0, 0, 3, 1, 2, 0, 2, 3, 1, 0, 1,
    2, 1, 3, 2, 3, 1, 3, 2, 0, 2, 0, 1, 1, 3, 3, 0, 1, 2, 1, 3, 3, 2, 3, 2,
    0, 2, 3, 1, 0, 2, 3, 2, 1, 3, 2, 0, 3, 3, 2, 3, 0, 1, 2, 3, 1, 2, 3, 3,
    1, 2, 0, 3,
)


def layer(page_table, cache_len, tree_size, parents, queries, tree_kv, cache, resid, gain, w_out, w_gate, w_up, w_down):
    heads, width = w_out.shape
    depth, units = w_gate.shape
    half = units // 2
    sums = 2 * half + LANES
    vmem = pl.BlockSpec(memory_space=pltpu.VMEM)
    smem = pl.BlockSpec(memory_space=pltpu.SMEM)
    hbm = pl.BlockSpec(memory_space=pl.ANY)
    sem = pltpu.SemaphoreType.DMA

    def scatter_buffers(lanes, pair):
        first = [pltpu.VMEM((CHUNKS, BLOCK, lanes), BF)] if pair else []
        return [
            *first,
            pltpu.VMEM((CHUNKS, 2, BLOCK // 2 if pair else BLOCK, lanes), BF),
            pltpu.VMEM((CHUNKS, 2, 2, BLOCK, lanes), BF),
            pltpu.VMEM((CHUNKS, BLOCK, lanes), BF),
        ]

    scratch = [
        pltpu.VMEM((heads, width), BF),
        pltpu.VMEM((2 * depth, units), BF),
        pltpu.VMEM((units, width), BF),
        pltpu.VMEM((CHUNKS, 8, 2, NODES, heads), BF),
        pltpu.VMEM((CHUNKS, 8, BLOCK, width), BF),
        pltpu.VMEM((CHUNKS, BLOCK, width), BF),
        pltpu.VMEM((CHUNKS, 2, 8, BLOCK, width + LANES), BF),
        pltpu.VMEM((2, 8, BLOCK, sums), BF),
        pltpu.VMEM((CHUNKS, 2, 8, BLOCK, half), BF),
        pltpu.VMEM((MAXTREE, MAXTREE), F32),
        *scatter_buffers(width, False),
        *scatter_buffers(sums, True),
        *scatter_buffers(width, False),
        sem((4,)),
        sem((2,)),
        sem((2,)),
        *[sem((CHUNKS, 12))] * 6,
        *[sem((CHUNKS * PIECES, 10))] * 6,
    ]
    return pl.pallas_call(
        layer_kernel,
        out_shape=jax.ShapeDtypeStruct(resid.shape, BF),
        in_specs=[smem, smem, smem, vmem, vmem, vmem, vmem, vmem, vmem, hbm, hbm, hbm, hbm],
        out_specs=vmem,
        scratch_shapes=scratch,
        compiler_params=pltpu.CompilerParams(
            collective_id=0, has_side_effects=True, vmem_limit_bytes=62 * 1024 * 1024
        ),
        cost_estimate=pl.CostEstimate(
            flops=2 * 1024 * (heads * width + 3 * depth * units), bytes_accessed=26 * 1024 * 1024, transcendentals=0
        ),
    )(
        page_table,
        cache_len,
        tree_size,
        parents,
        queries,
        tree_kv,
        cache,
        resid,
        gain,
        w_out,
        w_gate,
        w_up,
        w_down,
    )


def body(
    resid,
    queries,
    tree_kv,
    cache,
    page_table,
    cache_len,
    tree_size,
    parents,
    w_out,
    gain,
    w_gate,
    w_up,
    w_down,
):
    return layer(
        page_table,
        cache_len,
        tree_size,
        parents,
        queries,
        tree_kv,
        cache,
        resid,
        gain,
        w_out,
        w_gate,
        w_up,
        w_down,
    )


def solution(mesh):
    in_specs = (
        P("gx", "gy"),
        P("gy", "gx"),
        P("gy", "gx"),
        P("gx", "gy", None, None),
        P("gy", None),
        P("gy"),
        P("gy"),
        P("gy", None),
        P("gx", "gy"),
        P("gy"),
        P("gy", "gx"),
        P("gy", "gx"),
        P("gx", "gy"),
    )
    out_specs = P("gx", "gy")
    return jax.shard_map(body, mesh=mesh, in_specs=in_specs, out_specs=out_specs, check_vma=False)
```

```python
import jax
import jax.numpy as jnp
from jax import lax
from jax.experimental import pallas as pl
from jax.experimental.pallas import tpu as pltpu
from jax.sharding import PartitionSpec as P

D = 16384
HD = 128
MAXTREE = 64
PAGE = 128
MAXPAGES = 8
EPSILON = 1e-05

MESH = pl.DeviceIdType.MESH
BF = jnp.bfloat16
F32 = jnp.float32

CHUNKS = 4
NODES = MAXTREE // CHUNKS
BLOCK = 2 * NODES
ROWS = 8 * BLOCK
LANES = 128
FRONT, BACK = pl.ds(0, BLOCK // 2), pl.ds(BLOCK // 2, BLOCK // 2)
TILE = 1024
PIECES = 4


def visible_nodes(parents, tree_len):
    shape = (MAXTREE, MAXTREE)
    column, row = lax.broadcasted_iota(jnp.int32, shape, 1), lax.broadcasted_iota(jnp.int32, shape, 0)
    eye = jnp.where(row == column, 1.0, 0.0)
    reach = eye + jnp.where(parents == row, 1.0, 0.0)
    for sweep in range((MAXTREE - 1).bit_length()):
        held = reach.astype(BF)
        reach = jnp.minimum(jnp.dot(held, held, preferred_element_type=F32), 1.0)
    turned = lax.dot_general(
        reach.astype(BF), eye.astype(BF), (((0,), (0,)), ((), ())), preferred_element_type=F32
    )
    return jnp.where(column < tree_len, turned, 0.0)


def attend(query, visible, live, cached, tree_kv, cache, page_table):
    heads = query.shape[1] // HD
    keys = jnp.concatenate([query[:, h * HD : (h + 1) * HD] for h in range(heads)], axis=0)
    contract = (((1,), (1,)), ((), ()))
    context = cache[0].reshape(MAXPAGES * PAGE, 2 * HD)
    scale = HD ** (-0.5)
    ctx_scores = lax.dot_general(keys, context[:, 0:HD], contract, preferred_element_type=F32) * scale
    tree_scores = lax.dot_general(keys, tree_kv[:, 0:HD], contract, preferred_element_type=F32) * scale
    offset = lax.broadcasted_iota(jnp.int32, (1, PAGE), 1)
    bounds = []
    for page in range(MAXPAGES):
        place = jnp.int32(0)
        for p in range(1, MAXPAGES):
            place = jnp.where(page_table[0, p] == page, p, place)
        bounds.append(offset < cached - place * PAGE)
    allowed = jnp.concatenate([jnp.where(bound, 1.0, 0.0) for bound in bounds], axis=1)
    ctx_scores = jnp.where(allowed > 0.5, ctx_scores, -1e30)
    seen = jnp.concatenate([visible] * heads, axis=0)
    tree_scores = jnp.where(seen > 0.5, tree_scores, -1e30)
    row_max = jnp.maximum(
        jnp.max(ctx_scores, axis=-1, keepdims=True), jnp.max(tree_scores, axis=-1, keepdims=True)
    )
    ctx_exp = jnp.exp(ctx_scores - row_max)
    tree_exp = jnp.exp(tree_scores - row_max)
    total = jnp.sum(ctx_exp, axis=-1, keepdims=True) + jnp.sum(tree_exp, axis=-1, keepdims=True)
    share = 1.0 / total
    mixed = jnp.dot((ctx_exp * share).astype(BF), context[:, HD:], preferred_element_type=F32)
    mixed += jnp.dot((tree_exp * share).astype(BF), tree_kv[:, HD:], preferred_element_type=F32)
    count = query.shape[0]
    parts = [jnp.where(live, mixed[h * count : (h + 1) * count, :], 0.0).astype(BF) for h in range(heads)]
    return jnp.concatenate(parts, axis=1)


def remote(src, dst, send_sem, recv_sem, device):
    return pltpu.make_async_remote_copy(
        src_ref=src,
        dst_ref=dst,
        send_sem=send_sem,
        recv_sem=recv_sem,
        device_id=device,
        device_id_type=MESH,
    )


def multiply(rows, weights, result, tile, done):
    width = weights.shape[1]
    for j, at in enumerate(range(0, width, tile)):
        size = min(tile, width - at)
        product = jnp.dot(rows(), weights[:, at : at + size], preferred_element_type=F32)
        result[:, :, at : at + size] = product.astype(BF).reshape(8, BLOCK, size)
        done(j)


def other_core(device):
    gx, gy = device
    return gx, gy + 1 - 2 * lax.rem(gy, 2)


class Place:
    def __init__(self, r, p, prev, follow, pair, sib, core, index):
        self.r, self.p = r, p
        self.prev, self.follow, self.pair, self.sib = prev, follow, pair, sib
        self.core = core
        self.index = index

    def block(self, p, shift):
        return self.index(p, lax.rem(self.r + (4 + shift), 4))


class Scatter:
    def __init__(self, place, part, buffers, send, recv, cuts):
        self.at, self.part = place, part
        self.far, self.near, self.last = buffers
        self.send, self.recv = send, recv
        self.cuts = cuts
        self.open = {}

    def push(self, slot, src, dst, sem, device):
        copy = remote(src, dst, self.send.at[slot, sem], self.recv.at[slot, sem], device)
        copy.start()
        return copy

    def hand(self, k, src, dst, sem, device):
        self.open.setdefault(k, []).append(self.push(k * len(self.cuts), src, dst, sem, device))

    def arrived(self, k, ref, sem, pieces=False):
        for j, columns in enumerate(self.cuts if pieces else [None]):
            slot = k * len(self.cuts) + j
            piece = ref.at[:, columns] if pieces else ref
            remote(piece, piece, self.send.at[slot, sem], self.recv.at[slot, sem], self.at.pair).wait_recv()

    def first_sends(self, k):
        at, part = self.at, self.part(k)
        return [
            (part.at[at.block(0, 2)], self.far.at[k, 0], 0, at.follow),
            (part.at[at.block(1, 2)], self.far.at[k, 1], 1, at.prev),
            (part.at[at.block(1, 1)], self.near.at[k, 0, 1], 3, at.follow),
            (part.at[at.block(0, -1)], self.near.at[k, 1, 0], 4, at.prev),
        ]

    def step1(self, k, j):
        columns = self.cuts[j]
        for src, dst, sem, device in self.first_sends(k):
            copy = self.push(k * len(self.cuts) + j, src.at[:, columns], dst.at[:, columns], sem, device)
            self.open.setdefault(k, []).append(copy)

    def step2(self, k):
        at, part = self.at, self.part(k)
        for way, (p, shift, device, sem) in enumerate(((0, 1, at.follow, 2), (1, -1, at.prev, 5))):
            self.arrived(k, self.far.at[k, way], way, True)
            mine = at.block(p, shift)
            part[mine] = (part[mine].astype(F32) + self.far[k, way].astype(F32)).astype(BF)
            self.hand(k, part.at[mine], self.near.at[k, way, p], sem, device)

    def ring_sum(self, k, p):
        return (
            self.part(k)[self.at.block(p, 0)].astype(F32)
            + self.near[k, 0, p].astype(F32)
            + self.near[k, 1, p].astype(F32)
        )

    def step3(self, k):
        at, part = self.at, self.part(k)
        self.arrived(k, self.near.at[k, 0, 0], 2)
        self.arrived(k, self.near.at[k, 0, 1], 3, True)
        self.arrived(k, self.near.at[k, 1, 0], 4, True)
        self.arrived(k, self.near.at[k, 1, 1], 5)
        other = 1 - at.p
        theirs = at.block(other, 0)
        part[theirs] = self.ring_sum(k, other).astype(BF)
        self.hand(k, part.at[theirs], self.last.at[k], 6, at.pair)

    def total(self, k):
        self.arrived(k, self.last.at[k], 6)
        return self.ring_sum(k, self.at.p) + self.last[k].astype(F32)

    def close(self, k):
        for copy in self.open.pop(k, []):
            copy.wait_send()


class PairScatter(Scatter):
    def __init__(self, place, part, buffers, send, recv, cuts):
        super().__init__(place, part, buffers[1:], send, recv, cuts)
        self.first = buffers[0]

    def first_sends(self, k):
        at, part = self.at, self.part(k)
        p, other = at.p, 1 - at.p
        return [
            (part.at[at.block(other, 2)], self.first.at[k], 0, at.pair),
            (part.at[at.block(other, 1)], self.near.at[k, 0, other], 3, at.follow),
            (part.at[at.block(other, -1)], self.near.at[k, 1, other], 4, at.prev),
            (part.at[at.block(p, 1), BACK], self.near.at[k, 0, p, BACK], 6, at.follow),
            (part.at[at.block(p, -1), FRONT], self.near.at[k, 1, p, FRONT], 8, at.prev),
        ]

    def step2(self, k):
        at, part = self.at, self.part(k)
        self.arrived(k, self.first.at[k], 0, True)
        mine = at.block(at.p, 2)
        part[mine] = (part[mine].astype(F32) + self.first[k].astype(F32)).astype(BF)
        self.hand(k, part.at[mine, FRONT], self.far.at[k, 0], 1, at.follow)
        self.hand(k, part.at[mine, BACK], self.far.at[k, 1], 2, at.prev)

    def step3(self, k):
        at, part = self.at, self.part(k)
        other = 1 - at.p
        self.arrived(k, self.near.at[k, 0, other], 3, True)
        self.arrived(k, self.near.at[k, 1, other], 4, True)
        theirs = at.block(other, 0)
        part[theirs] = self.ring_sum(k, other).astype(BF)
        self.hand(k, part.at[theirs], self.last.at[k], 9, at.pair)

    def step4(self, k):
        at, part = self.at, self.part(k)
        for way, (shift, rows, sem, device) in enumerate(((1, FRONT, 5, at.follow), (-1, BACK, 7, at.prev))):
            self.arrived(k, self.far.at[k, way], 1 + way)
            mine = at.block(at.p, shift)
            part[mine, rows] = (part[mine, rows].astype(F32) + self.far[k, way].astype(F32)).astype(BF)
            self.hand(k, part.at[mine, rows], self.near.at[k, way, at.p, rows], sem, device)

    def total(self, k):
        p = self.at.p
        for way, (added, alone) in enumerate(((FRONT, BACK), (BACK, FRONT))):
            self.arrived(k, self.near.at[k, way, p, added], 5 + 2 * way)
            self.arrived(k, self.near.at[k, way, p, alone], 6 + 2 * way, True)
        self.arrived(k, self.last.at[k], 9)
        return self.ring_sum(k, p) + self.last[k].astype(F32)


class Gather:
    def __init__(self, place, ref, send, recv):
        self.at, self.ref = place, ref
        self.send, self.recv = send, recv
        self.open = {}

    def push(self, k, block, sem, device):
        ref = self.ref(k, self.at.core, block)
        copy = remote(ref, ref, self.send.at[k, sem], self.recv.at[k, sem], device)
        copy.start()
        self.open.setdefault(k, []).append(copy)

    def arrived(self, k, block, sem, core):
        ref = self.ref(k, core, block)
        remote(ref, ref, self.send.at[k, sem], self.recv.at[k, sem], self.at.pair).wait_recv()

    def both(self, shift):
        return pl.ds(self.at.block(0, shift), 2)

    def share(self, k, shift):
        self.push(k, self.both(shift), 7 + shift % 4, self.at.sib)

    def step1(self, k):
        at = self.at
        mine = at.block(at.p, 0)
        self.push(k, mine, 0, at.pair)
        self.push(k, mine, 1 + at.p, at.follow)
        self.push(k, mine, 3 + at.p, at.prev)

    def step2(self, k):
        at = self.at
        other = 1 - at.p
        block = at.block(other, 0)
        self.arrived(k, block, 0, at.core)
        self.push(k, block, 1 + other, at.follow)
        self.push(k, block, 3 + other, at.prev)
        self.share(k, 0)

    def step3(self, k):
        at = self.at
        left, right = at.block(0, -1), at.block(1, 1)
        self.arrived(k, left, 1, at.core)
        self.push(k, left, 5, at.follow)
        self.arrived(k, right, 4, at.core)
        self.push(k, right, 6, at.prev)
        self.arrived(k, at.block(1, -1), 2, at.core)
        self.share(k, -1)
        self.arrived(k, at.block(0, 1), 3, at.core)
        self.share(k, 1)

    def step4(self, k):
        at = self.at
        self.arrived(k, at.block(0, 2), 5, at.core)
        self.arrived(k, at.block(1, 2), 6, at.core)
        self.share(k, 2)

    def step5(self, k):
        for shift in (0, 1, -1, 2):
            self.arrived(k, self.both(shift), 7 + shift % 4, 1 - self.at.core)

    def close(self, k):
        for copy in self.open.pop(k, []):
            copy.wait_send()


class FarGather(Gather):
    def step3(self, k):
        at = self.at
        left, right = at.block(0, -1), at.block(1, 1)
        self.arrived(k, left, 1, at.core)
        self.push(k, left, 5, at.follow)
        self.push(k, left, 12, other_core(at.follow))
        self.arrived(k, right, 4, at.core)
        self.push(k, right, 6, at.prev)
        self.push(k, right, 13, other_core(at.prev))
        self.arrived(k, at.block(1, -1), 2, at.core)
        self.share(k, -1)
        self.arrived(k, at.block(0, 1), 3, at.core)
        self.share(k, 1)

    def step5(self, k):
        at = self.at
        for shift in (0, 1, -1):
            self.arrived(k, self.both(shift), 7 + shift % 4, 1 - at.core)
        for core, sems in ((at.core, (5, 6)), (1 - at.core, (12, 13))):
            self.arrived(k, at.block(0, 2), sems[0], core)
            self.arrived(k, at.block(1, 2), sems[1], core)


class PairGather(Gather):
    def hand(self, k, ref, sem, device):
        copy = remote(ref, ref, self.send.at[k, sem], self.recv.at[k, sem], device)
        copy.start()
        self.open.setdefault(k, []).append(copy)

    def landed(self, k, ref, sem):
        remote(ref, ref, self.send.at[k, sem], self.recv.at[k, sem], self.at.pair).wait_recv()

    def step1(self, k):
        at = self.at
        mine = at.block(at.p, 0)
        self.push(k, mine, 0, at.pair)
        self.push(k, mine, 1, at.follow)
        self.push(k, mine, 2, at.prev)

    def step2(self, k):
        at = self.at
        block = at.block(1 - at.p, 0)
        self.arrived(k, block, 0, at.core)
        self.push(k, block, 3, at.follow)
        self.push(k, block, 4, at.prev)
        self.share(k, 0)

    def step3(self, k):
        at = self.at
        left, right = at.block(at.p, -1), at.block(at.p, 1)
        self.arrived(k, left, 1, at.core)
        self.hand(k, self.ref(k, at.core, left).at[FRONT], 5, at.follow)
        self.arrived(k, right, 2, at.core)
        self.hand(k, self.ref(k, at.core, right).at[BACK], 6, at.prev)

    def step4(self, k):
        at = self.at
        self.arrived(k, at.block(1 - at.p, -1), 3, at.core)
        self.share(k, -1)
        self.arrived(k, at.block(1 - at.p, 1), 4, at.core)
        self.share(k, 1)

    def far1(self, k):
        at = self.at
        block = at.block(at.p, 2)
        self.landed(k, self.ref(k, at.core, block).at[FRONT], 5)
        self.landed(k, self.ref(k, at.core, block).at[BACK], 6)
        self.push(k, block, 11, at.pair)

    def far2(self, k):
        at = self.at
        self.arrived(k, at.block(1 - at.p, 2), 11, at.core)
        self.share(k, 2)


def layer_kernel(
    page_table,
    cache_len,
    tree_size,
    parents,
    queries,
    tree_kv,
    cache,
    resid,
    gain,
    w_out,
    w_gate,
    w_up,
    w_down,
    out,
    wo,
    wgu,
    wd,
    attn_all,
    proj,
    hid,
    normed_all,
    sums,
    hidden_all,
    visible,
    first_a,
    far_a,
    near_a,
    last_a,
    first_b,
    far_b,
    near_b,
    last_b,
    first_c,
    far_c,
    near_c,
    last_c,
    load_sem,
    swap_send,
    swap_recv,
    ga_send,
    ga_recv,
    gb_send,
    gb_recv,
    gc_send,
    gc_recv,
    sa_send,
    sa_recv,
    sb_send,
    sb_recv,
    sc_send,
    sc_recv,
):
    gx, gy = lax.axis_index("gx"), lax.axis_index("gy")
    yh, x = lax.div(gx, 4), lax.rem(gx, 4)
    z, yl, core = lax.div(gy, 4), lax.rem(lax.div(gy, 2), 2), lax.rem(gy, 2)
    width = wo.shape[1]
    half = wgu.shape[1] // 2
    depth = w_gate.shape[0]

    sib = (gx, z * 4 + yl * 2 + (1 - core))
    along_x = Place(
        x,
        yh,
        (yh * 4 + lax.rem(x + 3, 4), gy),
        (yh * 4 + lax.rem(x + 1, 4), gy),
        ((1 - yh) * 4 + x, gy),
        sib,
        core,
        lambda p, r: r * 2 + p,
    )
    along_z = Place(
        z,
        yl,
        (gx, lax.rem(z + 3, 4) * 4 + yl * 2 + core),
        (gx, lax.rem(z + 1, 4) * 4 + yl * 2 + core),
        (gx, z * 4 + (1 - yl) * 2 + core),
        sib,
        core,
        lambda p, r: r * 2 + p,
    )

    loads = []

    def load(src, dst):
        copy = pltpu.make_async_copy(src, dst, load_sem.at[len(loads)])
        copy.start()
        loads.append(copy)

    load(w_out, wo)
    mine, theirs = pl.multiple_of(core * half, LANES), pl.multiple_of((1 - core) * half, LANES)
    deep = pl.ds(pl.multiple_of(core * depth, depth), depth)
    load(w_gate.at[:, pl.ds(mine, half)], wgu.at[deep, pl.ds(0, half)])
    load(w_up.at[:, pl.ds(mine, half)], wgu.at[deep, pl.ds(half, half)])
    load(w_down, wd)

    barrier = pltpu.get_barrier_semaphore()
    near = [sib, other_core(along_z.prev), other_core(along_z.follow)]
    for place in (along_x, along_z):
        near += [place.prev, place.follow, place.pair]
    for device in near:
        pl.semaphore_signal(barrier, inc=1, device_id=device, device_id_type=MESH)
    visible[...] = visible_nodes(parents[...], tree_size[0])
    pl.semaphore_wait(barrier, len(near))

    side = width // 1
    halves = [pl.ds(at, side) for at in range(0, width, side)]
    quarters = [pl.ds(at, min(TILE, sums.shape[-1] - at)) for at in range(0, sums.shape[-1], TILE)]
    assert len(quarters) == PIECES
    gather_a = FarGather(along_z, lambda k, c, b: attn_all.at[k, b, c], ga_send, ga_recv)
    gather_b = Gather(along_x, lambda k, c, b: normed_all.at[k, c, b], gb_send, gb_recv)
    gather_c = PairGather(along_z, lambda k, c, b: hidden_all.at[k, c, b], gc_send, gc_recv)
    scatter_a = PairScatter(along_x, lambda k: proj.at[k], (first_a, far_a, near_a, last_a), sa_send, sa_recv, halves)
    scatter_b = PairScatter(along_z, lambda k: sums.at[k % 2], (first_b, far_b, near_b, last_b), sb_send, sb_recv, quarters)
    scatter_c = PairScatter(along_x, lambda k: proj.at[k], (first_c, far_c, near_c, last_c), sc_send, sc_recv, halves)

    swaps = [
        remote(
            w.at[:, pl.ds(theirs, half)],
            wgu.at[deep, pl.ds(n * half, half)],
            swap_send.at[n],
            swap_recv.at[n],
            sib,
        )
        for n, w in enumerate((w_gate, w_up))
    ]
    for copy in swaps:
        copy.start()

    def start(k):
        nodes = slice(k * NODES, (k + 1) * NODES)
        node = lax.broadcasted_iota(jnp.int32, (NODES, 1), 0) + k * NODES
        attn_all[k, along_z.block(yl, 0), core] = attend(
            queries[nodes, :], visible[nodes, :], node < tree_size[0], cache_len[0], tree_kv[...], cache, page_table
        )
        gather_a.step1(k)

    def project(k):
        gather_a.step5(k)
        if k == 0:
            loads[0].wait()

        multiply(
            lambda: jnp.concatenate(
                [attn_all[k, q].reshape(BLOCK, attn_all.shape[-1]) for q in (0, 4, 1, 5, 2, 6, 3, 7)], axis=0
            ),
            wo,
            proj.at[k],
            side,
            lambda j: scatter_a.step1(k, j),
        )

    def norm(k):
        projected = scatter_a.total(k)
        rows = jnp.concatenate([resid[r * MAXTREE + k * NODES : r * MAXTREE + (k + 1) * NODES, :] for r in (0, 1)], axis=0)
        value = (rows.astype(F32) + projected).astype(BF)
        hid[k] = value
        wide = value.astype(F32)
        mine = along_x.block(yh, 0)
        normed_all[k, core, mine, :, 0:width] = (wide * gain[...].astype(F32).reshape(1, width)).astype(BF)
        squares = jnp.sum(wide * wide, axis=1, keepdims=True)
        normed_all[k, core, mine, :, width:] = jnp.broadcast_to(squares, (BLOCK, LANES)).astype(BF)
        gather_b.step1(k)

    def gate_up(k):
        gather_b.step5(k)
        if k == 0:
            loads[1].wait()
            loads[2].wait()
            for copy in swaps:
                copy.wait()
        if k >= 2:
            scatter_b.close(k - 2)
        part = sums.at[k % 2]
        squares = normed_all[k, 0, :, :, width:].astype(F32) + normed_all[k, 1, :, :, width:].astype(F32)
        part[:, :, 2 * half :] = squares.astype(BF)

        multiply(
            lambda: jnp.concatenate(
                [normed_all[k, c, :, :, 0:width].reshape(ROWS, width) for c in (0, 1)], axis=1
            ),
            wgu,
            part,
            TILE,
            lambda j: scatter_b.step1(k, j),
        )

    def activate(k):
        total = scatter_b.total(k)
        scale = lax.rsqrt(total[:, 2 * half : 2 * half + 1] / D + EPSILON)
        gate = total[:, 0:half] * scale
        up = total[:, half : 2 * half] * scale
        hidden_all[k, core, along_z.block(yl, 0)] = (gate / (1.0 + jnp.exp(-gate)) * up).astype(BF)
        gather_c.step1(k)

    def down(k):
        gather_c.step5(k)
        if k == 0:
            loads[3].wait()
        scatter_a.close(k)

        multiply(
            lambda: jnp.concatenate([hidden_all[k, c].reshape(ROWS, half) for c in (0, 1)], axis=1),
            wd,
            proj.at[k],
            side,
            lambda j: scatter_c.step1(k, j),
        )

    def finish(k):
        total = (hid[k].astype(F32) + scatter_c.total(k)).astype(BF)
        for r in (0, 1):
            out[r * MAXTREE + k * NODES : r * MAXTREE + (k + 1) * NODES, :] = total[r * NODES : (r + 1) * NODES, :]

    stages = [
        start,
        gather_a.step2,
        gather_a.step3,
        project,
        scatter_a.step2,
        scatter_a.step3,
        scatter_a.step4,
        norm,
        gather_b.step2,
        gather_b.step3,
        gather_b.step4,
        gate_up,
        scatter_b.step2,
        scatter_b.step3,
        scatter_b.step4,
        activate,
        gather_c.step2,
        gather_c.step3,
        gather_c.step4,
        gather_c.far1,
        gather_c.far2,
        down,
        scatter_c.step2,
        scatter_c.step3,
        scatter_c.step4,
        finish,
    ]
    ahead = [iter(stages) for k in range(CHUNKS)]
    for k in TURNS:
        next(ahead[k])(k)
    for group in (gather_a, gather_b, gather_c, scatter_a, scatter_b, scatter_c):
        for k in range(CHUNKS):
            group.close(k)


TURNS = (
    0, 3, 0, 1, 0, 2, 1, 0, 2, 1, 0, 0, 2, 0, 1, 0, 3, 1, 1, 0, 1, 2, 3, 0,
    1, 2, 0, 2, 1, 0, 2, 3, 1, 2, 0, 0, 3, 1, 3, 2, 0, 1, 2, 3, 0, 2, 3, 1,
    2, 1, 3, 1, 3, 0, 2, 3, 0, 1, 3, 2, 0, 3, 2, 0, 3, 1, 3, 2, 0, 1, 3, 2,
    1, 2, 1, 0, 3, 2, 3, 2, 1, 3, 0, 3, 2, 1, 0, 0, 3, 2, 1, 3, 1, 2, 1, 2,
    3, 2, 3, 3, 1, 2, 0, 3,
)


def layer(page_table, cache_len, tree_size, parents, queries, tree_kv, cache, resid, gain, w_out, w_gate, w_up, w_down):
    heads, width = w_out.shape
    depth, units = w_gate.shape
    half = units // 2
    sums = 2 * half + LANES
    vmem = pl.BlockSpec(memory_space=pltpu.VMEM)
    smem = pl.BlockSpec(memory_space=pltpu.SMEM)
    hbm = pl.BlockSpec(memory_space=pl.ANY)
    sem = pltpu.SemaphoreType.DMA

    def scatter_buffers(lanes, pair):
        first = [pltpu.VMEM((CHUNKS, BLOCK, lanes), BF)] if pair else []
        return [
            *first,
            pltpu.VMEM((CHUNKS, 2, BLOCK // 2 if pair else BLOCK, lanes), BF),
            pltpu.VMEM((CHUNKS, 2, 2, BLOCK, lanes), BF),
            pltpu.VMEM((CHUNKS, BLOCK, lanes), BF),
        ]

    scratch = [
        pltpu.VMEM((heads, width), BF),
        pltpu.VMEM((2 * depth, units), BF),
        pltpu.VMEM((units, width), BF),
        pltpu.VMEM((CHUNKS, 8, 2, NODES, heads), BF),
        pltpu.VMEM((CHUNKS, 8, BLOCK, width), BF),
        pltpu.VMEM((CHUNKS, BLOCK, width), BF),
        pltpu.VMEM((CHUNKS, 2, 8, BLOCK, width + LANES), BF),
        pltpu.VMEM((2, 8, BLOCK, sums), BF),
        pltpu.VMEM((CHUNKS, 2, 8, BLOCK, half), BF),
        pltpu.VMEM((MAXTREE, MAXTREE), F32),
        *scatter_buffers(width, True),
        *scatter_buffers(sums, True),
        *scatter_buffers(width, True),
        sem((4,)),
        sem((2,)),
        sem((2,)),
        *[sem((CHUNKS, 14))] * 6,
        *[sem((CHUNKS * PIECES, 10))] * 6,
    ]
    return pl.pallas_call(
        layer_kernel,
        out_shape=jax.ShapeDtypeStruct(resid.shape, BF),
        in_specs=[smem, smem, smem, vmem, vmem, vmem, vmem, vmem, vmem, hbm, hbm, hbm, hbm],
        out_specs=vmem,
        scratch_shapes=scratch,
        compiler_params=pltpu.CompilerParams(
            collective_id=0, has_side_effects=True, vmem_limit_bytes=62 * 1024 * 1024
        ),
        cost_estimate=pl.CostEstimate(
            flops=2 * 1024 * (heads * width + 3 * depth * units), bytes_accessed=26 * 1024 * 1024, transcendentals=0
        ),
    )(
        page_table,
        cache_len,
        tree_size,
        parents,
        queries,
        tree_kv,
        cache,
        resid,
        gain,
        w_out,
        w_gate,
        w_up,
        w_down,
    )


def body(
    resid,
    queries,
    tree_kv,
    cache,
    page_table,
    cache_len,
    tree_size,
    parents,
    w_out,
    gain,
    w_gate,
    w_up,
    w_down,
):
    return layer(
        page_table,
        cache_len,
        tree_size,
        parents,
        queries,
        tree_kv,
        cache,
        resid,
        gain,
        w_out,
        w_gate,
        w_up,
        w_down,
    )


def solution(mesh):
    in_specs = (
        P("gx", "gy"),
        P("gy", "gx"),
        P("gy", "gx"),
        P("gx", "gy", None, None),
        P("gy", None),
        P("gy"),
        P("gy"),
        P("gy", None),
        P("gx", "gy"),
        P("gy"),
        P("gy", "gx"),
        P("gy", "gx"),
        P("gx", "gy"),
    )
    out_specs = P("gx", "gy")
    return jax.shard_map(body, mesh=mesh, in_specs=in_specs, out_specs=out_specs, check_vma=False)
```

```python
import math

import jax
import jax.numpy as jnp
from jax import lax
from jax.experimental import pallas as pl
from jax.experimental.pallas import tpu as pltpu
from jax.sharding import PartitionSpec as P

D = 16384
HD = 128
MAXTREE = 64
PAGE = 128
MAXPAGES = 8
EPSILON = 1e-05

MESH = pl.DeviceIdType.MESH
BF = jnp.bfloat16
F32 = jnp.float32

CHUNKS = 4
NODES = MAXTREE // CHUNKS
BLOCK = 2 * NODES
ROWS = 8 * BLOCK
LANES = 128
FRONT, BACK = pl.ds(0, BLOCK // 2), pl.ds(BLOCK // 2, BLOCK // 2)
TILE = 1024
PIECES = 4


def visible_nodes(parents, tree_len):
    shape = (MAXTREE, MAXTREE)
    column, row = lax.broadcasted_iota(jnp.int32, shape, 1), lax.broadcasted_iota(jnp.int32, shape, 0)
    eye = jnp.where(row == column, 1.0, 0.0)
    reach = eye + jnp.where(parents == row, 1.0, 0.0)
    for sweep in range((MAXTREE - 1).bit_length()):
        held = reach.astype(BF)
        reach = jnp.minimum(jnp.dot(held, held, preferred_element_type=F32), 1.0)
    turned = lax.dot_general(
        reach.astype(BF), eye.astype(BF), (((0,), (0,)), ((), ())), preferred_element_type=F32
    )
    return jnp.where(column < tree_len, turned, 0.0)


def attend(query, visible, live, cached, tree_kv, cache, page_table):
    heads = query.shape[1] // HD
    keys = jnp.concatenate([query[:, h * HD : (h + 1) * HD] for h in range(heads)], axis=0)
    contract = (((1,), (1,)), ((), ()))
    context = cache[0].reshape(MAXPAGES * PAGE, 2 * HD)
    scale = HD ** (-0.5) * math.log2(math.e)
    ctx_scores = lax.dot_general(keys, context[:, 0:HD], contract, preferred_element_type=F32)
    tree_scores = lax.dot_general(keys, tree_kv[:, 0:HD], contract, preferred_element_type=F32)
    offset = lax.broadcasted_iota(jnp.int32, (1, PAGE), 1)
    bounds = []
    for page in range(MAXPAGES):
        place = jnp.int32(0)
        for p in range(1, MAXPAGES):
            place = jnp.where(page_table[0, p] == page, p, place)
        bounds.append(offset < cached - place * PAGE)
    allowed = jnp.concatenate([jnp.where(bound, 1.0, 0.0) for bound in bounds], axis=1)
    ctx_scores = jnp.where(allowed > 0.5, ctx_scores, -1e30)
    seen = jnp.concatenate([visible] * heads, axis=0)
    tree_scores = jnp.where(seen > 0.5, tree_scores, -1e30)
    row_max = jnp.maximum(
        jnp.max(ctx_scores, axis=-1, keepdims=True), jnp.max(tree_scores, axis=-1, keepdims=True)
    )
    ctx_exp = jnp.exp2((ctx_scores - row_max) * scale)
    tree_exp = jnp.exp2((tree_scores - row_max) * scale)
    total = jnp.sum(ctx_exp, axis=-1, keepdims=True) + jnp.sum(tree_exp, axis=-1, keepdims=True)
    mixed = jnp.dot(ctx_exp.astype(BF), context[:, HD:], preferred_element_type=F32)
    mixed += jnp.dot(tree_exp.astype(BF), tree_kv[:, HD:], preferred_element_type=F32)
    mixed *= 1.0 / total
    count = query.shape[0]
    parts = [jnp.where(live, mixed[h * count : (h + 1) * count, :], 0.0).astype(BF) for h in range(heads)]
    return jnp.concatenate(parts, axis=1)


def remote(src, dst, send_sem, recv_sem, device):
    return pltpu.make_async_remote_copy(
        src_ref=src,
        dst_ref=dst,
        send_sem=send_sem,
        recv_sem=recv_sem,
        device_id=device,
        device_id_type=MESH,
    )


def multiply(rows, weights, result, tile, done):
    width = weights.shape[1]
    for j, at in enumerate(range(0, width, tile)):
        size = min(tile, width - at)
        product = jnp.dot(rows(), weights[:, at : at + size], preferred_element_type=F32)
        result[:, :, at : at + size] = product.astype(BF).reshape(8, BLOCK, size)
        done(j)


def other_core(device):
    gx, gy = device
    return gx, gy + 1 - 2 * lax.rem(gy, 2)


class Place:
    def __init__(self, r, p, prev, follow, pair, sib, core, index):
        self.r, self.p = r, p
        self.prev, self.follow, self.pair, self.sib = prev, follow, pair, sib
        self.core = core
        self.index = index

    def block(self, p, shift):
        return self.index(p, lax.rem(self.r + (4 + shift), 4))


class Scatter:
    def __init__(self, place, part, buffers, send, recv, cuts):
        self.at, self.part = place, part
        self.far, self.near, self.last = buffers
        self.send, self.recv = send, recv
        self.cuts = cuts
        self.open = {}

    def push(self, slot, src, dst, sem, device):
        copy = remote(src, dst, self.send.at[slot, sem], self.recv.at[slot, sem], device)
        copy.start()
        return copy

    def hand(self, k, src, dst, sem, device):
        self.open.setdefault(k, []).append(self.push(k * len(self.cuts), src, dst, sem, device))

    def arrived(self, k, ref, sem, pieces=False):
        for j, columns in enumerate(self.cuts if pieces else [None]):
            slot = k * len(self.cuts) + j
            piece = ref.at[:, columns] if pieces else ref
            remote(piece, piece, self.send.at[slot, sem], self.recv.at[slot, sem], self.at.pair).wait_recv()

    def first_sends(self, k):
        at, part = self.at, self.part(k)
        return [
            (part.at[at.block(0, 2)], self.far.at[k, 0], 0, at.follow),
            (part.at[at.block(1, 2)], self.far.at[k, 1], 1, at.prev),
            (part.at[at.block(1, 1)], self.near.at[k, 0, 1], 3, at.follow),
            (part.at[at.block(0, -1)], self.near.at[k, 1, 0], 4, at.prev),
        ]

    def step1(self, k, j):
        columns = self.cuts[j]
        for src, dst, sem, device in self.first_sends(k):
            copy = self.push(k * len(self.cuts) + j, src.at[:, columns], dst.at[:, columns], sem, device)
            self.open.setdefault(k, []).append(copy)

    def step2(self, k):
        at, part = self.at, self.part(k)
        for way, (p, shift, device, sem) in enumerate(((0, 1, at.follow, 2), (1, -1, at.prev, 5))):
            self.arrived(k, self.far.at[k, way], way, True)
            mine = at.block(p, shift)
            part[mine] = (part[mine].astype(F32) + self.far[k, way].astype(F32)).astype(BF)
            self.hand(k, part.at[mine], self.near.at[k, way, p], sem, device)

    def ring_sum(self, k, p):
        return (
            self.part(k)[self.at.block(p, 0)].astype(F32)
            + self.near[k, 0, p].astype(F32)
            + self.near[k, 1, p].astype(F32)
        )

    def step3(self, k):
        at, part = self.at, self.part(k)
        self.arrived(k, self.near.at[k, 0, 0], 2)
        self.arrived(k, self.near.at[k, 0, 1], 3, True)
        self.arrived(k, self.near.at[k, 1, 0], 4, True)
        self.arrived(k, self.near.at[k, 1, 1], 5)
        other = 1 - at.p
        theirs = at.block(other, 0)
        part[theirs] = self.ring_sum(k, other).astype(BF)
        self.hand(k, part.at[theirs], self.last.at[k], 6, at.pair)

    def total(self, k):
        self.arrived(k, self.last.at[k], 6)
        return self.ring_sum(k, self.at.p) + self.last[k].astype(F32)

    def close(self, k):
        for copy in self.open.pop(k, []):
            copy.wait_send()


class PairScatter(Scatter):
    def __init__(self, place, part, buffers, send, recv, cuts):
        super().__init__(place, part, buffers[1:], send, recv, cuts)
        self.first = buffers[0]

    def first_sends(self, k):
        at, part = self.at, self.part(k)
        p, other = at.p, 1 - at.p
        return [
            (part.at[at.block(other, 2)], self.first.at[k], 0, at.pair),
            (part.at[at.block(other, 1)], self.near.at[k, 0, other], 3, at.follow),
            (part.at[at.block(other, -1)], self.near.at[k, 1, other], 4, at.prev),
            (part.at[at.block(p, 1), BACK], self.near.at[k, 0, p, BACK], 6, at.follow),
            (part.at[at.block(p, -1), FRONT], self.near.at[k, 1, p, FRONT], 8, at.prev),
        ]

    def step2(self, k):
        at, part = self.at, self.part(k)
        self.arrived(k, self.first.at[k], 0, True)
        mine = at.block(at.p, 2)
        part[mine] = (part[mine].astype(F32) + self.first[k].astype(F32)).astype(BF)
        self.hand(k, part.at[mine, FRONT], self.far.at[k, 0], 1, at.follow)
        self.hand(k, part.at[mine, BACK], self.far.at[k, 1], 2, at.prev)

    def step3(self, k):
        at, part = self.at, self.part(k)
        other = 1 - at.p
        self.arrived(k, self.near.at[k, 0, other], 3, True)
        self.arrived(k, self.near.at[k, 1, other], 4, True)
        theirs = at.block(other, 0)
        part[theirs] = self.ring_sum(k, other).astype(BF)
        self.hand(k, part.at[theirs], self.last.at[k], 9, at.pair)

    def step4(self, k):
        at, part = self.at, self.part(k)
        for way, (shift, rows, sem, device) in enumerate(((1, FRONT, 5, at.follow), (-1, BACK, 7, at.prev))):
            self.arrived(k, self.far.at[k, way], 1 + way)
            mine = at.block(at.p, shift)
            part[mine, rows] = (part[mine, rows].astype(F32) + self.far[k, way].astype(F32)).astype(BF)
            self.hand(k, part.at[mine, rows], self.near.at[k, way, at.p, rows], sem, device)

    def total(self, k):
        p = self.at.p
        for way, (added, alone) in enumerate(((FRONT, BACK), (BACK, FRONT))):
            self.arrived(k, self.near.at[k, way, p, added], 5 + 2 * way)
            self.arrived(k, self.near.at[k, way, p, alone], 6 + 2 * way, True)
        self.arrived(k, self.last.at[k], 9)
        return self.ring_sum(k, p) + self.last[k].astype(F32)


class Gather:
    def __init__(self, place, ref, send, recv):
        self.at, self.ref = place, ref
        self.send, self.recv = send, recv
        self.open = {}

    def push(self, k, block, sem, device):
        ref = self.ref(k, self.at.core, block)
        copy = remote(ref, ref, self.send.at[k, sem], self.recv.at[k, sem], device)
        copy.start()
        self.open.setdefault(k, []).append(copy)

    def arrived(self, k, block, sem, core):
        ref = self.ref(k, core, block)
        remote(ref, ref, self.send.at[k, sem], self.recv.at[k, sem], self.at.pair).wait_recv()

    def both(self, shift):
        return pl.ds(self.at.block(0, shift), 2)

    def share(self, k, shift):
        self.push(k, self.both(shift), 7 + shift % 4, self.at.sib)

    def step1(self, k):
        at = self.at
        mine = at.block(at.p, 0)
        self.push(k, mine, 0, at.pair)
        self.push(k, mine, 1 + at.p, at.follow)
        self.push(k, mine, 3 + at.p, at.prev)

    def step2(self, k):
        at = self.at
        other = 1 - at.p
        block = at.block(other, 0)
        self.arrived(k, block, 0, at.core)
        self.push(k, block, 1 + other, at.follow)
        self.push(k, block, 3 + other, at.prev)
        self.share(k, 0)

    def step3(self, k):
        at = self.at
        left, right = at.block(0, -1), at.block(1, 1)
        self.arrived(k, left, 1, at.core)
        self.push(k, left, 5, at.follow)
        self.arrived(k, right, 4, at.core)
        self.push(k, right, 6, at.prev)
        self.arrived(k, at.block(1, -1), 2, at.core)
        self.share(k, -1)
        self.arrived(k, at.block(0, 1), 3, at.core)
        self.share(k, 1)

    def step4(self, k):
        at = self.at
        self.arrived(k, at.block(0, 2), 5, at.core)
        self.arrived(k, at.block(1, 2), 6, at.core)
        self.share(k, 2)

    def step5(self, k):
        for shift in (0, 1, -1, 2):
            self.arrived(k, self.both(shift), 7 + shift % 4, 1 - self.at.core)

    def close(self, k):
        for copy in self.open.pop(k, []):
            copy.wait_send()


class FarGather(Gather):
    def step3(self, k):
        at = self.at
        left, right = at.block(0, -1), at.block(1, 1)
        self.arrived(k, left, 1, at.core)
        self.push(k, left, 5, at.follow)
        self.push(k, left, 12, other_core(at.follow))
        self.arrived(k, right, 4, at.core)
        self.push(k, right, 6, at.prev)
        self.push(k, right, 13, other_core(at.prev))
        self.arrived(k, at.block(1, -1), 2, at.core)
        self.share(k, -1)
        self.arrived(k, at.block(0, 1), 3, at.core)
        self.share(k, 1)

    def step5(self, k):
        at = self.at
        for shift in (0, 1, -1):
            self.arrived(k, self.both(shift), 7 + shift % 4, 1 - at.core)
        for core, sems in ((at.core, (5, 6)), (1 - at.core, (12, 13))):
            self.arrived(k, at.block(0, 2), sems[0], core)
            self.arrived(k, at.block(1, 2), sems[1], core)


class PairGather(Gather):
    def hand(self, k, ref, sem, device):
        copy = remote(ref, ref, self.send.at[k, sem], self.recv.at[k, sem], device)
        copy.start()
        self.open.setdefault(k, []).append(copy)

    def landed(self, k, ref, sem):
        remote(ref, ref, self.send.at[k, sem], self.recv.at[k, sem], self.at.pair).wait_recv()

    def step1(self, k):
        at = self.at
        mine = at.block(at.p, 0)
        self.push(k, mine, 0, at.pair)
        self.push(k, mine, 1, at.follow)
        self.push(k, mine, 2, at.prev)

    def step2(self, k):
        at = self.at
        block = at.block(1 - at.p, 0)
        self.arrived(k, block, 0, at.core)
        self.push(k, block, 3, at.follow)
        self.push(k, block, 4, at.prev)
        self.share(k, 0)

    def step3(self, k):
        at = self.at
        left, right = at.block(at.p, -1), at.block(at.p, 1)
        self.arrived(k, left, 1, at.core)
        self.hand(k, self.ref(k, at.core, left).at[FRONT], 5, at.follow)
        self.arrived(k, right, 2, at.core)
        self.hand(k, self.ref(k, at.core, right).at[BACK], 6, at.prev)

    def step4(self, k):
        at = self.at
        self.arrived(k, at.block(1 - at.p, -1), 3, at.core)
        self.share(k, -1)
        self.arrived(k, at.block(1 - at.p, 1), 4, at.core)
        self.share(k, 1)

    def far1(self, k):
        at = self.at
        block = at.block(at.p, 2)
        self.landed(k, self.ref(k, at.core, block).at[FRONT], 5)
        self.landed(k, self.ref(k, at.core, block).at[BACK], 6)
        self.push(k, block, 11, at.pair)

    def far2(self, k):
        at = self.at
        self.arrived(k, at.block(1 - at.p, 2), 11, at.core)
        self.share(k, 2)


def layer_kernel(
    page_table,
    cache_len,
    tree_size,
    parents,
    queries,
    tree_kv,
    cache,
    resid,
    gain,
    w_out,
    w_gate,
    w_up,
    w_down,
    out,
    wo,
    wgu,
    wd,
    attn_all,
    proj,
    hid,
    normed_all,
    sums,
    hidden_all,
    visible,
    first_a,
    far_a,
    near_a,
    last_a,
    first_b,
    far_b,
    near_b,
    last_b,
    first_c,
    far_c,
    near_c,
    last_c,
    load_sem,
    swap_send,
    swap_recv,
    ga_send,
    ga_recv,
    gb_send,
    gb_recv,
    gc_send,
    gc_recv,
    sa_send,
    sa_recv,
    sb_send,
    sb_recv,
    sc_send,
    sc_recv,
):
    gx, gy = lax.axis_index("gx"), lax.axis_index("gy")
    yh, x = lax.div(gx, 4), lax.rem(gx, 4)
    z, yl, core = lax.div(gy, 4), lax.rem(lax.div(gy, 2), 2), lax.rem(gy, 2)
    width = wo.shape[1]
    half = wgu.shape[1] // 2
    depth = w_gate.shape[0]

    sib = (gx, z * 4 + yl * 2 + (1 - core))
    along_x = Place(
        x,
        yh,
        (yh * 4 + lax.rem(x + 3, 4), gy),
        (yh * 4 + lax.rem(x + 1, 4), gy),
        ((1 - yh) * 4 + x, gy),
        sib,
        core,
        lambda p, r: r * 2 + p,
    )
    along_z = Place(
        z,
        yl,
        (gx, lax.rem(z + 3, 4) * 4 + yl * 2 + core),
        (gx, lax.rem(z + 1, 4) * 4 + yl * 2 + core),
        (gx, z * 4 + (1 - yl) * 2 + core),
        sib,
        core,
        lambda p, r: r * 2 + p,
    )

    loads = []

    def load(src, dst):
        copy = pltpu.make_async_copy(src, dst, load_sem.at[len(loads)])
        copy.start()
        loads.append(copy)

    load(w_out, wo)
    mine, theirs = pl.multiple_of(core * half, LANES), pl.multiple_of((1 - core) * half, LANES)
    deep = pl.ds(pl.multiple_of(core * depth, depth), depth)
    load(w_gate.at[:, pl.ds(mine, half)], wgu.at[deep, pl.ds(0, half)])
    load(w_up.at[:, pl.ds(mine, half)], wgu.at[deep, pl.ds(half, half)])
    load(w_down, wd)

    barrier = pltpu.get_barrier_semaphore()
    near = [sib, other_core(along_z.prev), other_core(along_z.follow)]
    for place in (along_x, along_z):
        near += [place.prev, place.follow, place.pair]
    for device in near:
        pl.semaphore_signal(barrier, inc=1, device_id=device, device_id_type=MESH)
    visible[...] = visible_nodes(parents[...], tree_size[0])

    def attention(k):
        nodes = slice(k * NODES, (k + 1) * NODES)
        node = lax.broadcasted_iota(jnp.int32, (NODES, 1), 0) + k * NODES
        attn_all[k, along_z.block(yl, 0), core] = attend(
            queries[nodes, :], visible[nodes, :], node < tree_size[0], cache_len[0], tree_kv[...], cache, page_table
        )

    attention(0)
    pl.semaphore_wait(barrier, len(near))

    side = width // 1
    halves = [pl.ds(at, side) for at in range(0, width, side)]
    quarters = [pl.ds(at, min(TILE, sums.shape[-1] - at)) for at in range(0, sums.shape[-1], TILE)]
    assert len(quarters) == PIECES
    gather_a = FarGather(along_z, lambda k, c, b: attn_all.at[k, b, c], ga_send, ga_recv)
    gather_b = Gather(along_x, lambda k, c, b: normed_all.at[k, c, b], gb_send, gb_recv)
    gather_c = PairGather(along_z, lambda k, c, b: hidden_all.at[k, c, b], gc_send, gc_recv)
    scatter_a = PairScatter(along_x, lambda k: proj.at[k], (first_a, far_a, near_a, last_a), sa_send, sa_recv, halves)
    scatter_b = PairScatter(along_z, lambda k: sums.at[k % 2], (first_b, far_b, near_b, last_b), sb_send, sb_recv, quarters)
    scatter_c = PairScatter(along_x, lambda k: proj.at[k], (first_c, far_c, near_c, last_c), sc_send, sc_recv, halves)

    swaps = [
        remote(
            w.at[:, pl.ds(theirs, half)],
            wgu.at[deep, pl.ds(n * half, half)],
            swap_send.at[n],
            swap_recv.at[n],
            sib,
        )
        for n, w in enumerate((w_gate, w_up))
    ]
    for copy in swaps:
        copy.start()

    def start(k):
        if k > 0:
            attention(k)
        gather_a.step1(k)

    def project(k):
        gather_a.step5(k)
        if k == 0:
            loads[0].wait()

        multiply(
            lambda: jnp.concatenate(
                [attn_all[k, q].reshape(BLOCK, attn_all.shape[-1]) for q in (0, 4, 1, 5, 2, 6, 3, 7)], axis=0
            ),
            wo,
            proj.at[k],
            side,
            lambda j: scatter_a.step1(k, j),
        )

    def norm(k):
        projected = scatter_a.total(k)
        rows = jnp.concatenate([resid[r * MAXTREE + k * NODES : r * MAXTREE + (k + 1) * NODES, :] for r in (0, 1)], axis=0)
        value = (rows.astype(F32) + projected).astype(BF)
        hid[k] = value
        wide = value.astype(F32)
        mine = along_x.block(yh, 0)
        normed_all[k, core, mine, :, 0:width] = (wide * gain[...].astype(F32).reshape(1, width)).astype(BF)
        squares = jnp.sum(wide * wide, axis=1, keepdims=True)
        normed_all[k, core, mine, :, width:] = jnp.broadcast_to(squares, (BLOCK, LANES)).astype(BF)
        gather_b.step1(k)

    def gate_up(k):
        gather_b.step5(k)
        if k == 0:
            loads[1].wait()
            loads[2].wait()
            for copy in swaps:
                copy.wait()
        if k >= 2:
            scatter_b.close(k - 2)
        part = sums.at[k % 2]
        squares = normed_all[k, 0, :, :, width:].astype(F32) + normed_all[k, 1, :, :, width:].astype(F32)
        part[:, :, 2 * half :] = squares.astype(BF)

        multiply(
            lambda: jnp.concatenate(
                [normed_all[k, c, :, :, 0:width].reshape(ROWS, width) for c in (0, 1)], axis=1
            ),
            wgu,
            part,
            TILE,
            lambda j: scatter_b.step1(k, j),
        )

    def activate(k):
        total = scatter_b.total(k)
        scale = lax.rsqrt(total[:, 2 * half : 2 * half + 1] / D + EPSILON)
        gate = total[:, 0:half] * scale
        up = total[:, half : 2 * half] * scale
        hidden_all[k, core, along_z.block(yl, 0)] = (gate / (1.0 + jnp.exp(-gate)) * up).astype(BF)
        gather_c.step1(k)

    def down(k):
        gather_c.step5(k)
        if k == 0:
            loads[3].wait()
        scatter_a.close(k)

        multiply(
            lambda: jnp.concatenate([hidden_all[k, c].reshape(ROWS, half) for c in (0, 1)], axis=1),
            wd,
            proj.at[k],
            side,
            lambda j: scatter_c.step1(k, j),
        )

    def finish(k):
        total = (hid[k].astype(F32) + scatter_c.total(k)).astype(BF)
        for r in (0, 1):
            out[r * MAXTREE + k * NODES : r * MAXTREE + (k + 1) * NODES, :] = total[r * NODES : (r + 1) * NODES, :]

    stages = [
        start,
        gather_a.step2,
        gather_a.step3,
        project,
        scatter_a.step2,
        scatter_a.step3,
        scatter_a.step4,
        norm,
        gather_b.step2,
        gather_b.step3,
        gather_b.step4,
        gate_up,
        scatter_b.step2,
        scatter_b.step3,
        scatter_b.step4,
        activate,
        gather_c.step2,
        gather_c.step3,
        gather_c.step4,
        gather_c.far1,
        gather_c.far2,
        down,
        scatter_c.step2,
        scatter_c.step3,
        scatter_c.step4,
        finish,
    ]
    ahead = [iter(stages) for k in range(CHUNKS)]
    for k in TURNS:
        next(ahead[k])(k)
    for group in (gather_a, gather_b, gather_c, scatter_a, scatter_b, scatter_c):
        for k in range(CHUNKS):
            group.close(k)


TURNS = (
    0, 1, 0, 3, 1, 0, 2, 1, 3, 2, 0, 1, 0, 0, 2, 3, 1, 1, 0, 1, 0, 1, 2, 0,
    3, 0, 1, 2, 2, 0, 3, 3, 1, 2, 0, 3, 1, 2, 0, 3, 1, 0, 0, 2, 3, 1, 2, 0,
    1, 2, 3, 1, 2, 0, 2, 0, 1, 2, 3, 2, 3, 0, 0, 2, 0, 3, 3, 1, 1, 0, 3, 2,
    1, 2, 1, 3, 1, 0, 2, 2, 3, 0, 3, 1, 2, 3, 3, 2, 1, 3, 1, 0, 3, 2, 2, 3,
    3, 1, 2, 3, 0, 1, 2, 3,
)


def layer(page_table, cache_len, tree_size, parents, queries, tree_kv, cache, resid, gain, w_out, w_gate, w_up, w_down):
    heads, width = w_out.shape
    depth, units = w_gate.shape
    half = units // 2
    sums = 2 * half + LANES
    vmem = pl.BlockSpec(memory_space=pltpu.VMEM)
    smem = pl.BlockSpec(memory_space=pltpu.SMEM)
    hbm = pl.BlockSpec(memory_space=pl.ANY)
    sem = pltpu.SemaphoreType.DMA

    def scatter_buffers(lanes, pair):
        first = [pltpu.VMEM((CHUNKS, BLOCK, lanes), BF)] if pair else []
        return [
            *first,
            pltpu.VMEM((CHUNKS, 2, BLOCK // 2 if pair else BLOCK, lanes), BF),
            pltpu.VMEM((CHUNKS, 2, 2, BLOCK, lanes), BF),
            pltpu.VMEM((CHUNKS, BLOCK, lanes), BF),
        ]

    scratch = [
        pltpu.VMEM((heads, width), BF),
        pltpu.VMEM((2 * depth, units), BF),
        pltpu.VMEM((units, width), BF),
        pltpu.VMEM((CHUNKS, 8, 2, NODES, heads), BF),
        pltpu.VMEM((CHUNKS, 8, BLOCK, width), BF),
        pltpu.VMEM((CHUNKS, BLOCK, width), BF),
        pltpu.VMEM((CHUNKS, 2, 8, BLOCK, width + LANES), BF),
        pltpu.VMEM((2, 8, BLOCK, sums), BF),
        pltpu.VMEM((CHUNKS, 2, 8, BLOCK, half), BF),
        pltpu.VMEM((MAXTREE, MAXTREE), F32),
        *scatter_buffers(width, True),
        *scatter_buffers(sums, True),
        *scatter_buffers(width, True),
        sem((4,)),
        sem((2,)),
        sem((2,)),
        *[sem((CHUNKS, 14))] * 6,
        *[sem((CHUNKS * PIECES, 10))] * 6,
    ]
    return pl.pallas_call(
        layer_kernel,
        out_shape=jax.ShapeDtypeStruct(resid.shape, BF),
        in_specs=[smem, smem, smem, vmem, vmem, vmem, vmem, vmem, vmem, hbm, hbm, hbm, hbm],
        out_specs=vmem,
        scratch_shapes=scratch,
        compiler_params=pltpu.CompilerParams(
            collective_id=0, has_side_effects=True, vmem_limit_bytes=62 * 1024 * 1024
        ),
        cost_estimate=pl.CostEstimate(
            flops=2 * 1024 * (heads * width + 3 * depth * units), bytes_accessed=26 * 1024 * 1024, transcendentals=0
        ),
    )(
        page_table,
        cache_len,
        tree_size,
        parents,
        queries,
        tree_kv,
        cache,
        resid,
        gain,
        w_out,
        w_gate,
        w_up,
        w_down,
    )


def body(
    resid,
    queries,
    tree_kv,
    cache,
    page_table,
    cache_len,
    tree_size,
    parents,
    w_out,
    gain,
    w_gate,
    w_up,
    w_down,
):
    return layer(
        page_table,
        cache_len,
        tree_size,
        parents,
        queries,
        tree_kv,
        cache,
        resid,
        gain,
        w_out,
        w_gate,
        w_up,
        w_down,
    )


def solution(mesh):
    in_specs = (
        P("gx", "gy"),
        P("gy", "gx"),
        P("gy", "gx"),
        P("gx", "gy", None, None),
        P("gy", None),
        P("gy"),
        P("gy"),
        P("gy", None),
        P("gx", "gy"),
        P("gy"),
        P("gy", "gx"),
        P("gy", "gx"),
        P("gx", "gy"),
    )
    out_specs = P("gx", "gy")
    return jax.shard_map(body, mesh=mesh, in_specs=in_specs, out_specs=out_specs, check_vma=False)
```

```python
import math

import jax
import jax.numpy as jnp
from jax import lax
from jax.experimental import pallas as pl
from jax.experimental.pallas import tpu as pltpu
from jax.sharding import PartitionSpec as P

D = 16384
HD = 128
MAXTREE = 64
PAGE = 128
MAXPAGES = 8
EPSILON = 1e-05

MESH = pl.DeviceIdType.MESH
BF = jnp.bfloat16
F32 = jnp.float32

CHUNKS = 4
NODES = MAXTREE // CHUNKS
BLOCK = 2 * NODES
ROWS = 8 * BLOCK
LANES = 128
FRONT, BACK = pl.ds(0, BLOCK // 2), pl.ds(BLOCK // 2, BLOCK // 2)
TILE = 1024
PIECES = 4


def visible_nodes(parents, tree_len):
    shape = (MAXTREE, MAXTREE)
    column, row = lax.broadcasted_iota(jnp.int32, shape, 1), lax.broadcasted_iota(jnp.int32, shape, 0)
    eye = jnp.where(row == column, 1.0, 0.0)
    reach = eye + jnp.where(parents == row, 1.0, 0.0)
    for sweep in range((MAXTREE - 1).bit_length()):
        held = reach.astype(BF)
        reach = jnp.minimum(jnp.dot(held, held, preferred_element_type=F32), 1.0)
    turned = lax.dot_general(
        reach.astype(BF), eye.astype(BF), (((0,), (0,)), ((), ())), preferred_element_type=F32
    )
    return jnp.where(column < tree_len, turned, 0.0)


def attend(query, visible, live, cached, tree_kv, cache, page_table):
    heads = query.shape[1] // HD
    keys = jnp.concatenate([query[:, h * HD : (h + 1) * HD] for h in range(heads)], axis=0)
    contract = (((1,), (1,)), ((), ()))
    context = cache[0].reshape(MAXPAGES * PAGE, 2 * HD)
    scale = HD ** (-0.5) * math.log2(math.e)
    ctx_scores = lax.dot_general(keys, context[:, 0:HD], contract, preferred_element_type=F32)
    tree_scores = lax.dot_general(keys, tree_kv[:, 0:HD], contract, preferred_element_type=F32)
    offset = lax.broadcasted_iota(jnp.int32, (1, PAGE), 1)
    bounds = []
    for page in range(MAXPAGES):
        place = jnp.int32(0)
        for p in range(1, MAXPAGES):
            place = jnp.where(page_table[0, p] == page, p, place)
        bounds.append(offset < cached - place * PAGE)
    allowed = jnp.concatenate([jnp.where(bound, 1.0, 0.0) for bound in bounds], axis=1)
    ctx_scores = jnp.where(allowed > 0.5, ctx_scores, -1e30)
    seen = jnp.concatenate([visible] * heads, axis=0)
    tree_scores = jnp.where(seen > 0.5, tree_scores, -1e30)
    row_max = jnp.maximum(
        jnp.max(ctx_scores, axis=-1, keepdims=True), jnp.max(tree_scores, axis=-1, keepdims=True)
    )
    ctx_exp = jnp.exp2((ctx_scores - row_max) * scale)
    tree_exp = jnp.exp2((tree_scores - row_max) * scale)
    total = jnp.sum(ctx_exp, axis=-1, keepdims=True) + jnp.sum(tree_exp, axis=-1, keepdims=True)
    mixed = jnp.dot(ctx_exp.astype(BF), context[:, HD:], preferred_element_type=F32)
    mixed += jnp.dot(tree_exp.astype(BF), tree_kv[:, HD:], preferred_element_type=F32)
    mixed *= 1.0 / total
    count = query.shape[0]
    parts = [jnp.where(live, mixed[h * count : (h + 1) * count, :], 0.0).astype(BF) for h in range(heads)]
    return jnp.concatenate(parts, axis=1)


def remote(src, dst, send_sem, recv_sem, device):
    return pltpu.make_async_remote_copy(
        src_ref=src,
        dst_ref=dst,
        send_sem=send_sem,
        recv_sem=recv_sem,
        device_id=device,
        device_id_type=MESH,
    )


def multiply(rows, weights, result, tile, done):
    width = weights.shape[1]
    for j, at in enumerate(range(0, width, tile)):
        size = min(tile, width - at)
        product = jnp.dot(rows(), weights[:, at : at + size], preferred_element_type=F32)
        result[:, :, at : at + size] = product.astype(BF).reshape(8, BLOCK, size)
        done(j)


def other_core(device):
    gx, gy = device
    return gx, gy + 1 - 2 * lax.rem(gy, 2)


class Place:
    def __init__(self, r, p, prev, follow, pair, sib, core, index):
        self.r, self.p = r, p
        self.prev, self.follow, self.pair, self.sib = prev, follow, pair, sib
        self.core = core
        self.index = index

    def block(self, p, shift):
        return self.index(p, lax.rem(self.r + (4 + shift), 4))


class Scatter:
    def __init__(self, place, part, buffers, send, recv, cuts):
        self.at, self.part = place, part
        self.far, self.near, self.last = buffers
        self.send, self.recv = send, recv
        self.cuts = cuts
        self.open = {}

    def push(self, slot, src, dst, sem, device):
        copy = remote(src, dst, self.send.at[slot, sem], self.recv.at[slot, sem], device)
        copy.start()
        return copy

    def hand(self, k, src, dst, sem, device):
        self.open.setdefault(k, []).append(self.push(k * len(self.cuts), src, dst, sem, device))

    def arrived(self, k, ref, sem, pieces=False):
        for j, columns in enumerate(self.cuts if pieces else [None]):
            slot = k * len(self.cuts) + j
            piece = ref.at[:, columns] if pieces else ref
            remote(piece, piece, self.send.at[slot, sem], self.recv.at[slot, sem], self.at.pair).wait_recv()

    def first_sends(self, k):
        at, part = self.at, self.part(k)
        return [
            (part.at[at.block(0, 2)], self.far.at[k, 0], 0, at.follow),
            (part.at[at.block(1, 2)], self.far.at[k, 1], 1, at.prev),
            (part.at[at.block(1, 1)], self.near.at[k, 0, 1], 3, at.follow),
            (part.at[at.block(0, -1)], self.near.at[k, 1, 0], 4, at.prev),
        ]

    def step1(self, k, j):
        columns = self.cuts[j]
        for src, dst, sem, device in self.first_sends(k):
            copy = self.push(k * len(self.cuts) + j, src.at[:, columns], dst.at[:, columns], sem, device)
            self.open.setdefault(k, []).append(copy)

    def step2(self, k):
        at, part = self.at, self.part(k)
        for way, (p, shift, device, sem) in enumerate(((0, 1, at.follow, 2), (1, -1, at.prev, 5))):
            self.arrived(k, self.far.at[k, way], way, True)
            mine = at.block(p, shift)
            part[mine] = (part[mine].astype(F32) + self.far[k, way].astype(F32)).astype(BF)
            self.hand(k, part.at[mine], self.near.at[k, way, p], sem, device)

    def ring_sum(self, k, p):
        return (
            self.part(k)[self.at.block(p, 0)].astype(F32)
            + self.near[k, 0, p].astype(F32)
            + self.near[k, 1, p].astype(F32)
        )

    def step3(self, k):
        at, part = self.at, self.part(k)
        self.arrived(k, self.near.at[k, 0, 0], 2)
        self.arrived(k, self.near.at[k, 0, 1], 3, True)
        self.arrived(k, self.near.at[k, 1, 0], 4, True)
        self.arrived(k, self.near.at[k, 1, 1], 5)
        other = 1 - at.p
        theirs = at.block(other, 0)
        part[theirs] = self.ring_sum(k, other).astype(BF)
        self.hand(k, part.at[theirs], self.last.at[k], 6, at.pair)

    def total(self, k):
        self.arrived(k, self.last.at[k], 6)
        return self.ring_sum(k, self.at.p) + self.last[k].astype(F32)

    def close(self, k):
        for copy in self.open.pop(k, []):
            copy.wait_send()


class PairScatter(Scatter):
    def __init__(self, place, part, buffers, send, recv, cuts):
        super().__init__(place, part, buffers[1:], send, recv, cuts)
        self.first = buffers[0]

    def first_sends(self, k):
        at, part = self.at, self.part(k)
        p, other = at.p, 1 - at.p
        return [
            (part.at[at.block(other, 2)], self.first.at[k], 0, at.pair),
            (part.at[at.block(other, 1)], self.near.at[k, 0, other], 3, at.follow),
            (part.at[at.block(other, -1)], self.near.at[k, 1, other], 4, at.prev),
            (part.at[at.block(p, 1), BACK], self.near.at[k, 0, p, BACK], 6, at.follow),
            (part.at[at.block(p, -1), FRONT], self.near.at[k, 1, p, FRONT], 8, at.prev),
        ]

    def step2(self, k):
        at, part = self.at, self.part(k)
        self.arrived(k, self.first.at[k], 0, True)
        mine = at.block(at.p, 2)
        part[mine] = (part[mine].astype(F32) + self.first[k].astype(F32)).astype(BF)
        self.hand(k, part.at[mine, FRONT], self.far.at[k, 0], 1, at.follow)
        self.hand(k, part.at[mine, BACK], self.far.at[k, 1], 2, at.prev)

    def step3(self, k):
        at, part = self.at, self.part(k)
        other = 1 - at.p
        self.arrived(k, self.near.at[k, 0, other], 3, True)
        self.arrived(k, self.near.at[k, 1, other], 4, True)
        theirs = at.block(other, 0)
        part[theirs] = self.ring_sum(k, other).astype(BF)
        self.hand(k, part.at[theirs], self.last.at[k], 9, at.pair)

    def step4(self, k):
        at, part = self.at, self.part(k)
        for way, (shift, rows, sem, device) in enumerate(((1, FRONT, 5, at.follow), (-1, BACK, 7, at.prev))):
            self.arrived(k, self.far.at[k, way], 1 + way)
            mine = at.block(at.p, shift)
            part[mine, rows] = (part[mine, rows].astype(F32) + self.far[k, way].astype(F32)).astype(BF)
            self.hand(k, part.at[mine, rows], self.near.at[k, way, at.p, rows], sem, device)

    def total(self, k):
        p = self.at.p
        for way, (added, alone) in enumerate(((FRONT, BACK), (BACK, FRONT))):
            self.arrived(k, self.near.at[k, way, p, added], 5 + 2 * way)
            self.arrived(k, self.near.at[k, way, p, alone], 6 + 2 * way, True)
        self.arrived(k, self.last.at[k], 9)
        return self.ring_sum(k, p) + self.last[k].astype(F32)


class Gather:
    def __init__(self, place, ref, send, recv):
        self.at, self.ref = place, ref
        self.send, self.recv = send, recv
        self.open = {}

    def push(self, k, block, sem, device):
        ref = self.ref(k, self.at.core, block)
        copy = remote(ref, ref, self.send.at[k, sem], self.recv.at[k, sem], device)
        copy.start()
        self.open.setdefault(k, []).append(copy)

    def arrived(self, k, block, sem, core):
        ref = self.ref(k, core, block)
        remote(ref, ref, self.send.at[k, sem], self.recv.at[k, sem], self.at.pair).wait_recv()

    def both(self, shift):
        return pl.ds(self.at.block(0, shift), 2)

    def share(self, k, shift):
        self.push(k, self.both(shift), 7 + shift % 4, self.at.sib)

    def step1(self, k):
        at = self.at
        mine = at.block(at.p, 0)
        self.push(k, mine, 0, at.pair)
        self.push(k, mine, 1 + at.p, at.follow)
        self.push(k, mine, 3 + at.p, at.prev)

    def step2(self, k):
        at = self.at
        other = 1 - at.p
        block = at.block(other, 0)
        self.arrived(k, block, 0, at.core)
        self.push(k, block, 1 + other, at.follow)
        self.push(k, block, 3 + other, at.prev)
        self.share(k, 0)

    def step3(self, k):
        at = self.at
        left, right = at.block(0, -1), at.block(1, 1)
        self.arrived(k, left, 1, at.core)
        self.push(k, left, 5, at.follow)
        self.arrived(k, right, 4, at.core)
        self.push(k, right, 6, at.prev)
        self.arrived(k, at.block(1, -1), 2, at.core)
        self.share(k, -1)
        self.arrived(k, at.block(0, 1), 3, at.core)
        self.share(k, 1)

    def step4(self, k):
        at = self.at
        self.arrived(k, at.block(0, 2), 5, at.core)
        self.arrived(k, at.block(1, 2), 6, at.core)
        self.share(k, 2)

    def step5(self, k):
        for shift in (0, 1, -1, 2):
            self.arrived(k, self.both(shift), 7 + shift % 4, 1 - self.at.core)

    def close(self, k):
        for copy in self.open.pop(k, []):
            copy.wait_send()


class FarGather(Gather):
    def step3(self, k):
        at = self.at
        left, right = at.block(0, -1), at.block(1, 1)
        self.arrived(k, left, 1, at.core)
        self.push(k, left, 5, at.follow)
        self.push(k, left, 12, other_core(at.follow))
        self.arrived(k, right, 4, at.core)
        self.push(k, right, 6, at.prev)
        self.push(k, right, 13, other_core(at.prev))
        self.arrived(k, at.block(1, -1), 2, at.core)
        self.share(k, -1)
        self.arrived(k, at.block(0, 1), 3, at.core)
        self.share(k, 1)

    def step5(self, k):
        at = self.at
        for shift in (0, 1, -1):
            self.arrived(k, self.both(shift), 7 + shift % 4, 1 - at.core)
        for core, sems in ((at.core, (5, 6)), (1 - at.core, (12, 13))):
            self.arrived(k, at.block(0, 2), sems[0], core)
            self.arrived(k, at.block(1, 2), sems[1], core)


class PairGather(Gather):
    def hand(self, k, ref, sem, device):
        copy = remote(ref, ref, self.send.at[k, sem], self.recv.at[k, sem], device)
        copy.start()
        self.open.setdefault(k, []).append(copy)

    def landed(self, k, ref, sem):
        remote(ref, ref, self.send.at[k, sem], self.recv.at[k, sem], self.at.pair).wait_recv()

    def step1(self, k):
        at = self.at
        mine = at.block(at.p, 0)
        self.push(k, mine, 0, at.pair)
        self.push(k, mine, 1, at.follow)
        self.push(k, mine, 2, at.prev)

    def step2(self, k):
        at = self.at
        block = at.block(1 - at.p, 0)
        self.arrived(k, block, 0, at.core)
        self.push(k, block, 3, at.follow)
        self.push(k, block, 4, at.prev)
        self.share(k, 0)

    def step3(self, k):
        at = self.at
        left, right = at.block(at.p, -1), at.block(at.p, 1)
        self.arrived(k, left, 1, at.core)
        self.hand(k, self.ref(k, at.core, left).at[FRONT], 5, at.follow)
        self.arrived(k, right, 2, at.core)
        self.hand(k, self.ref(k, at.core, right).at[BACK], 6, at.prev)

    def step4(self, k):
        at = self.at
        self.arrived(k, at.block(1 - at.p, -1), 3, at.core)
        self.share(k, -1)
        self.arrived(k, at.block(1 - at.p, 1), 4, at.core)
        self.share(k, 1)

    def far1(self, k):
        at = self.at
        block = at.block(at.p, 2)
        self.landed(k, self.ref(k, at.core, block).at[FRONT], 5)
        self.landed(k, self.ref(k, at.core, block).at[BACK], 6)
        self.push(k, block, 11, at.pair)

    def far2(self, k):
        at = self.at
        self.arrived(k, at.block(1 - at.p, 2), 11, at.core)
        self.share(k, 2)


def layer_kernel(
    page_table,
    cache_len,
    tree_size,
    parents,
    queries_hbm,
    tree_kv_hbm,
    cache_hbm,
    resid_hbm,
    gain,
    w_out,
    w_gate,
    w_up,
    w_down,
    out_hbm,
    queries,
    tree_kv,
    cache,
    resid,
    out,
    wo,
    wgu,
    wd,
    attn_all,
    proj,
    hid,
    normed_all,
    sums,
    hidden_all,
    visible,
    first_a,
    far_a,
    near_a,
    last_a,
    first_b,
    far_b,
    near_b,
    last_b,
    first_c,
    far_c,
    near_c,
    last_c,
    load_sem,
    store_sem,
    swap_send,
    swap_recv,
    ga_send,
    ga_recv,
    gb_send,
    gb_recv,
    gc_send,
    gc_recv,
    sa_send,
    sa_recv,
    sb_send,
    sb_recv,
    sc_send,
    sc_recv,
):
    gx, gy = lax.axis_index("gx"), lax.axis_index("gy")
    yh, x = lax.div(gx, 4), lax.rem(gx, 4)
    z, yl, core = lax.div(gy, 4), lax.rem(lax.div(gy, 2), 2), lax.rem(gy, 2)
    width = wo.shape[1]
    half = wgu.shape[1] // 2
    depth = w_gate.shape[0]

    sib = (gx, z * 4 + yl * 2 + (1 - core))
    along_x = Place(
        x,
        yh,
        (yh * 4 + lax.rem(x + 3, 4), gy),
        (yh * 4 + lax.rem(x + 1, 4), gy),
        ((1 - yh) * 4 + x, gy),
        sib,
        core,
        lambda p, r: r * 2 + p,
    )
    along_z = Place(
        z,
        yl,
        (gx, lax.rem(z + 3, 4) * 4 + yl * 2 + core),
        (gx, lax.rem(z + 1, 4) * 4 + yl * 2 + core),
        (gx, z * 4 + (1 - yl) * 2 + core),
        sib,
        core,
        lambda p, r: r * 2 + p,
    )

    barrier = pltpu.get_barrier_semaphore()
    near = [sib, other_core(along_z.prev), other_core(along_z.follow)]
    for place in (along_x, along_z):
        near += [place.prev, place.follow, place.pair]
    for device in near:
        pl.semaphore_signal(barrier, inc=1, device_id=device, device_id_type=MESH)
    loads = []

    def load(src, dst):
        copy = pltpu.make_async_copy(src, dst, load_sem.at[len(loads)])
        copy.start()
        loads.append(copy)

    load(queries_hbm, queries)
    load(tree_kv_hbm, tree_kv)
    load(cache_hbm, cache)
    load(resid_hbm, resid)
    load(w_out, wo)
    mine, theirs = pl.multiple_of(core * half, LANES), pl.multiple_of((1 - core) * half, LANES)
    deep = pl.ds(pl.multiple_of(core * depth, depth), depth)
    load(w_gate.at[:, pl.ds(mine, half)], wgu.at[deep, pl.ds(0, half)])
    load(w_up.at[:, pl.ds(mine, half)], wgu.at[deep, pl.ds(half, half)])
    load(w_down, wd)

    visible[...] = visible_nodes(parents[...], tree_size[0])

    def attention(k):
        nodes = slice(k * NODES, (k + 1) * NODES)
        node = lax.broadcasted_iota(jnp.int32, (NODES, 1), 0) + k * NODES
        attn_all[k, along_z.block(yl, 0), core] = attend(
            queries[nodes, :], visible[nodes, :], node < tree_size[0], cache_len[0], tree_kv[...], cache, page_table
        )

    for copy in loads[0:3]:
        copy.wait()
    attention(0)
    pl.semaphore_wait(barrier, len(near))

    side = width // 1
    halves = [pl.ds(at, side) for at in range(0, width, side)]
    quarters = [pl.ds(at, min(TILE, sums.shape[-1] - at)) for at in range(0, sums.shape[-1], TILE)]
    assert len(quarters) == PIECES
    gather_a = FarGather(along_z, lambda k, c, b: attn_all.at[k, b, c], ga_send, ga_recv)
    gather_b = Gather(along_x, lambda k, c, b: normed_all.at[k, c, b], gb_send, gb_recv)
    gather_c = PairGather(along_z, lambda k, c, b: hidden_all.at[k, c, b], gc_send, gc_recv)
    scatter_a = PairScatter(along_x, lambda k: proj.at[k], (first_a, far_a, near_a, last_a), sa_send, sa_recv, halves)
    scatter_b = PairScatter(along_z, lambda k: sums.at[k % 2], (first_b, far_b, near_b, last_b), sb_send, sb_recv, quarters)
    scatter_c = PairScatter(along_x, lambda k: proj.at[k], (first_c, far_c, near_c, last_c), sc_send, sc_recv, halves)

    swaps = [
        remote(
            w.at[:, pl.ds(theirs, half)],
            wgu.at[deep, pl.ds(n * half, half)],
            swap_send.at[n],
            swap_recv.at[n],
            sib,
        )
        for n, w in enumerate((w_gate, w_up))
    ]
    for copy in swaps:
        copy.start()

    def start(k):
        if k > 0:
            attention(k)
        gather_a.step1(k)

    def project(k):
        gather_a.step5(k)
        if k == 0:
            loads[4].wait()

        multiply(
            lambda: jnp.concatenate(
                [attn_all[k, q].reshape(BLOCK, attn_all.shape[-1]) for q in (0, 4, 1, 5, 2, 6, 3, 7)], axis=0
            ),
            wo,
            proj.at[k],
            side,
            lambda j: scatter_a.step1(k, j),
        )

    def norm(k):
        if k == 0:
            loads[3].wait()
        projected = scatter_a.total(k)
        rows = jnp.concatenate([resid[r * MAXTREE + k * NODES : r * MAXTREE + (k + 1) * NODES, :] for r in (0, 1)], axis=0)
        value = (rows.astype(F32) + projected).astype(BF)
        hid[k] = value
        wide = value.astype(F32)
        mine = along_x.block(yh, 0)
        normed_all[k, core, mine, :, 0:width] = (wide * gain[...].astype(F32).reshape(1, width)).astype(BF)
        squares = jnp.sum(wide * wide, axis=1, keepdims=True)
        normed_all[k, core, mine, :, width:] = jnp.broadcast_to(squares, (BLOCK, LANES)).astype(BF)
        gather_b.step1(k)

    def gate_up(k):
        gather_b.step5(k)
        if k == 0:
            loads[5].wait()
            loads[6].wait()
            for copy in swaps:
                copy.wait()
        if k >= 2:
            scatter_b.close(k - 2)
        part = sums.at[k % 2]
        squares = normed_all[k, 0, :, :, width:].astype(F32) + normed_all[k, 1, :, :, width:].astype(F32)
        part[:, :, 2 * half :] = squares.astype(BF)

        multiply(
            lambda: jnp.concatenate(
                [normed_all[k, c, :, :, 0:width].reshape(ROWS, width) for c in (0, 1)], axis=1
            ),
            wgu,
            part,
            TILE,
            lambda j: scatter_b.step1(k, j),
        )

    def activate(k):
        total = scatter_b.total(k)
        scale = lax.rsqrt(total[:, 2 * half : 2 * half + 1] / D + EPSILON)
        gate = total[:, 0:half] * scale
        up = total[:, half : 2 * half] * scale
        hidden_all[k, core, along_z.block(yl, 0)] = (gate / (1.0 + jnp.exp(-gate)) * up).astype(BF)
        gather_c.step1(k)

    def down(k):
        gather_c.step5(k)
        if k == 0:
            loads[7].wait()
        scatter_a.close(k)

        multiply(
            lambda: jnp.concatenate([hidden_all[k, c].reshape(ROWS, half) for c in (0, 1)], axis=1),
            wd,
            proj.at[k],
            side,
            lambda j: scatter_c.step1(k, j),
        )

    stores = []

    def finish(k):
        total = (hid[k].astype(F32) + scatter_c.total(k)).astype(BF)
        for r in (0, 1):
            rows = slice(r * MAXTREE + k * NODES, r * MAXTREE + (k + 1) * NODES)
            out[rows, :] = total[r * NODES : (r + 1) * NODES, :]
            copy = pltpu.make_async_copy(out.at[rows], out_hbm.at[rows], store_sem.at[2 * k + r])
            copy.start()
            stores.append(copy)

    stages = [
        start,
        gather_a.step2,
        gather_a.step3,
        project,
        scatter_a.step2,
        scatter_a.step3,
        scatter_a.step4,
        norm,
        gather_b.step2,
        gather_b.step3,
        gather_b.step4,
        gate_up,
        scatter_b.step2,
        scatter_b.step3,
        scatter_b.step4,
        activate,
        gather_c.step2,
        gather_c.step3,
        gather_c.step4,
        gather_c.far1,
        gather_c.far2,
        down,
        scatter_c.step2,
        scatter_c.step3,
        scatter_c.step4,
        finish,
    ]
    ahead = [iter(stages) for k in range(CHUNKS)]
    for k in TURNS:
        next(ahead[k])(k)
    for group in (gather_a, gather_b, gather_c, scatter_a, scatter_b, scatter_c):
        for k in range(CHUNKS):
            group.close(k)
    for copy in stores:
        copy.wait()


TURNS = (
    0, 3, 0, 1, 0, 2, 1, 0, 2, 1, 0, 0, 2, 0, 1, 0, 3, 1, 1, 0, 1, 2, 3, 0,
    1, 2, 0, 2, 1, 0, 2, 3, 1, 2, 0, 0, 3, 1, 3, 2, 0, 1, 2, 3, 0, 2, 3, 1,
    2, 1, 3, 1, 3, 0, 2, 3, 0, 1, 3, 2, 0, 3, 2, 0, 3, 1, 3, 2, 0, 1, 3, 2,
    1, 2, 1, 0, 3, 2, 3, 2, 1, 3, 0, 3, 2, 1, 0, 0, 3, 2, 1, 3, 1, 2, 1, 2,
    3, 2, 3, 3, 1, 2, 0, 3,
)


def layer(page_table, cache_len, tree_size, parents, queries, tree_kv, cache, resid, gain, w_out, w_gate, w_up, w_down):
    heads, width = w_out.shape
    depth, units = w_gate.shape
    half = units // 2
    sums = 2 * half + LANES
    vmem = pl.BlockSpec(memory_space=pltpu.VMEM)
    smem = pl.BlockSpec(memory_space=pltpu.SMEM)
    hbm = pl.BlockSpec(memory_space=pl.ANY)
    sem = pltpu.SemaphoreType.DMA

    def scatter_buffers(lanes, pair):
        first = [pltpu.VMEM((CHUNKS, BLOCK, lanes), BF)] if pair else []
        return [
            *first,
            pltpu.VMEM((CHUNKS, 2, BLOCK // 2 if pair else BLOCK, lanes), BF),
            pltpu.VMEM((CHUNKS, 2, 2, BLOCK, lanes), BF),
            pltpu.VMEM((CHUNKS, BLOCK, lanes), BF),
        ]

    scratch = [
        *[pltpu.VMEM(a.shape, BF) for a in (queries, tree_kv, cache, resid, resid)],
        pltpu.VMEM((heads, width), BF),
        pltpu.VMEM((2 * depth, units), BF),
        pltpu.VMEM((units, width), BF),
        pltpu.VMEM((CHUNKS, 8, 2, NODES, heads), BF),
        pltpu.VMEM((CHUNKS, 8, BLOCK, width), BF),
        pltpu.VMEM((CHUNKS, BLOCK, width), BF),
        pltpu.VMEM((CHUNKS, 2, 8, BLOCK, width + LANES), BF),
        pltpu.VMEM((2, 8, BLOCK, sums), BF),
        pltpu.VMEM((CHUNKS, 2, 8, BLOCK, half), BF),
        pltpu.VMEM((MAXTREE, MAXTREE), F32),
        *scatter_buffers(width, True),
        *scatter_buffers(sums, True),
        *scatter_buffers(width, True),
        sem((8,)),
        sem((2 * CHUNKS,)),
        sem((2,)),
        sem((2,)),
        *[sem((CHUNKS, 14))] * 6,
        *[sem((CHUNKS * PIECES, 10))] * 6,
    ]
    return pl.pallas_call(
        layer_kernel,
        out_shape=jax.ShapeDtypeStruct(resid.shape, BF),
        in_specs=[smem, smem, smem, vmem, hbm, hbm, hbm, hbm, vmem, hbm, hbm, hbm, hbm],
        out_specs=hbm,
        scratch_shapes=scratch,
        compiler_params=pltpu.CompilerParams(
            collective_id=0, has_side_effects=True, vmem_limit_bytes=62 * 1024 * 1024
        ),
        cost_estimate=pl.CostEstimate(
            flops=2 * 1024 * (heads * width + 3 * depth * units), bytes_accessed=26 * 1024 * 1024, transcendentals=0
        ),
    )(
        page_table,
        cache_len,
        tree_size,
        parents,
        queries,
        tree_kv,
        cache,
        resid,
        gain,
        w_out,
        w_gate,
        w_up,
        w_down,
    )


def body(
    resid,
    queries,
    tree_kv,
    cache,
    page_table,
    cache_len,
    tree_size,
    parents,
    w_out,
    gain,
    w_gate,
    w_up,
    w_down,
):
    return layer(
        page_table,
        cache_len,
        tree_size,
        parents,
        queries,
        tree_kv,
        cache,
        resid,
        gain,
        w_out,
        w_gate,
        w_up,
        w_down,
    )


def solution(mesh):
    in_specs = (
        P("gx", "gy"),
        P("gy", "gx"),
        P("gy", "gx"),
        P("gx", "gy", None, None),
        P("gy", None),
        P("gy"),
        P("gy"),
        P("gy", None),
        P("gx", "gy"),
        P("gy"),
        P("gy", "gx"),
        P("gy", "gx"),
        P("gx", "gy"),
    )
    out_specs = P("gx", "gy")
    return jax.shard_map(body, mesh=mesh, in_specs=in_specs, out_specs=out_specs, check_vma=False)
```

```python
import math

import jax
import jax.numpy as jnp
from jax import lax
from jax.experimental import pallas as pl
from jax.experimental.pallas import tpu as pltpu
from jax.sharding import PartitionSpec as P

D = 16384
HD = 128
MAXTREE = 64
PAGE = 128
MAXPAGES = 8
EPSILON = 1e-05

MESH = pl.DeviceIdType.MESH
BF = jnp.bfloat16
F32 = jnp.float32

CHUNKS = 4
NODES = MAXTREE // CHUNKS
BLOCK = 2 * NODES
ROWS = 8 * BLOCK
LANES = 128
FRONT, BACK = pl.ds(0, BLOCK // 2), pl.ds(BLOCK // 2, BLOCK // 2)
TILE = 1024
PIECES = 4


def visible_nodes(parents, tree_len):
    shape = (MAXTREE, MAXTREE)
    column, row = lax.broadcasted_iota(jnp.int32, shape, 1), lax.broadcasted_iota(jnp.int32, shape, 0)
    eye = jnp.where(row == column, 1.0, 0.0)
    reach = eye + jnp.where(parents == row, 1.0, 0.0)
    for sweep in range((MAXTREE - 1).bit_length()):
        held = reach.astype(BF)
        reach = jnp.minimum(jnp.dot(held, held, preferred_element_type=F32), 1.0)
    turned = lax.dot_general(
        reach.astype(BF), eye.astype(BF), (((0,), (0,)), ((), ())), preferred_element_type=F32
    )
    return jnp.where(column < tree_len, turned, 0.0)


def attend(query, visible, live, cached, tree_kv, cache, page_table):
    heads = query.shape[1] // HD
    keys = jnp.concatenate([query[:, h * HD : (h + 1) * HD] for h in range(heads)], axis=0)
    contract = (((1,), (1,)), ((), ()))
    context = cache[0].reshape(MAXPAGES * PAGE, 2 * HD)
    scale = HD ** (-0.5) * math.log2(math.e)
    ctx_scores = lax.dot_general(keys, context[:, 0:HD], contract, preferred_element_type=F32)
    tree_scores = lax.dot_general(keys, tree_kv[:, 0:HD], contract, preferred_element_type=F32)
    offset = lax.broadcasted_iota(jnp.int32, (1, PAGE), 1)
    bounds = []
    for page in range(MAXPAGES):
        place = jnp.int32(0)
        for p in range(1, MAXPAGES):
            place = jnp.where(page_table[0, p] == page, p, place)
        bounds.append(offset < cached - place * PAGE)
    allowed = jnp.concatenate([jnp.where(bound, 1.0, 0.0) for bound in bounds], axis=1)
    ctx_scores = jnp.where(allowed > 0.5, ctx_scores, -1e30)
    seen = jnp.concatenate([visible] * heads, axis=0)
    tree_scores = jnp.where(seen > 0.5, tree_scores, -1e30)
    row_max = jnp.maximum(
        jnp.max(ctx_scores, axis=-1, keepdims=True), jnp.max(tree_scores, axis=-1, keepdims=True)
    )
    ctx_exp = jnp.exp2((ctx_scores - row_max) * scale)
    tree_exp = jnp.exp2((tree_scores - row_max) * scale)
    total = jnp.sum(ctx_exp, axis=-1, keepdims=True) + jnp.sum(tree_exp, axis=-1, keepdims=True)
    mixed = jnp.dot(ctx_exp.astype(BF), context[:, HD:], preferred_element_type=F32)
    mixed += jnp.dot(tree_exp.astype(BF), tree_kv[:, HD:], preferred_element_type=F32)
    mixed *= 1.0 / total
    count = query.shape[0]
    parts = [jnp.where(live, mixed[h * count : (h + 1) * count, :], 0.0).astype(BF) for h in range(heads)]
    return jnp.concatenate(parts, axis=1)


def remote(src, dst, send_sem, recv_sem, device):
    return pltpu.make_async_remote_copy(
        src_ref=src,
        dst_ref=dst,
        send_sem=send_sem,
        recv_sem=recv_sem,
        device_id=device,
        device_id_type=MESH,
    )


def multiply(rows, weights, result, tile, done):
    width = weights.shape[1]
    for j, at in enumerate(range(0, width, tile)):
        size = min(tile, width - at)
        product = jnp.dot(rows(), weights[:, at : at + size], preferred_element_type=F32)
        result[:, :, at : at + size] = product.astype(BF).reshape(8, BLOCK, size)
        done(j)


def other_core(device):
    gx, gy = device
    return gx, gy + 1 - 2 * lax.rem(gy, 2)


class Place:
    def __init__(self, r, p, prev, follow, pair, sib, core, index):
        self.r, self.p = r, p
        self.prev, self.follow, self.pair, self.sib = prev, follow, pair, sib
        self.core = core
        self.index = index

    def block(self, p, shift):
        return self.index(p, lax.rem(self.r + (4 + shift), 4))


class Scatter:
    def __init__(self, place, part, buffers, send, recv, cuts):
        self.at, self.part = place, part
        self.far, self.near, self.last = buffers
        self.send, self.recv = send, recv
        self.cuts = cuts
        self.open = {}

    def push(self, slot, src, dst, sem, device):
        copy = remote(src, dst, self.send.at[slot, sem], self.recv.at[slot, sem], device)
        copy.start()
        return copy

    def hand(self, k, src, dst, sem, device):
        self.open.setdefault(k, []).append(self.push(k * len(self.cuts), src, dst, sem, device))

    def arrived(self, k, ref, sem, pieces=False):
        for j, columns in enumerate(self.cuts if pieces else [None]):
            slot = k * len(self.cuts) + j
            piece = ref.at[:, columns] if pieces else ref
            remote(piece, piece, self.send.at[slot, sem], self.recv.at[slot, sem], self.at.pair).wait_recv()

    def first_sends(self, k):
        at, part = self.at, self.part(k)
        return [
            (part.at[at.block(0, 2)], self.far.at[k, 0], 0, at.follow),
            (part.at[at.block(1, 2)], self.far.at[k, 1], 1, at.prev),
            (part.at[at.block(1, 1)], self.near.at[k, 0, 1], 3, at.follow),
            (part.at[at.block(0, -1)], self.near.at[k, 1, 0], 4, at.prev),
        ]

    def step1(self, k, j):
        columns = self.cuts[j]
        for src, dst, sem, device in self.first_sends(k):
            copy = self.push(k * len(self.cuts) + j, src.at[:, columns], dst.at[:, columns], sem, device)
            self.open.setdefault(k, []).append(copy)

    def step2(self, k):
        at, part = self.at, self.part(k)
        for way, (p, shift, device, sem) in enumerate(((0, 1, at.follow, 2), (1, -1, at.prev, 5))):
            self.arrived(k, self.far.at[k, way], way, True)
            mine = at.block(p, shift)
            part[mine] = (part[mine].astype(F32) + self.far[k, way].astype(F32)).astype(BF)
            self.hand(k, part.at[mine], self.near.at[k, way, p], sem, device)

    def ring_sum(self, k, p):
        return (
            self.part(k)[self.at.block(p, 0)].astype(F32)
            + self.near[k, 0, p].astype(F32)
            + self.near[k, 1, p].astype(F32)
        )

    def step3(self, k):
        at, part = self.at, self.part(k)
        self.arrived(k, self.near.at[k, 0, 0], 2)
        self.arrived(k, self.near.at[k, 0, 1], 3, True)
        self.arrived(k, self.near.at[k, 1, 0], 4, True)
        self.arrived(k, self.near.at[k, 1, 1], 5)
        other = 1 - at.p
        theirs = at.block(other, 0)
        part[theirs] = self.ring_sum(k, other).astype(BF)
        self.hand(k, part.at[theirs], self.last.at[k], 6, at.pair)

    def total(self, k):
        self.arrived(k, self.last.at[k], 6)
        return self.ring_sum(k, self.at.p) + self.last[k].astype(F32)

    def close(self, k):
        for copy in self.open.pop(k, []):
            copy.wait_send()


class PairScatter(Scatter):
    def __init__(self, place, part, buffers, send, recv, cuts):
        super().__init__(place, part, buffers[1:], send, recv, cuts)
        self.first = buffers[0]

    def first_sends(self, k):
        at, part = self.at, self.part(k)
        p, other = at.p, 1 - at.p
        return [
            (part.at[at.block(other, 2)], self.first.at[k], 0, at.pair),
            (part.at[at.block(other, 1)], self.near.at[k, 0, other], 3, at.follow),
            (part.at[at.block(other, -1)], self.near.at[k, 1, other], 4, at.prev),
            (part.at[at.block(p, 1), BACK], self.near.at[k, 0, p, BACK], 6, at.follow),
            (part.at[at.block(p, -1), FRONT], self.near.at[k, 1, p, FRONT], 8, at.prev),
        ]

    def step2(self, k):
        at, part = self.at, self.part(k)
        self.arrived(k, self.first.at[k], 0, True)
        mine = at.block(at.p, 2)
        part[mine] = (part[mine].astype(F32) + self.first[k].astype(F32)).astype(BF)
        self.hand(k, part.at[mine, FRONT], self.far.at[k, 0], 1, at.follow)
        self.hand(k, part.at[mine, BACK], self.far.at[k, 1], 2, at.prev)

    def step3(self, k):
        at, part = self.at, self.part(k)
        other = 1 - at.p
        self.arrived(k, self.near.at[k, 0, other], 3, True)
        self.arrived(k, self.near.at[k, 1, other], 4, True)
        theirs = at.block(other, 0)
        part[theirs] = self.ring_sum(k, other).astype(BF)
        self.hand(k, part.at[theirs], self.last.at[k], 9, at.pair)

    def step4(self, k):
        at, part = self.at, self.part(k)
        for way, (shift, rows, sem, device) in enumerate(((1, FRONT, 5, at.follow), (-1, BACK, 7, at.prev))):
            self.arrived(k, self.far.at[k, way], 1 + way)
            mine = at.block(at.p, shift)
            part[mine, rows] = (part[mine, rows].astype(F32) + self.far[k, way].astype(F32)).astype(BF)
            self.hand(k, part.at[mine, rows], self.near.at[k, way, at.p, rows], sem, device)

    def total(self, k):
        p = self.at.p
        for way, (added, alone) in enumerate(((FRONT, BACK), (BACK, FRONT))):
            self.arrived(k, self.near.at[k, way, p, added], 5 + 2 * way)
            self.arrived(k, self.near.at[k, way, p, alone], 6 + 2 * way, True)
        self.arrived(k, self.last.at[k], 9)
        return self.ring_sum(k, p) + self.last[k].astype(F32)


class Gather:
    def __init__(self, place, ref, send, recv):
        self.at, self.ref = place, ref
        self.send, self.recv = send, recv
        self.open = {}

    def push(self, k, block, sem, device):
        ref = self.ref(k, self.at.core, block)
        copy = remote(ref, ref, self.send.at[k, sem], self.recv.at[k, sem], device)
        copy.start()
        self.open.setdefault(k, []).append(copy)

    def arrived(self, k, block, sem, core):
        ref = self.ref(k, core, block)
        remote(ref, ref, self.send.at[k, sem], self.recv.at[k, sem], self.at.pair).wait_recv()

    def both(self, shift):
        return pl.ds(self.at.block(0, shift), 2)

    def share(self, k, shift):
        self.push(k, self.both(shift), 7 + shift % 4, self.at.sib)

    def step1(self, k):
        at = self.at
        mine = at.block(at.p, 0)
        self.push(k, mine, 0, at.pair)
        self.push(k, mine, 1 + at.p, at.follow)
        self.push(k, mine, 3 + at.p, at.prev)

    def step2(self, k):
        at = self.at
        other = 1 - at.p
        block = at.block(other, 0)
        self.arrived(k, block, 0, at.core)
        self.push(k, block, 1 + other, at.follow)
        self.push(k, block, 3 + other, at.prev)
        self.share(k, 0)

    def step3(self, k):
        at = self.at
        left, right = at.block(0, -1), at.block(1, 1)
        self.arrived(k, left, 1, at.core)
        self.push(k, left, 5, at.follow)
        self.arrived(k, right, 4, at.core)
        self.push(k, right, 6, at.prev)
        self.arrived(k, at.block(1, -1), 2, at.core)
        self.share(k, -1)
        self.arrived(k, at.block(0, 1), 3, at.core)
        self.share(k, 1)

    def step4(self, k):
        at = self.at
        self.arrived(k, at.block(0, 2), 5, at.core)
        self.arrived(k, at.block(1, 2), 6, at.core)
        self.share(k, 2)

    def step5(self, k):
        for shift in (0, 1, -1, 2):
            self.arrived(k, self.both(shift), 7 + shift % 4, 1 - self.at.core)

    def close(self, k):
        for copy in self.open.pop(k, []):
            copy.wait_send()


class FarGather(Gather):
    def step3(self, k):
        at = self.at
        left, right = at.block(0, -1), at.block(1, 1)
        self.arrived(k, left, 1, at.core)
        self.push(k, left, 5, at.follow)
        self.push(k, left, 12, other_core(at.follow))
        self.arrived(k, right, 4, at.core)
        self.push(k, right, 6, at.prev)
        self.push(k, right, 13, other_core(at.prev))
        self.arrived(k, at.block(1, -1), 2, at.core)
        self.share(k, -1)
        self.arrived(k, at.block(0, 1), 3, at.core)
        self.share(k, 1)

    def step5(self, k):
        at = self.at
        for shift in (0, 1, -1):
            self.arrived(k, self.both(shift), 7 + shift % 4, 1 - at.core)
        for core, sems in ((at.core, (5, 6)), (1 - at.core, (12, 13))):
            self.arrived(k, at.block(0, 2), sems[0], core)
            self.arrived(k, at.block(1, 2), sems[1], core)


class PairGather(Gather):
    def hand(self, k, ref, sem, device):
        copy = remote(ref, ref, self.send.at[k, sem], self.recv.at[k, sem], device)
        copy.start()
        self.open.setdefault(k, []).append(copy)

    def landed(self, k, ref, sem):
        remote(ref, ref, self.send.at[k, sem], self.recv.at[k, sem], self.at.pair).wait_recv()

    def step1(self, k):
        at = self.at
        mine = at.block(at.p, 0)
        self.push(k, mine, 0, at.pair)
        self.push(k, mine, 1, at.follow)
        self.push(k, mine, 2, at.prev)

    def step2(self, k):
        at = self.at
        block = at.block(1 - at.p, 0)
        self.arrived(k, block, 0, at.core)
        self.push(k, block, 3, at.follow)
        self.push(k, block, 4, at.prev)
        self.share(k, 0)

    def step3(self, k):
        at = self.at
        left, right = at.block(at.p, -1), at.block(at.p, 1)
        self.arrived(k, left, 1, at.core)
        self.hand(k, self.ref(k, at.core, left).at[FRONT], 5, at.follow)
        self.arrived(k, right, 2, at.core)
        self.hand(k, self.ref(k, at.core, right).at[BACK], 6, at.prev)

    def step4(self, k):
        at = self.at
        self.arrived(k, at.block(1 - at.p, -1), 3, at.core)
        self.share(k, -1)
        self.arrived(k, at.block(1 - at.p, 1), 4, at.core)
        self.share(k, 1)

    def far1(self, k):
        at = self.at
        block = at.block(at.p, 2)
        self.landed(k, self.ref(k, at.core, block).at[FRONT], 5)
        self.landed(k, self.ref(k, at.core, block).at[BACK], 6)
        self.push(k, block, 11, at.pair)

    def far2(self, k):
        at = self.at
        self.arrived(k, at.block(1 - at.p, 2), 11, at.core)
        self.share(k, 2)


def layer_kernel(
    page_table,
    cache_len,
    tree_size,
    parents,
    queries_hbm,
    tree_kv_hbm,
    cache_hbm,
    resid_hbm,
    gain,
    w_out,
    w_gate,
    w_up,
    w_down,
    out_hbm,
    queries,
    tree_kv,
    cache,
    resid,
    out,
    wo,
    wgu,
    wd,
    attn_all,
    proj,
    hid,
    normed_all,
    sums,
    hidden_all,
    visible,
    first_a,
    far_a,
    near_a,
    last_a,
    first_b,
    far_b,
    near_b,
    last_b,
    first_c,
    far_c,
    near_c,
    last_c,
    load_sem,
    store_sem,
    swap_send,
    swap_recv,
    ga_send,
    ga_recv,
    gb_send,
    gb_recv,
    gc_send,
    gc_recv,
    sa_send,
    sa_recv,
    sb_send,
    sb_recv,
    sc_send,
    sc_recv,
):
    gx, gy = lax.axis_index("gx"), lax.axis_index("gy")
    yh, x = lax.div(gx, 4), lax.rem(gx, 4)
    z, yl, core = lax.div(gy, 4), lax.rem(lax.div(gy, 2), 2), lax.rem(gy, 2)
    width = wo.shape[1]
    half = wgu.shape[1] // 2
    depth = w_gate.shape[0]

    sib = (gx, z * 4 + yl * 2 + (1 - core))
    along_x = Place(
        x,
        yh,
        (yh * 4 + lax.rem(x + 3, 4), gy),
        (yh * 4 + lax.rem(x + 1, 4), gy),
        ((1 - yh) * 4 + x, gy),
        sib,
        core,
        lambda p, r: r * 2 + p,
    )
    along_z = Place(
        z,
        yl,
        (gx, lax.rem(z + 3, 4) * 4 + yl * 2 + core),
        (gx, lax.rem(z + 1, 4) * 4 + yl * 2 + core),
        (gx, z * 4 + (1 - yl) * 2 + core),
        sib,
        core,
        lambda p, r: r * 2 + p,
    )

    barrier = pltpu.get_barrier_semaphore()
    near = [sib, other_core(along_z.prev), other_core(along_z.follow)]
    for place in (along_x, along_z):
        near += [place.prev, place.follow, place.pair]
    for device in near:
        pl.semaphore_signal(barrier, inc=1, device_id=device, device_id_type=MESH)
    loads = []

    def load(src, dst):
        copy = pltpu.make_async_copy(src, dst, load_sem.at[len(loads)])
        copy.start()
        loads.append(copy)

    load(queries_hbm, queries)
    load(tree_kv_hbm, tree_kv)
    load(cache_hbm, cache)
    load(resid_hbm, resid)
    load(w_out, wo)
    mine, theirs = pl.multiple_of(core * half, LANES), pl.multiple_of((1 - core) * half, LANES)
    deep = pl.ds(pl.multiple_of(core * depth, depth), depth)
    load(w_gate.at[:, pl.ds(mine, half)], wgu.at[deep, pl.ds(0, half)])
    load(w_up.at[:, pl.ds(mine, half)], wgu.at[deep, pl.ds(half, half)])
    load(w_down, wd)

    visible[...] = visible_nodes(parents[...], tree_size[0])

    def attention(k):
        nodes = slice(k * NODES, (k + 1) * NODES)
        node = lax.broadcasted_iota(jnp.int32, (NODES, 1), 0) + k * NODES
        attn_all[k, along_z.block(yl, 0), core] = attend(
            queries[nodes, :], visible[nodes, :], node < tree_size[0], cache_len[0], tree_kv[...], cache, page_table
        )

    for copy in loads[0:3]:
        copy.wait()
    attention(0)
    pl.semaphore_wait(barrier, len(near))

    whole = [pl.ds(0, width)]
    down_cuts = [pl.ds(at, width // 2) for at in range(0, width, width // 2)]
    quarters = [pl.ds(at, min(TILE, sums.shape[-1] - at)) for at in range(0, sums.shape[-1], TILE)]
    assert len(quarters) == PIECES
    gather_a = FarGather(along_z, lambda k, c, b: attn_all.at[k, b, c], ga_send, ga_recv)
    gather_b = Gather(along_x, lambda k, c, b: normed_all.at[k, c, b], gb_send, gb_recv)
    gather_c = PairGather(along_z, lambda k, c, b: hidden_all.at[k, c, b], gc_send, gc_recv)
    scatter_a = PairScatter(along_x, lambda k: proj.at[k], (first_a, far_a, near_a, last_a), sa_send, sa_recv, whole)
    scatter_b = PairScatter(along_z, lambda k: sums.at[k % 2], (first_b, far_b, near_b, last_b), sb_send, sb_recv, quarters)
    scatter_c = PairScatter(along_x, lambda k: proj.at[k], (first_c, far_c, near_c, last_c), sc_send, sc_recv, down_cuts)

    swaps = [
        remote(
            w.at[:, pl.ds(theirs, half)],
            wgu.at[deep, pl.ds(n * half, half)],
            swap_send.at[n],
            swap_recv.at[n],
            sib,
        )
        for n, w in enumerate((w_gate, w_up))
    ]
    for copy in swaps:
        copy.start()

    def start(k):
        if k > 0:
            attention(k)
        gather_a.step1(k)

    def project(k):
        gather_a.step5(k)
        if k == 0:
            loads[4].wait()

        multiply(
            lambda: jnp.concatenate(
                [attn_all[k, q].reshape(BLOCK, attn_all.shape[-1]) for q in (0, 4, 1, 5, 2, 6, 3, 7)], axis=0
            ),
            wo,
            proj.at[k],
            width,
            lambda j: scatter_a.step1(k, j),
        )

    def norm(k):
        if k == 0:
            loads[3].wait()
        projected = scatter_a.total(k)
        rows = jnp.concatenate([resid[r * MAXTREE + k * NODES : r * MAXTREE + (k + 1) * NODES, :] for r in (0, 1)], axis=0)
        value = (rows.astype(F32) + projected).astype(BF)
        hid[k] = value
        wide = value.astype(F32)
        mine = along_x.block(yh, 0)
        normed_all[k, core, mine, :, 0:width] = (wide * gain[...].astype(F32).reshape(1, width)).astype(BF)
        squares = jnp.sum(wide * wide, axis=1, keepdims=True)
        normed_all[k, core, mine, :, width:] = jnp.broadcast_to(squares, (BLOCK, LANES)).astype(BF)
        gather_b.step1(k)

    def gate_up(k):
        gather_b.step5(k)
        if k == 0:
            loads[5].wait()
            loads[6].wait()
            for copy in swaps:
                copy.wait()
        if k >= 2:
            scatter_b.close(k - 2)
        part = sums.at[k % 2]
        squares = normed_all[k, 0, :, :, width:].astype(F32) + normed_all[k, 1, :, :, width:].astype(F32)
        part[:, :, 2 * half :] = squares.astype(BF)

        multiply(
            lambda: jnp.concatenate(
                [normed_all[k, c, :, :, 0:width].reshape(ROWS, width) for c in (0, 1)], axis=1
            ),
            wgu,
            part,
            TILE,
            lambda j: scatter_b.step1(k, j),
        )

    def activate(k):
        total = scatter_b.total(k)
        scale = lax.rsqrt(total[:, 2 * half : 2 * half + 1] / D + EPSILON)
        gate = total[:, 0:half] * scale
        up = total[:, half : 2 * half] * scale
        hidden_all[k, core, along_z.block(yl, 0)] = (gate / (1.0 + jnp.exp(-gate)) * up).astype(BF)
        gather_c.step1(k)

    def down(k):
        gather_c.step5(k)
        if k == 0:
            loads[7].wait()
        scatter_a.close(k)

        multiply(
            lambda: jnp.concatenate([hidden_all[k, c].reshape(ROWS, half) for c in (0, 1)], axis=1),
            wd,
            proj.at[k],
            width // 2,
            lambda j: scatter_c.step1(k, j),
        )

    stores = []

    def finish(k):
        total = (hid[k].astype(F32) + scatter_c.total(k)).astype(BF)
        for r in (0, 1):
            rows = slice(r * MAXTREE + k * NODES, r * MAXTREE + (k + 1) * NODES)
            out[rows, :] = total[r * NODES : (r + 1) * NODES, :]
            copy = pltpu.make_async_copy(out.at[rows], out_hbm.at[rows], store_sem.at[2 * k + r])
            copy.start()
            stores.append(copy)

    stages = [
        start,
        gather_a.step2,
        gather_a.step3,
        project,
        scatter_a.step2,
        scatter_a.step3,
        scatter_a.step4,
        norm,
        gather_b.step2,
        gather_b.step3,
        gather_b.step4,
        gate_up,
        scatter_b.step2,
        scatter_b.step3,
        scatter_b.step4,
        activate,
        gather_c.step2,
        gather_c.step3,
        gather_c.step4,
        gather_c.far1,
        gather_c.far2,
        down,
        scatter_c.step2,
        scatter_c.step3,
        scatter_c.step4,
        finish,
    ]
    ahead = [iter(stages) for k in range(CHUNKS)]
    for k in TURNS:
        next(ahead[k])(k)
    for group in (gather_a, gather_b, gather_c, scatter_a, scatter_b, scatter_c):
        for k in range(CHUNKS):
            group.close(k)
    for copy in stores:
        copy.wait()


TURNS = (
    0, 3, 0, 1, 0, 2, 1, 0, 2, 1, 0, 0, 2, 0, 1, 0, 3, 1, 1, 0, 1, 2, 3, 0,
    1, 2, 0, 2, 1, 0, 2, 3, 1, 2, 0, 0, 3, 1, 3, 2, 0, 1, 2, 3, 0, 2, 3, 1,
    2, 1, 3, 1, 3, 0, 2, 3, 0, 1, 3, 2, 0, 3, 2, 0, 3, 1, 3, 2, 0, 1, 3, 2,
    1, 2, 1, 0, 3, 2, 3, 2, 1, 3, 0, 3, 2, 1, 0, 0, 3, 2, 1, 3, 1, 2, 1, 2,
    3, 2, 3, 3, 1, 2, 0, 3,
)


def layer(page_table, cache_len, tree_size, parents, queries, tree_kv, cache, resid, gain, w_out, w_gate, w_up, w_down):
    heads, width = w_out.shape
    depth, units = w_gate.shape
    half = units // 2
    sums = 2 * half + LANES
    vmem = pl.BlockSpec(memory_space=pltpu.VMEM)
    smem = pl.BlockSpec(memory_space=pltpu.SMEM)
    hbm = pl.BlockSpec(memory_space=pl.ANY)
    sem = pltpu.SemaphoreType.DMA

    def scatter_buffers(lanes, pair):
        first = [pltpu.VMEM((CHUNKS, BLOCK, lanes), BF)] if pair else []
        return [
            *first,
            pltpu.VMEM((CHUNKS, 2, BLOCK // 2 if pair else BLOCK, lanes), BF),
            pltpu.VMEM((CHUNKS, 2, 2, BLOCK, lanes), BF),
            pltpu.VMEM((CHUNKS, BLOCK, lanes), BF),
        ]

    scratch = [
        *[pltpu.VMEM(a.shape, BF) for a in (queries, tree_kv, cache, resid, resid)],
        pltpu.VMEM((heads, width), BF),
        pltpu.VMEM((2 * depth, units), BF),
        pltpu.VMEM((units, width), BF),
        pltpu.VMEM((CHUNKS, 8, 2, NODES, heads), BF),
        pltpu.VMEM((CHUNKS, 8, BLOCK, width), BF),
        pltpu.VMEM((CHUNKS, BLOCK, width), BF),
        pltpu.VMEM((CHUNKS, 2, 8, BLOCK, width + LANES), BF),
        pltpu.VMEM((2, 8, BLOCK, sums), BF),
        pltpu.VMEM((CHUNKS, 2, 8, BLOCK, half), BF),
        pltpu.VMEM((MAXTREE, MAXTREE), F32),
        *scatter_buffers(width, True),
        *scatter_buffers(sums, True),
        *scatter_buffers(width, True),
        sem((8,)),
        sem((2 * CHUNKS,)),
        sem((2,)),
        sem((2,)),
        *[sem((CHUNKS, 14))] * 6,
        *[sem((CHUNKS * PIECES, 10))] * 6,
    ]
    return pl.pallas_call(
        layer_kernel,
        out_shape=jax.ShapeDtypeStruct(resid.shape, BF),
        in_specs=[smem, smem, smem, vmem, hbm, hbm, hbm, hbm, vmem, hbm, hbm, hbm, hbm],
        out_specs=hbm,
        scratch_shapes=scratch,
        compiler_params=pltpu.CompilerParams(
            collective_id=0, has_side_effects=True, vmem_limit_bytes=62 * 1024 * 1024
        ),
        cost_estimate=pl.CostEstimate(
            flops=2 * 1024 * (heads * width + 3 * depth * units), bytes_accessed=26 * 1024 * 1024, transcendentals=0
        ),
    )(
        page_table,
        cache_len,
        tree_size,
        parents,
        queries,
        tree_kv,
        cache,
        resid,
        gain,
        w_out,
        w_gate,
        w_up,
        w_down,
    )


def body(
    resid,
    queries,
    tree_kv,
    cache,
    page_table,
    cache_len,
    tree_size,
    parents,
    w_out,
    gain,
    w_gate,
    w_up,
    w_down,
):
    return layer(
        page_table,
        cache_len,
        tree_size,
        parents,
        queries,
        tree_kv,
        cache,
        resid,
        gain,
        w_out,
        w_gate,
        w_up,
        w_down,
    )


def solution(mesh):
    in_specs = (
        P("gx", "gy"),
        P("gy", "gx"),
        P("gy", "gx"),
        P("gx", "gy", None, None),
        P("gy", None),
        P("gy"),
        P("gy"),
        P("gy", None),
        P("gx", "gy"),
        P("gy"),
        P("gy", "gx"),
        P("gy", "gx"),
        P("gx", "gy"),
    )
    out_specs = P("gx", "gy")
    return jax.shard_map(body, mesh=mesh, in_specs=in_specs, out_specs=out_specs, check_vma=False)
```
